32 devices in a mesh: pert: 2 (over y), space: 16 (over z, x, core).
Axes of the slice: x: 2, y: 2, z: 4, core: 2. Of those that a mesh axis runs over, the one named last changes fastest.
Arguments:
- spectra: float32 [320, 320, 256], P('space', None, 'pert'), may hold values from -6 to 6
- wave_order: int32 [320], replicated, may hold values from 0 to 319, as said below
- traj_wind: bfloat16 [2, 32, 480, 960], P(None, 'pert', 'space'), may hold values from -0.029907227 to 0.029907227
- traj_state: bfloat16 [2, 2, 32, 480, 960], P(None, None, 'pert', 'space'), may hold values from -6 to 6
- vertical_modes: float32 [32, 32], replicated, may hold values from -0.75 to 0.75
- mode_speeds: float32 [32], replicated, may hold values from 1e-06 to 0.001
Outputs:
- spectra_out: float32 [320, 320, 256], P('space', None, 'pert')
The draws below stay inside these ranges and needn't reach their ends.
Inputs may be any that keep to these rules, and one draw needn't show every extreme that they name: wave_order is a permutation of 0 to 319 in which slots 2 i and 2 i + 1 hold two wavenumbers that add up to 319.
All inputs are finite; a program needn't handle non-finite values.
Results may differ from the reference program's by a relative error of at most 0.0085.
Values may be sent and summed in bfloat16 or wider, within the bound.
No kernel may reach another device: no remote copies, remote signals or barrier semaphores. Data moves between devices by JAX's collectives and lax.ppermute only.
A program may use at most 128 MiB of HBM per device.

```python
import math
import jax
import jax.numpy as jnp
from jax import lax

NLAT = 480
NLON = 960
M = 320
VARS = 2
LEV = 32
STEPS = 2
CH = 256


def draw_wave_order(key, part):
    pair_count = M // 2
    key_pairs = jax.random.fold_in(key, 11)
    key_flips = jax.random.fold_in(key, 12)
    pair_order = jax.random.permutation(key_pairs, pair_count).astype(jnp.int32)
    flip_bits = jax.random.randint(key_flips, (pair_count,), 0, 2).astype(jnp.int32)
    lower_wave = pair_order
    upper_wave = M - 1 - pair_order
    leading = jnp.where(flip_bits == 1, upper_wave, lower_wave)
    trailing = jnp.where(flip_bits == 1, lower_wave, upper_wave)
    return jnp.stack([leading, trailing], axis=1).reshape(M).astype(jnp.int32)


def block_scale(stream_key, shape, pieces, smallest, top_value):
    gain, own = 1.0, jax.random.fold_in(stream_key, 6)
    for position, parts in pieces:
        draws = jnp.exp(jax.random.uniform(jax.random.fold_in(own, position), (parts,), jnp.float32, smallest / len(pieces), top_value / len(pieces)))
        gain = gain * jnp.repeat(draws, shape[position] // parts).reshape([-1 if axis == position else 1 for axis in range(len(shape))])
    return gain


def gaussian(rng, shape, deviation, most, pieces=(), kind=jnp.bfloat16):
    array = jax.random.normal(rng, shape, jnp.float32) * deviation
    if len(pieces) > 0:
        array = block_scale(rng, shape, pieces, -0.22, 0.18) * array
    return jnp.clip(array, min=-most, max=most).astype(kind)


def setup_inputs(seed: int = 0) -> dict:
    seeds = jax.random.split(jax.random.key(seed), 7)
    spectra = gaussian(seeds[0], (M, M, CH), 1.0, 6.0, ((0, 16), (2, 2)), jnp.float32)
    wave_order = draw_wave_order(jax.random.fold_in(seeds[6], 71), 0)
    traj_wind = gaussian(seeds[2], (STEPS, LEV, NLAT, NLON), 0.005, 0.029907227, ((1, 2), (2, 16)))
    traj_state = gaussian(seeds[3], (STEPS, VARS, LEV, NLAT, NLON), 1.0, 6.0, ((2, 2), (3, 16)))
    vertical_modes = gaussian(seeds[4], (LEV, LEV), (2 * LEV) ** -0.5, 0.75, (), jnp.float32)
    mode_speeds = jnp.clip(jnp.exp(jax.random.uniform(seeds[5], (LEV,), jnp.float32, math.log(9.999999974752427e-07), math.log(0.001))), 9.999999974752427e-07, 0.001)
    return {"spectra": spectra, "wave_order": wave_order, "traj_wind": traj_wind, "traj_state": traj_state, "vertical_modes": vertical_modes, "mode_speeds": mode_speeds}


def grid_angles():
    colatitude = (jnp.arange(NLAT, dtype=jnp.float32) + 0.5) * (math.pi / NLAT)
    return (jnp.cos(colatitude), jnp.sin(colatitude))

def sectoral_log(wave_float, sine_values):
    gammas = jax.scipy.special.gammaln
    start = 0.5 * (gammas(wave_float + 1.5) - gammas(wave_float + 1.0) - gammas(jnp.float32(1.5))) - 0.5 * math.log(2.0)
    return start[:, None] + wave_float[:, None] * jnp.log(sine_values)[None, :]

def coefficient(wave_float, degree):
    return jnp.sqrt((4.0 * degree * degree - 1.0) / ((degree - wave_float) * (degree + wave_float)))

def legendre_table(wave_list):
    cosines, sine_values = grid_angles()
    wave_float = wave_list.astype(jnp.float32)[:, None]
    log_start = sectoral_log(wave_list.astype(jnp.float32), sine_values)
    second = jnp.sqrt(2.0 * wave_float + 3.0) * cosines[None, :]
    largest = jnp.maximum(jnp.abs(second), 1.0)
    initial = (second / largest, 1.0 / largest, jnp.log(largest))
    row_zero = jnp.exp(log_start)
    row_one = second / largest * jnp.exp(log_start + jnp.log(largest))

    def advance(loop_carry, offset):
        current, previous, log_scale = loop_carry
        degree = wave_float + offset.astype(jnp.float32)
        upper_coef = coefficient(wave_float, degree)
        lower_coef = coefficient(wave_float, degree - 1.0)
        following = upper_coef * (cosines[None, :] * current - previous / lower_coef)
        biggest = jnp.maximum(jnp.abs(following), jnp.abs(current))
        log_next = log_scale + jnp.log(biggest)
        scaled = following / biggest
        return ((scaled, current / biggest, log_next), scaled * jnp.exp(log_start + log_next))
    offsets = jnp.arange(2, M, dtype=jnp.int32)
    final_carry, later_rows = lax.scan(advance, initial, offsets)
    stacked = jnp.concatenate([row_zero[None], row_one[None], later_rows], axis=0)
    legendre = jnp.moveaxis(stacked, 0, 1)
    inside = wave_list[:, None] + jnp.arange(M, dtype=jnp.int32)[None, :] <= M - 1
    return legendre * inside[:, :, None].astype(jnp.float32)

def zonal_tables(wave_list):
    cell_index = jnp.arange(NLON, dtype=jnp.int32)
    phase_index = wave_list[:, None] * cell_index[None, :] % NLON
    angles = phase_index.astype(jnp.float32) * (2.0 * math.pi / NLON)
    factor = jnp.where(wave_list == 0, 1.0, 2.0).astype(jnp.float32)[:, None]
    synth_table = jnp.stack([factor * jnp.cos(angles), -factor * jnp.sin(angles)]).astype(jnp.bfloat16)
    analysis = (jnp.stack([jnp.cos(angles).T, -jnp.sin(angles).T], axis=1) / NLON).astype(jnp.bfloat16)
    return (synth_table, analysis)

def spectral_mask(wave_list, columns):
    degree_offset = jnp.arange(M, dtype=jnp.int32)
    inside = wave_list[:, None] + degree_offset[None, :] <= M - 1
    imaginary = jnp.arange(columns, dtype=jnp.int32) % 2 == 1
    dropped = (wave_list[:, None] == 0) & imaginary[None, :]
    return (inside[:, :, None] & jnp.logical_not(dropped)[:, None, :]).astype(jnp.float32)

def damping_rates(wave_list, mode_speeds):
    degree = (wave_list[:, None] + jnp.arange(M, dtype=jnp.int32)[None, :]).astype(jnp.float32)
    stiffness = mode_speeds[None, None, :] * (degree * (degree + 1.0))[:, :, None]
    return stiffness / (1.0 + stiffness)

def zonal_slope(fourier, wave_list):
    part_pairs = fourier.reshape(fourier.shape[:-1] + (fourier.shape[-1] // 2, 2)).astype(jnp.float32)
    factor = wave_list.astype(jnp.float32).reshape((-1,) + (1,) * (part_pairs.ndim - 1))
    turned = jnp.stack([-part_pairs[..., 1], part_pairs[..., 0]], axis=-1) * factor
    return turned.reshape(fourier.shape).astype(jnp.bfloat16)

def synthesis(fourier, synth_table):
    part_pairs = fourier.reshape(fourier.shape[0], fourier.shape[1], -1, 2).astype(jnp.float32)
    return jnp.einsum('jtrc,cjx->trx', part_pairs, synth_table.astype(jnp.float32))

def tendency(grid_values, grid_slopes, wind_now, traj_now):
    lat_count = grid_values.shape[0]
    shaped = (lat_count, -1, VARS, LEV, NLON)
    values_five = grid_values.reshape(shaped)
    slopes_five = grid_slopes.reshape(shaped)
    wind_rows = jnp.transpose(wind_now, (1, 0, 2)).astype(jnp.float32)[:, None, None, :, :]
    state_rows = jnp.roll(jnp.transpose(traj_now, (2, 0, 1, 3)), -1, axis=1).astype(jnp.float32)[:, None]
    shifted = jnp.roll(values_five, -2, axis=2)
    forcing = -wind_rows * slopes_five - state_rows * shifted
    return forcing.reshape(lat_count, -1, NLON).astype(jnp.bfloat16)

def analysis_step(forcing, analysis):
    lat_count = forcing.shape[0]
    fourier = jnp.einsum('trx,xcj->jtrc', forcing.astype(jnp.float32), analysis.astype(jnp.float32))
    return fourier.astype(jnp.bfloat16).reshape(analysis.shape[2], lat_count, -1)

def reference(spectra, wave_order, traj_wind, traj_state, vertical_modes, mode_speeds):
    legendre = legendre_table(wave_order)
    angle_pair = grid_angles()
    inverse_table = legendre.astype(jnp.bfloat16)
    forward_table = (legendre * (angle_pair[1] * (math.pi / NLAT))[None, None, :]).astype(jnp.bfloat16)
    synth_table, analysis = zonal_tables(wave_order)
    member_cols = 2 * VARS * LEV
    members = jnp.moveaxis(spectra.reshape(M, M, -1, member_cols), 2, 0)
    keep_mask = spectral_mask(wave_order, member_cols)
    damping = damping_rates(wave_order, mode_speeds)

    def advance_member(member):
        spectral_state = member * keep_mask
        for step_idx in range(STEPS):
            fourier_rows = jnp.einsum('jkt,jkc->jtc', inverse_table.astype(jnp.float32), spectral_state.astype(jnp.bfloat16).astype(jnp.float32)).astype(jnp.bfloat16)
            slope_rows = zonal_slope(fourier_rows, wave_order)
            grid_values = synthesis(fourier_rows, synth_table)
            grid_slopes = synthesis(slope_rows, synth_table)
            forcing = tendency(grid_values, grid_slopes, traj_wind[step_idx], traj_state[step_idx])
            wave_rows = analysis_step(forcing, analysis)
            change = jnp.einsum('jkt,jtc->jkc', forward_table.astype(jnp.float32), wave_rows.astype(jnp.float32))
            combined = spectral_state + change
            shaped = combined.reshape(M, M, VARS, LEV, 2)
            projected = jnp.einsum('ab,jkvbc->jkvac', vertical_modes, shaped, precision=lax.Precision.HIGHEST)
            weighted = projected * damping[:, :, None, :, None]
            returned = jnp.einsum('ab,jkvac->jkvbc', vertical_modes, weighted, precision=lax.Precision.HIGHEST)
            spectral_state = (combined - returned.reshape(combined.shape)) * keep_mask
        return spectral_state
    result = lax.map(advance_member, members)
    return jnp.moveaxis(result, 0, 2).reshape(M, M, -1)
```

```python
import math

import jax
import jax.numpy as jnp
import numpy as np
from jax import lax
from jax.experimental import pallas as pl
from jax.experimental.pallas import tpu as pltpu
from jax.sharding import PartitionSpec as P

NLAT = 480
NLON = 960
M = 320
VARS = 2
LEV = 32
STEPS = 2
ROWS = 336
ROWS_T = 384
DEPTH = 384
VMEM_BYTES = 48 * 1024 * 1024
BIG = 2.0**32
HIGHEST = lax.Precision.HIGHEST


def params():
    return pltpu.CompilerParams(vmem_limit_bytes=VMEM_BYTES)


def vmem(count):
    return [pl.BlockSpec(memory_space=pltpu.VMEM)] * count


def smem(count):
    return [pl.BlockSpec(memory_space=pltpu.SMEM)] * count


class Sizes:
    def __init__(self, space):
        self.space = space
        self.slots = M // space
        self.pairs = self.slots // 2
        self.lats = NLAT // space
        self.lat_pad = -(-self.lats // 8) * 8
        self.half = space // 2
        self.north = self.half * self.lat_pad
        self.pair_pad = -(-self.pairs // 8) * 8
        self.block = self.slots * self.lats
        self.block_pad = self.block + 8
        self.group = 6 if self.lats % 6 == 0 else -(-self.lats // 2) * 2
        self.groups = -(-self.lats // self.group)


def table_kernel(sz, wave_a, wave_b, start_a, start_b, cosines, table, table_t, rows_ref):
    shape = (sz.pair_pad, sz.north)
    wide = shape[1] // 128
    wa, wb = wave_a[...], wave_b[...]
    length = M - wa
    x = cosines[...]
    la, lb = start_a[...], start_b[...]

    def spread(v):
        return jnp.concatenate([v] * wide, axis=1)

    def body(block, carry):
        cur, prev, inv_prev, shift = carry
        big = jnp.maximum(jnp.abs(cur), jnp.abs(prev)) > BIG
        scale = jnp.where(big, 1.0 / BIG, 1.0)
        cur, prev = cur * scale, prev * scale
        shift = shift + jnp.where(big, 32.0, 0.0)
        second = spread(((block * 8).astype(jnp.float32) > length).astype(jnp.float32)) > 0.5
        base = jnp.exp2(0.5 * (jnp.where(second, lb, la) + shift))
        base_b = jnp.exp2(0.5 * lb)
        for j in range(8):
            r = (block * 8 + j).astype(jnp.float32)
            in_b = r >= length
            fresh = r == length
            m = jnp.where(in_b, wb, wa)
            k = jnp.where(in_b, r - length, r)
            n = m + k
            den = k * (2.0 * m + k)
            num = 4.0 * n * n - 1.0
            first = k < 0.5
            safe_den = jnp.where(first, 1.0, den)
            upper = jnp.where(first, 0.0, jnp.sqrt(num / safe_den))
            inv = jnp.where(first, 0.0, jnp.sqrt(safe_den / jnp.where(first, 1.0, num)))
            up_w = spread(upper)
            lo_w = spread(upper * inv_prev)
            new = up_w * x * cur - lo_w * prev
            fresh_w = spread(fresh.astype(jnp.float32)) > 0.5
            start = jnp.logical_or(fresh_w, r == 0.0)
            new = jnp.where(start, 1.0, new)
            prev = jnp.where(start, 0.0, cur)
            shift = jnp.where(fresh_w, 0.0, shift)
            base = jnp.where(fresh_w, base_b, base)
            cur = new
            inv_prev = inv
            value = (cur * base) * base
            for c in range(wide):
                rows_ref[c, pl.ds(block * 8 + j, sz.pair_pad, stride=ROWS), :] = value[
                    :, c * 128 : (c + 1) * 128
                ]
        return cur, prev, inv_prev, shift

    zero = jnp.zeros(shape, jnp.float32)
    lax.fori_loop(0, ROWS // 8, body, (zero, zero, jnp.zeros_like(wa), zero))
    ridx = lax.broadcasted_iota(jnp.int32, (ROWS, sz.north), 0)

    def emit(i, _):
        at = pl.multiple_of(i * ROWS, ROWS)
        full = jnp.concatenate([rows_ref[c, pl.ds(at, ROWS), :] for c in range(wide)], axis=1)
        full = jnp.where(ridx <= M, full, 0.0)
        table[i] = full.astype(jnp.bfloat16)
        padded = jnp.concatenate(
            [full, jnp.zeros((ROWS_T - ROWS, sz.north), jnp.float32)], axis=0
        )
        table_t[i] = jnp.transpose(padded).astype(jnp.bfloat16)
        return 0

    lax.fori_loop(0, sz.pairs, emit, 0)


def make_tables(sz, wave_a, wave_b, log_a, log_b, cosines):
    return pl.pallas_call(
        lambda *refs: table_kernel(sz, *refs),
        out_shape=(
            jax.ShapeDtypeStruct((sz.pairs, ROWS, sz.north), jnp.bfloat16),
            jax.ShapeDtypeStruct((sz.pairs, sz.north, ROWS_T), jnp.bfloat16),
        ),
        in_specs=vmem(5),
        out_specs=tuple(vmem(2)),
        scratch_shapes=[pltpu.VMEM((sz.north // 128, sz.pair_pad * ROWS, 128), jnp.float32)],
        compiler_params=params(),
        name="legendre_tables",
    )(wave_a, wave_b, log_a, log_b, cosines)


def row_facts(waves, i, columns):
    wave_a, wave_b = waves[2 * i], waves[2 * i + 1]
    length = M - wave_a
    r = lax.broadcasted_iota(jnp.int32, (ROWS, columns), 0)
    in_a = r < length
    k = jnp.where(in_a, r, r - length)
    even = jnp.bitwise_and(k, 1) == 0
    return wave_a, wave_b, length, r, in_a, k, even


def send_rows(sz, i, state, facts, table_t, stage):
    _, _, _, _, in_a, _, even = facts
    zero = jnp.zeros_like(state)
    in_b = jnp.logical_not(in_a)
    odd = jnp.logical_not(even)
    parts = [
        jnp.where(jnp.logical_and(side, sign), state, zero).astype(jnp.bfloat16)
        for side in (in_a, in_b)
        for sign in (even, odd)
    ]
    columns = state.shape[1]
    rhs = jnp.concatenate(parts, axis=1)
    rhs = jnp.concatenate([rhs, jnp.zeros((ROWS_T - ROWS, 4 * columns), jnp.bfloat16)], axis=0)
    out = jnp.dot(table_t[i], rhs, preferred_element_type=jnp.float32)
    for s in range(2):
        e = out[:, (2 * s) * columns : (2 * s + 1) * columns]
        o = out[:, (2 * s + 1) * columns : (2 * s + 2) * columns]
        north, south = e + o, e - o
        at = (2 * i + s) * sz.lats
        for b in range(sz.half):
            lo = b * sz.lat_pad
            stage[b, pl.ds(at, sz.lat_pad), :] = north[lo : lo + sz.lat_pad]
            stage[sz.space - 1 - b, pl.ds(at, sz.lat_pad), :] = south[lo : lo + sz.lat_pad]


def flush(sz, stage, send):
    def body(d, _):
        send[d] = stage[d, : sz.block, :].astype(jnp.bfloat16)
        return 0

    lax.fori_loop(0, sz.space, body, 0)


def load_rows(sz, recv, stage):
    def body(d, _):
        stage[d, : sz.block, :] = recv[d].astype(jnp.float32)
        stage[d, pl.ds(sz.block, 8), :] = jnp.zeros((8, stage.shape[2]), jnp.float32)
        return 0

    lax.fori_loop(0, sz.space, body, 0)


def change_rows(sz, i, facts, table, weights, stage):
    _, _, _, _, in_a, _, even = facts
    parts = []
    w = weights[...]
    for s in range(2):
        at = (2 * i + s) * sz.lats
        north = jnp.concatenate(
            [stage[b, pl.ds(at, sz.lat_pad), :] for b in range(sz.half)], axis=0
        )
        south = jnp.concatenate(
            [stage[sz.space - 1 - b, pl.ds(at, sz.lat_pad), :] for b in range(sz.half)], axis=0
        )
        parts.append(((north + south) * w).astype(jnp.bfloat16))
        parts.append(((north - south) * w).astype(jnp.bfloat16))
    rhs = jnp.concatenate(parts, axis=1)
    out = jnp.dot(table[i], rhs, preferred_element_type=jnp.float32)
    c = out.shape[1] // 4
    side_a = jnp.where(even, out[:, :c], out[:, c : 2 * c])
    side_b = jnp.where(even, out[:, 2 * c : 3 * c], out[:, 3 * c :])
    return jnp.where(in_a, side_a, side_b)


def kept(state, facts):
    wave_a, wave_b, _, r, in_a, _, _ = facts
    columns = state.shape[1]
    imaginary = lax.broadcasted_iota(jnp.int32, state.shape, 1) >= columns // 2
    wave = jnp.where(in_a, wave_a, wave_b)
    dropped = jnp.logical_or(jnp.logical_and(wave == 0, imaginary), r > M)
    return jnp.where(dropped, 0.0, state)


def updated(state, change, facts, mixing, mixing_t, speeds):
    wave_a, wave_b, _, _, in_a, k, _ = facts
    combined = state + change
    projected = jnp.dot(combined, mixing[...], precision=HIGHEST)
    n = (jnp.where(in_a, wave_a, wave_b) + k).astype(jnp.float32)
    stiffness = speeds[...] * (n * (n + 1.0))
    weighted = projected * (stiffness / (1.0 + stiffness))
    returned = jnp.dot(weighted, mixing_t[...], precision=HIGHEST)
    return kept(combined - returned, facts)


def first_kernel(sz, waves, spectra, turn, table_t, state_ref, send, stage):
    columns = spectra.shape[2]

    def body(i, _):
        facts = row_facts(waves, i, columns)
        length, r, in_a = facts[2], facts[3], facts[4]
        blank = jnp.zeros((ROWS - M, columns), jnp.float32)
        rows_a = jnp.concatenate([spectra[2 * i], blank], axis=0)
        rows_b = jnp.concatenate([spectra[2 * i + 1], blank], axis=0)
        packed = jnp.where(in_a, rows_a, pltpu.roll(rows_b, length, 0))
        state = jnp.dot(packed, turn[...], precision=HIGHEST)
        state = kept(state, facts)
        state_ref[i] = state
        send_rows(sz, i, state, facts, table_t, stage)
        return 0

    lax.fori_loop(0, sz.pairs, body, 0)
    flush(sz, stage, send)


def middle_kernel(
    sz, waves, state_in, recv, table, table_t, weights, mixing, mixing_t, speeds,
    state_out, send, stage_in, stage,
):
    columns = state_in.shape[2]
    load_rows(sz, recv, stage_in)

    def body(i, _):
        facts = row_facts(waves, i, columns)
        change = change_rows(sz, i, facts, table, weights, stage_in)
        state = updated(state_in[i], change, facts, mixing, mixing_t, speeds)
        state_out[i] = state
        send_rows(sz, i, state, facts, table_t, stage)
        return 0

    lax.fori_loop(0, sz.pairs, body, 0)
    flush(sz, stage, send)


def last_kernel(
    sz, waves, state_in, recv, table, weights, mixing, mixing_t, speeds, turn_t, out, stage_in
):
    columns = state_in.shape[2]
    load_rows(sz, recv, stage_in)

    def body(i, _):
        facts = row_facts(waves, i, columns)
        wave_a, wave_b, length, r = facts[:4]
        change = change_rows(sz, i, facts, table, weights, stage_in)
        state = updated(state_in[i], change, facts, mixing, mixing_t, speeds)
        state = jnp.dot(state, turn_t[...], precision=HIGHEST)
        out[2 * i] = jnp.where(r < length, state, 0.0)[:M]
        rolled = pltpu.roll(state, ROWS - length, 0)
        out[2 * i + 1] = jnp.where(r < M - wave_b, rolled, 0.0)[:M]
        return 0

    lax.fori_loop(0, sz.pairs, body, 0)


def grid_kernel(sz, flip, recv, traj, synth, slope, scale, send, stage_in, stage, lhs, values, slopes, force):
    lanes = recv.shape[2]
    rows = lanes // 2
    flat = M * sz.lats

    def load(d, _):
        at = pl.multiple_of(d * sz.block, 8)
        stage_in[pl.ds(at, sz.block), :] = recv[d].astype(jnp.float32)
        return 0

    lax.fori_loop(0, sz.space, load, 0)
    blank = jnp.zeros((DEPTH - M, lanes), jnp.float32)

    def body(g, _):
        for q in range(sz.group):
            t = g * sz.group + q
            if sz.groups == 1 and q >= sz.lats:
                lhs[q * rows : (q + 1) * rows, :] = jnp.zeros((rows, 2 * DEPTH), jnp.bfloat16)
                continue
            block = stage_in[pl.ds(t, M, stride=sz.lats), :]
            turned = jnp.transpose(jnp.concatenate([block, blank], axis=0)).astype(jnp.bfloat16)
            lhs[q * rows : (q + 1) * rows, :DEPTH] = turned[:rows]
            lhs[q * rows : (q + 1) * rows, DEPTH:] = turned[rows:]
        left = lhs[...]
        values[...] = jnp.dot(left, synth[...], preferred_element_type=jnp.float32)
        slopes[...] = jnp.dot(left, slope[...], preferred_element_type=jnp.float32)
        for q in range(sz.group):
            if sz.groups == 1 and q >= sz.lats:
                force[q * rows : (q + 1) * rows, :] = jnp.zeros((rows, NLON), jnp.bfloat16)
                continue
            t = g * sz.group + q
            here = jnp.where(flip[0] == 1, sz.lats - 1 - t, t)
            wind = traj[here, 0].astype(jnp.float32)
            for v in range(VARS):
                lo = q * rows + v * LEV
                other = traj[here, 1 + (v + 1) % VARS].astype(jnp.float32)
                force[lo : lo + LEV, :] = (
                    wind * slopes[lo : lo + LEV, :] + other * values[lo : lo + LEV, :]
                ).astype(jnp.bfloat16)
        forcing = force[...]
        spectrum = [
            lax.dot_general(
                synth[c * DEPTH : c * DEPTH + M, :],
                forcing,
                (((1,), (1,)), ((), ())),
                preferred_element_type=jnp.float32,
            )
            * scale[...][:, : 1]
            for c in range(2)
        ]
        lane = lax.broadcasted_iota(jnp.int32, (M, lanes), 1)
        left_side = lane < rows
        for q in range(0, sz.group, 2):
            re = spectrum[0][:, q * rows : (q + 2) * rows]
            im = spectrum[1][:, q * rows : (q + 2) * rows]
            t = g * sz.group + q
            stage[pl.ds(t, M, stride=sz.lats), :] = jnp.where(left_side, re, pltpu.roll(im, rows, 1))
            if sz.groups == 1 and q + 1 >= sz.lats:
                continue
            stage[pl.ds(t + 1, M, stride=sz.lats), :] = jnp.where(
                left_side, pltpu.roll(re, rows, 1), im
            )
        return 0

    lax.fori_loop(0, sz.groups, body, 0)

    def out(d, _):
        at = pl.multiple_of(d * sz.block, 8)
        send[d] = stage[pl.ds(at, sz.block), :].astype(jnp.bfloat16)
        return 0

    lax.fori_loop(0, sz.space, out, 0)


def grid_stage(sz, flip, recv, traj, synth, slope, scale):
    lanes = recv.shape[2]
    wide = sz.group * lanes // 2
    return pl.pallas_call(
        lambda *refs: grid_kernel(sz, *refs),
        out_shape=jax.ShapeDtypeStruct(recv.shape, jnp.bfloat16),
        in_specs=smem(1) + vmem(5),
        out_specs=vmem(1)[0],
        scratch_shapes=[
            pltpu.VMEM((M * sz.lats, lanes), jnp.float32),
            pltpu.VMEM((M * sz.lats, lanes), jnp.float32),
            pltpu.VMEM((wide, 2 * DEPTH), jnp.bfloat16),
            pltpu.VMEM((wide, NLON), jnp.float32),
            pltpu.VMEM((wide, NLON), jnp.float32),
            pltpu.VMEM((wide, NLON), jnp.bfloat16),
        ],
        compiler_params=params(),
        name="grid_stage",
    )(flip, recv, traj, synth, slope, scale)


def zonal_tables(wave_list):
    cell_index = jnp.arange(NLON, dtype=jnp.int32)
    wave_pad = jnp.concatenate([wave_list, jnp.zeros((DEPTH - M,), jnp.int32)])
    phase_index = wave_pad[:, None] * cell_index[None, :] % NLON
    angles = phase_index.astype(jnp.float32) * (2.0 * math.pi / NLON)
    factor = jnp.where(wave_pad == 0, 1.0, 2.0).astype(jnp.float32)
    inside = (jnp.arange(DEPTH) < M).astype(jnp.float32)
    gain = (factor * inside)[:, None]
    cosine, sine = gain * jnp.cos(angles), gain * jnp.sin(angles)
    wave = wave_pad.astype(jnp.float32)[:, None]
    synth = jnp.concatenate([-cosine, sine], axis=0).astype(jnp.bfloat16)
    slope = jnp.concatenate([wave * sine, wave * cosine], axis=0).astype(jnp.bfloat16)
    scale = jnp.broadcast_to((-1.0 / (NLON * factor[:M]))[:, None], (M, 128))
    return synth, slope, scale


def column_turn(columns):
    turn = np.zeros((columns, columns), np.float32)
    for c in range(columns):
        part, row = c % 2, c // 2
        turn[c, part * (columns // 2) + row] = 1.0
    return turn


def sectoral(wave, log_sine):
    gammas = jax.scipy.special.gammaln
    start = 0.5 * (
        gammas(wave + 1.5) - gammas(wave + 1.0) - gammas(jnp.float32(1.5))
    ) - 0.5 * math.log(2.0)
    return (start[:, None] + wave[:, None] * log_sine[None, :]) * (1.0 / math.log(2.0))


def shards(sz, spectra, wave_order, traj_wind, traj_state, vertical_modes, mode_speeds):
    columns = spectra.shape[2]
    rank = lax.axis_index("space")
    waves = lax.dynamic_slice_in_dim(wave_order, rank * sz.slots, sz.slots)

    place = np.arange(sz.north)
    block, inner = place // sz.lat_pad, place % sz.lat_pad
    real = inner < sz.lats
    colat = np.where(real, (block * sz.lats + inner + 0.5) * (math.pi / NLAT), math.pi / 2)
    cosines = jnp.asarray(np.cos(colat), jnp.float32)[None, :]
    log_sine = jnp.asarray(np.log(np.sin(colat)), jnp.float32)
    weights = jnp.asarray(
        np.broadcast_to((np.sin(colat) * (math.pi / NLAT) * real)[:, None], (sz.north, columns)),
        jnp.float32,
    )

    pair_waves = jnp.zeros((sz.pair_pad, 2), jnp.int32).at[: sz.pairs].set(waves.reshape(-1, 2))
    pair_waves = pair_waves.astype(jnp.float32)
    wide_a = jnp.broadcast_to(pair_waves[:, :1], (sz.pair_pad, 128))
    wide_b = jnp.broadcast_to(pair_waves[:, 1:], (sz.pair_pad, 128))
    table, table_t = make_tables(
        sz, wide_a, wide_b, sectoral(pair_waves[:, 0], log_sine), sectoral(pair_waves[:, 1], log_sine), cosines
    )

    turn = column_turn(columns)
    same = np.kron(np.eye(columns // LEV, dtype=np.float32), np.ones((LEV, LEV), np.float32))
    mixing = jnp.tile(vertical_modes.T, (columns // LEV, columns // LEV)) * same
    mixing_t = jnp.tile(vertical_modes, (columns // LEV, columns // LEV)) * same
    speeds = jnp.tile(mode_speeds, columns // LEV)[None, :]
    turn, turn_t = jnp.asarray(turn), jnp.asarray(turn.T)

    synth, slope, scale = zonal_tables(wave_order)
    flip = jnp.where(rank >= sz.half, 1, 0).astype(jnp.int32).reshape(1)

    stage_shape = pltpu.VMEM((sz.space, sz.block_pad, columns), jnp.float32)
    state_shape = jax.ShapeDtypeStruct((sz.pairs, ROWS, columns), jnp.float32)
    send_shape = jax.ShapeDtypeStruct((sz.space, sz.block, columns), jnp.bfloat16)

    state, send = pl.pallas_call(
        lambda *refs: first_kernel(sz, *refs),
        out_shape=(state_shape, send_shape),
        in_specs=smem(1) + vmem(3),
        out_specs=tuple(vmem(2)),
        scratch_shapes=[stage_shape],
        compiler_params=params(),
        name="first_inverse",
    )(waves, spectra, turn, table_t)

    for step in range(STEPS):
        local = jnp.concatenate([traj_wind[step][None], traj_state[step]], axis=0)
        traj = lax.all_gather(local, "pert", axis=1, tiled=True)
        traj = jnp.transpose(traj, (2, 0, 1, 3))
        recv = lax.all_to_all(send, "space", 0, 0, tiled=True)
        send = grid_stage(sz, flip, recv, traj, synth, slope, scale)
        recv = lax.all_to_all(send, "space", 0, 0, tiled=True)
        if step < STEPS - 1:
            state, send = pl.pallas_call(
                lambda *refs: middle_kernel(sz, *refs),
                out_shape=(state_shape, send_shape),
                in_specs=smem(1) + vmem(8),
                out_specs=tuple(vmem(2)),
                scratch_shapes=[stage_shape, stage_shape],
                compiler_params=params(),
                name="forward_inverse",
            )(waves, state, recv, table, table_t, weights, mixing, mixing_t, speeds)
        else:
            out = pl.pallas_call(
                lambda *refs: last_kernel(sz, *refs),
                out_shape=jax.ShapeDtypeStruct(spectra.shape, jnp.float32),
                in_specs=smem(1) + vmem(8),
                out_specs=vmem(1)[0],
                scratch_shapes=[stage_shape],
                compiler_params=params(),
                name="forward_last",
            )(waves, state, recv, table, weights, mixing, mixing_t, speeds, turn_t)
    return out


def solution(mesh):
    sz = Sizes(mesh.shape["space"])
    placed = (
        P("space", None, "pert"),
        P(),
        P(None, "pert", "space", None),
        P(None, None, "pert", "space", None),
        P(),
        P(),
    )
    return jax.shard_map(
        lambda *args: shards(sz, *args),
        mesh=mesh,
        in_specs=placed,
        out_specs=P("space", None, "pert"),
        check_vma=False,
    )
```

```python
import math

import jax
import jax.numpy as jnp
import numpy as np
from jax import lax
from jax.experimental import pallas as pl
from jax.experimental.pallas import tpu as pltpu
from jax.sharding import PartitionSpec as P

NLAT = 480
NLON = 960
M = 320
VARS = 2
LEV = 32
STEPS = 2
ROWS = 336
ROWS_T = 384
DEPTH = 384
VMEM_BYTES = 48 * 1024 * 1024
BIG = 2.0**32


def params():
    return pltpu.CompilerParams(vmem_limit_bytes=VMEM_BYTES)


def cost(microseconds):
    return pl.CostEstimate(flops=int(microseconds * 1.0e9), bytes_accessed=1 << 20, transcendentals=0)


def vmem(count):
    return [pl.BlockSpec(memory_space=pltpu.VMEM)] * count


def smem(count):
    return [pl.BlockSpec(memory_space=pltpu.SMEM)] * count


class Sizes:
    def __init__(self, space):
        self.space = space
        self.slots = M // space
        self.pairs = self.slots // 2
        self.lats = NLAT // space
        self.half = space // 2
        self.parts = 2
        self.part_pad = -(-self.lats // (8 * self.parts)) * 8
        first = -(-self.lats // self.parts)
        self.part_lats = [first, self.lats - first]
        self.part_start = [0, first]
        self.part_rows = self.half * self.part_pad
        self.north = self.parts * self.part_rows
        self.pair_pad = -(-self.pairs // 8) * 8
        self.group = 8

    def block(self, part):
        return self.slots * self.part_lats[part]

    def block_pad(self, part):
        last = (self.slots - 1) * self.part_lats[part] + self.part_pad
        return -(-last // 8) * 8


def table_kernel(sz, wave_a, wave_b, start_a, start_b, cosines, table, table_t, rows_ref):
    shape = (sz.pair_pad, sz.north)
    wide = shape[1] // 128
    wa, wb = wave_a[...], wave_b[...]
    length = M - wa
    x = cosines[...]
    la, lb = start_a[...], start_b[...]

    def spread(v):
        return jnp.concatenate([v] * wide, axis=1)

    def body(block, carry):
        cur, prev, inv_prev, shift = carry
        big = jnp.maximum(jnp.abs(cur), jnp.abs(prev)) > BIG
        scale = jnp.where(big, 1.0 / BIG, 1.0)
        cur, prev = cur * scale, prev * scale
        shift = shift + jnp.where(big, 32.0, 0.0)
        second = spread(((block * 8).astype(jnp.float32) > length).astype(jnp.float32)) > 0.5
        base = jnp.exp2(0.5 * (jnp.where(second, lb, la) + shift))
        base_b = jnp.exp2(0.5 * lb)
        for j in range(8):
            r = (block * 8 + j).astype(jnp.float32)
            in_b = r >= length
            fresh = r == length
            m = jnp.where(in_b, wb, wa)
            k = jnp.where(in_b, r - length, r)
            n = m + k
            den = k * (2.0 * m + k)
            num = 4.0 * n * n - 1.0
            first = k < 0.5
            safe_den = jnp.where(first, 1.0, den)
            upper = jnp.where(first, 0.0, jnp.sqrt(num / safe_den))
            inv = jnp.where(first, 0.0, jnp.sqrt(safe_den / jnp.where(first, 1.0, num)))
            up_w = spread(upper)
            lo_w = spread(upper * inv_prev)
            new = up_w * x * cur - lo_w * prev
            fresh_w = spread(fresh.astype(jnp.float32)) > 0.5
            start = jnp.logical_or(fresh_w, r == 0.0)
            new = jnp.where(start, 1.0, new)
            prev = jnp.where(start, 0.0, cur)
            shift = jnp.where(fresh_w, 0.0, shift)
            base = jnp.where(fresh_w, base_b, base)
            cur = new
            inv_prev = inv
            value = (cur * base) * base
            for c in range(wide):
                rows_ref[c, pl.ds(block * 8 + j, sz.pair_pad, stride=ROWS), :] = value[
                    :, c * 128 : (c + 1) * 128
                ]
        return cur, prev, inv_prev, shift

    zero = jnp.zeros(shape, jnp.float32)
    lax.fori_loop(0, ROWS // 8, body, (zero, zero, jnp.zeros_like(wa), zero))
    ridx = lax.broadcasted_iota(jnp.int32, (ROWS, sz.north), 0)

    def emit(i, _):
        at = pl.multiple_of(i * ROWS, ROWS)
        full = jnp.concatenate([rows_ref[c, pl.ds(at, ROWS), :] for c in range(wide)], axis=1)
        full = jnp.where(ridx <= M, full, 0.0)
        table[i] = full.astype(jnp.bfloat16)
        padded = jnp.concatenate(
            [full, jnp.zeros((ROWS_T - ROWS, sz.north), jnp.float32)], axis=0
        )
        table_t[i] = jnp.transpose(padded).astype(jnp.bfloat16)
        return 0

    lax.fori_loop(0, sz.pairs, emit, 0)


def make_tables(sz, wave_a, wave_b, log_a, log_b, cosines):
    return pl.pallas_call(
        lambda *refs: table_kernel(sz, *refs),
        out_shape=(
            jax.ShapeDtypeStruct((sz.pairs, ROWS, sz.north), jnp.bfloat16),
            jax.ShapeDtypeStruct((sz.pairs, sz.north, ROWS_T), jnp.bfloat16),
        ),
        in_specs=vmem(5),
        out_specs=tuple(vmem(2)),
        scratch_shapes=[pltpu.VMEM((sz.north // 128, sz.pair_pad * ROWS, 128), jnp.float32)],
        compiler_params=params(),
        name="legendre_tables",
    )(wave_a, wave_b, log_a, log_b, cosines)


def row_facts(waves, i, columns):
    wave_a, wave_b = waves[2 * i], waves[2 * i + 1]
    length = M - wave_a
    r = lax.broadcasted_iota(jnp.int32, (ROWS, columns), 0)
    in_a = r < length
    k = jnp.where(in_a, r, r - length)
    even = jnp.bitwise_and(k, 1) == 0
    return wave_a, wave_b, length, r, in_a, k, even


def send_rows(sz, part, i, state, facts, table_t, stage):
    _, _, _, _, in_a, _, even = facts
    zero = jnp.zeros_like(state)
    in_b = jnp.logical_not(in_a)
    odd = jnp.logical_not(even)
    pieces = [
        jnp.where(jnp.logical_and(side, sign), state, zero).astype(jnp.bfloat16)
        for side in (in_a, in_b)
        for sign in (even, odd)
    ]
    columns = state.shape[1]
    rhs = jnp.concatenate(pieces, axis=1)
    rhs = jnp.concatenate([rhs, jnp.zeros((ROWS_T - ROWS, 4 * columns), jnp.bfloat16)], axis=0)
    rows = table_t[i, part * sz.part_rows : (part + 1) * sz.part_rows, :]
    out = jnp.dot(rows, rhs, preferred_element_type=jnp.float32)
    size = sz.part_pad
    for s in range(2):
        e = out[:, (2 * s) * columns : (2 * s + 1) * columns]
        o = out[:, (2 * s + 1) * columns : (2 * s + 2) * columns]
        north, south = e + o, e - o
        at = (2 * i + s) * sz.part_lats[part]
        for b in range(sz.half):
            lo = b * size
            stage[b, pl.ds(at, size), :] = north[lo : lo + size]
            stage[sz.space - 1 - b, pl.ds(at, size), :] = south[lo : lo + size]


def flush(sz, part, stage, send):
    def body(d, _):
        send[d] = stage[d, : sz.block(part), :].astype(jnp.bfloat16)
        return 0

    lax.fori_loop(0, sz.space, body, 0)


def load_rows(sz, part, recv, stage):
    rows = sz.block_pad(part)

    def body(d, _):
        stage[d, rows - 16 : rows, :] = jnp.zeros((16, stage.shape[2]), jnp.float32)
        stage[d, : sz.block(part), :] = recv[d].astype(jnp.float32)
        return 0

    lax.fori_loop(0, sz.space, body, 0)


def change_rows(sz, part, i, facts, table, weights, stage):
    _, _, _, _, in_a, _, even = facts
    pieces = []
    lo = part * sz.part_rows
    w = weights[lo : lo + sz.part_rows, :]
    size = sz.part_pad
    for s in range(2):
        at = (2 * i + s) * sz.part_lats[part]
        north = jnp.concatenate([stage[b, pl.ds(at, size), :] for b in range(sz.half)], axis=0)
        south = jnp.concatenate(
            [stage[sz.space - 1 - b, pl.ds(at, size), :] for b in range(sz.half)], axis=0
        )
        pieces.append(((north + south) * w).astype(jnp.bfloat16))
        pieces.append(((north - south) * w).astype(jnp.bfloat16))
    rhs = jnp.concatenate(pieces, axis=1)
    out = jnp.dot(table[i, :, lo : lo + sz.part_rows], rhs, preferred_element_type=jnp.float32)
    c = out.shape[1] // 4
    side_a = jnp.where(even, out[:, :c], out[:, c : 2 * c])
    side_b = jnp.where(even, out[:, 2 * c : 3 * c], out[:, 3 * c :])
    return jnp.where(in_a, side_a, side_b)


def kept(state, facts):
    wave_a, wave_b, _, r, in_a, _, _ = facts
    columns = state.shape[1]
    imaginary = lax.broadcasted_iota(jnp.int32, state.shape, 1) >= columns // 2
    wave = jnp.where(in_a, wave_a, wave_b)
    dropped = jnp.logical_or(jnp.logical_and(wave == 0, imaginary), r > M)
    return jnp.where(dropped, 0.0, state)


def halves(x):
    high = x.astype(jnp.bfloat16)
    low = (x - high.astype(jnp.float32)).astype(jnp.bfloat16)
    return jnp.concatenate([high, low], axis=1)


def dot_split(x, both):
    out = jnp.dot(halves(x), both, preferred_element_type=jnp.float32)
    c = out.shape[1] // 2
    return out[:, :c] + out[:, c:]


def updated(state, change, facts, mixing, mixing_t, speeds):
    wave_a, wave_b, _, _, in_a, k, _ = facts
    combined = state + change
    projected = dot_split(combined, mixing[...])
    n = (jnp.where(in_a, wave_a, wave_b) + k).astype(jnp.float32)
    stiffness = speeds[...] * (n * (n + 1.0))
    weighted = projected * (stiffness / (1.0 + stiffness))
    returned = dot_split(weighted, mixing_t[...])
    return kept(combined - returned, facts)


def first_kernel(sz, waves, spectra, turn, table_t, state_ref, send, stage):
    columns = spectra.shape[2]

    def body(i, _):
        facts = row_facts(waves, i, columns)
        length, in_a = facts[2], facts[4]
        blank = jnp.zeros((ROWS - M, columns), jnp.float32)
        rows_a = jnp.concatenate([spectra[2 * i], blank], axis=0)
        rows_b = jnp.concatenate([spectra[2 * i + 1], blank], axis=0)
        packed = jnp.where(in_a, rows_a, pltpu.roll(rows_b, length, 0))
        state = kept(dot_split(packed, turn[...]), facts)
        state_ref[i] = state
        send_rows(sz, 0, i, state, facts, table_t, stage)
        return 0

    lax.fori_loop(0, sz.pairs, body, 0)
    flush(sz, 0, stage, send)


def inverse_kernel(sz, part, waves, state, table_t, send, stage):
    def body(i, _):
        facts = row_facts(waves, i, state.shape[2])
        send_rows(sz, part, i, state[i], facts, table_t, stage)
        return 0

    lax.fori_loop(0, sz.pairs, body, 0)
    flush(sz, part, stage, send)


def forward_kernel(sz, part, waves, state, recv, table, weights, out, stage):
    load_rows(sz, part, recv, stage)

    def body(i, _):
        facts = row_facts(waves, i, state.shape[2])
        out[i] = state[i] + change_rows(sz, part, i, facts, table, weights, stage)
        return 0

    lax.fori_loop(0, sz.pairs, body, 0)


def middle_kernel(
    sz, waves, partial, recv, table, table_t, weights, mixing, mixing_t, speeds,
    state_out, send, stage_in, stage,
):
    columns = partial.shape[2]
    part = sz.parts - 1
    load_rows(sz, part, recv, stage_in)

    def body(i, _):
        facts = row_facts(waves, i, columns)
        change = change_rows(sz, part, i, facts, table, weights, stage_in)
        state = updated(partial[i], change, facts, mixing, mixing_t, speeds)
        state_out[i] = state
        send_rows(sz, 0, i, state, facts, table_t, stage)
        return 0

    lax.fori_loop(0, sz.pairs, body, 0)
    flush(sz, 0, stage, send)


def last_kernel(
    sz, waves, partial, recv, table, weights, mixing, mixing_t, speeds, turn_t, out, stage_in
):
    columns = partial.shape[2]
    part = sz.parts - 1
    load_rows(sz, part, recv, stage_in)

    def body(i, _):
        facts = row_facts(waves, i, columns)
        wave_a, wave_b, length, r = facts[:4]
        change = change_rows(sz, part, i, facts, table, weights, stage_in)
        state = updated(partial[i], change, facts, mixing, mixing_t, speeds)
        state = dot_split(state, turn_t[...])
        out[2 * i] = jnp.where(r < length, state, 0.0)[:M]
        rolled = pltpu.roll(state, ROWS - length, 0)
        out[2 * i + 1] = jnp.where(r < M - wave_b, rolled, 0.0)[:M]
        return 0

    lax.fori_loop(0, sz.pairs, body, 0)


def grid_kernel(
    sz, part, flip, recv, traj, synth, slope, scale, send, stage_in, stage, lhs, values, slopes, force
):
    lanes = recv.shape[2]
    rows = lanes // 2
    lats = sz.part_lats[part]
    block = sz.block(part)
    groups = -(-lats // sz.group)

    def load(d, _):
        stage_in[pl.ds(d * block, block), :] = recv[d].astype(jnp.float32)
        return 0

    lax.fori_loop(0, sz.space, load, 0)
    blank = jnp.zeros((DEPTH - M, lanes), jnp.float32)

    def body(g, _):
        for q in range(sz.group):
            t = jnp.minimum(g * sz.group + q, lats - 1)
            rows_t = stage_in[pl.ds(t, M, stride=lats), :]
            turned = jnp.transpose(jnp.concatenate([rows_t, blank], axis=0)).astype(jnp.bfloat16)
            lhs[q * rows : (q + 1) * rows, :DEPTH] = turned[:rows]
            lhs[q * rows : (q + 1) * rows, DEPTH:] = turned[rows:]
        left = lhs[...]
        values[...] = jnp.dot(left, synth[...], preferred_element_type=jnp.float32)
        slopes[...] = jnp.dot(left, slope[...], preferred_element_type=jnp.float32)
        for q in range(sz.group):
            t = jnp.minimum(g * sz.group + q, lats - 1)
            here = jnp.where(flip[0] == 1, lats - 1 - t, t)
            wind = traj[here, 0].astype(jnp.float32)
            for v in range(VARS):
                lo = q * rows + v * LEV
                other = traj[here, 1 + (v + 1) % VARS].astype(jnp.float32)
                force[lo : lo + LEV, :] = (
                    wind * slopes[lo : lo + LEV, :] + other * values[lo : lo + LEV, :]
                ).astype(jnp.bfloat16)
        forcing = force[...]
        spectrum = [
            lax.dot_general(
                synth[c * DEPTH : c * DEPTH + M, :],
                forcing,
                (((1,), (1,)), ((), ())),
                preferred_element_type=jnp.float32,
            )
            * scale[...][:, :1]
            for c in range(2)
        ]
        left_side = lax.broadcasted_iota(jnp.int32, (M, lanes), 1) < rows
        for q in range(0, sz.group, 2):
            re = spectrum[0][:, q * rows : (q + 2) * rows]
            im = spectrum[1][:, q * rows : (q + 2) * rows]
            pair = (
                jnp.where(left_side, re, pltpu.roll(im, rows, 1)),
                jnp.where(left_side, pltpu.roll(re, rows, 1), im),
            )
            for o in range(2):
                t = g * sz.group + q + o

                def store(t=t, value=pair[o]):
                    stage[pl.ds(t, M, stride=lats), :] = value

                if (groups - 1) * sz.group + q + o < lats:
                    store()
                else:
                    pl.when(t < lats)(store)
        return 0

    lax.fori_loop(0, groups, body, 0)

    def out(d, _):
        send[d] = stage[pl.ds(d * block, block), :].astype(jnp.bfloat16)
        return 0

    lax.fori_loop(0, sz.space, out, 0)


def grid_stage(sz, part, flip, recv, traj, synth, slope, scale):
    lanes = recv.shape[2]
    wide = sz.group * lanes // 2
    count = M * sz.part_lats[part]
    return pl.pallas_call(
        lambda *refs: grid_kernel(sz, part, *refs),
        out_shape=jax.ShapeDtypeStruct(recv.shape, jnp.bfloat16),
        in_specs=smem(1) + vmem(5),
        out_specs=vmem(1)[0],
        scratch_shapes=[
            pltpu.VMEM((count, lanes), jnp.float32),
            pltpu.VMEM((count, lanes), jnp.float32),
            pltpu.VMEM((wide, 2 * DEPTH), jnp.bfloat16),
            pltpu.VMEM((wide, NLON), jnp.float32),
            pltpu.VMEM((wide, NLON), jnp.float32),
            pltpu.VMEM((wide, NLON), jnp.bfloat16),
        ],
        compiler_params=params(),
        cost_estimate=cost(9.0),
        name="grid_stage",
    )(flip, recv, traj, synth, slope, scale)


def zonal_tables(wave_list):
    cell_index = jnp.arange(NLON, dtype=jnp.int32)
    wave_pad = jnp.concatenate([wave_list, jnp.zeros((DEPTH - M,), jnp.int32)])
    phase_index = wave_pad[:, None] * cell_index[None, :] % NLON
    angles = phase_index.astype(jnp.float32) * (2.0 * math.pi / NLON)
    factor = jnp.where(wave_pad == 0, 1.0, 2.0).astype(jnp.float32)
    inside = (jnp.arange(DEPTH) < M).astype(jnp.float32)
    gain = (factor * inside)[:, None]
    cosine, sine = gain * jnp.cos(angles), gain * jnp.sin(angles)
    wave = wave_pad.astype(jnp.float32)[:, None]
    synth = jnp.concatenate([-cosine, sine], axis=0).astype(jnp.bfloat16)
    slope = jnp.concatenate([wave * sine, wave * cosine], axis=0).astype(jnp.bfloat16)
    scale = jnp.broadcast_to((-1.0 / (NLON * factor[:M]))[:, None], (M, 128))
    return synth, slope, scale


def column_turn(columns):
    turn = np.zeros((columns, columns), np.float32)
    for c in range(columns):
        part, row = c % 2, c // 2
        turn[c, part * (columns // 2) + row] = 1.0
    return turn


def split_matrix(matrix):
    high = matrix.astype(jnp.bfloat16)
    low = (matrix - high.astype(jnp.float32)).astype(jnp.bfloat16)
    top = jnp.concatenate([high, low], axis=1)
    bottom = jnp.concatenate([high, jnp.zeros_like(low)], axis=1)
    return jnp.concatenate([top, bottom], axis=0)


def sectoral(wave, log_sine):
    gammas = jax.scipy.special.gammaln
    start = 0.5 * (
        gammas(wave + 1.5) - gammas(wave + 1.0) - gammas(jnp.float32(1.5))
    ) - 0.5 * math.log(2.0)
    return (start[:, None] + wave[:, None] * log_sine[None, :]) * (1.0 / math.log(2.0))


def shards(sz, spectra, wave_order, traj_wind, traj_state, vertical_modes, mode_speeds):
    columns = spectra.shape[2]
    rank = lax.axis_index("space")
    waves = lax.dynamic_slice_in_dim(wave_order, rank * sz.slots, sz.slots)

    place = np.arange(sz.north)
    part, within = place // sz.part_rows, place % sz.part_rows
    block, inner = within // sz.part_pad, within % sz.part_pad
    real = inner < np.asarray(sz.part_lats)[part]
    index = block * sz.lats + np.asarray(sz.part_start)[part] + inner
    colat = np.where(real, (index + 0.5) * (math.pi / NLAT), math.pi / 2)
    cosines = jnp.asarray(np.cos(colat), jnp.float32)[None, :]
    log_sine = jnp.asarray(np.log(np.sin(colat)), jnp.float32)
    weights = jnp.asarray(
        np.broadcast_to((np.sin(colat) * (math.pi / NLAT) * real)[:, None], (sz.north, columns)),
        jnp.float32,
    )

    pair_waves = jnp.zeros((sz.pair_pad, 2), jnp.int32).at[: sz.pairs].set(waves.reshape(-1, 2))
    pair_waves = pair_waves.astype(jnp.float32)
    wide_a = jnp.broadcast_to(pair_waves[:, :1], (sz.pair_pad, 128))
    wide_b = jnp.broadcast_to(pair_waves[:, 1:], (sz.pair_pad, 128))
    table, table_t = make_tables(
        sz, wide_a, wide_b, sectoral(pair_waves[:, 0], log_sine), sectoral(pair_waves[:, 1], log_sine), cosines
    )

    turn = column_turn(columns)
    same = np.kron(np.eye(columns // LEV, dtype=np.float32), np.ones((LEV, LEV), np.float32))
    mixing = split_matrix(jnp.tile(vertical_modes.T, (columns // LEV, columns // LEV)) * same)
    mixing_t = split_matrix(jnp.tile(vertical_modes, (columns // LEV, columns // LEV)) * same)
    speeds = jnp.tile(mode_speeds, columns // LEV)[None, :]
    turn, turn_t = split_matrix(jnp.asarray(turn)), split_matrix(jnp.asarray(turn.T))

    synth, slope, scale = zonal_tables(wave_order)
    south = rank >= sz.half
    flip = jnp.where(south, 1, 0).astype(jnp.int32).reshape(1)

    def stages(part):
        return pltpu.VMEM((sz.space, sz.block_pad(part), columns), jnp.float32)

    def sends(part):
        return jax.ShapeDtypeStruct((sz.space, sz.block(part), columns), jnp.bfloat16)

    state_shape = jax.ShapeDtypeStruct((sz.pairs, ROWS, columns), jnp.float32)

    def call(body, out_shape, args, scratch, microseconds, name):
        single = not isinstance(out_shape, tuple)
        outs = vmem(1)[0] if single else tuple(vmem(len(out_shape)))
        return pl.pallas_call(
            body,
            out_shape=out_shape,
            in_specs=smem(1) + vmem(len(args) - 1),
            out_specs=outs,
            scratch_shapes=scratch,
            compiler_params=params(),
            cost_estimate=cost(microseconds),
            name=name,
        )(*args)

    def gather(step, part):
        local = jnp.concatenate([traj_wind[step][None], traj_state[step]], axis=0)
        start, size = sz.part_start[part], sz.part_lats[part]
        at = jnp.where(south, sz.lats - start - size, start)
        local = lax.dynamic_slice_in_dim(local, at, size, axis=2)
        traj = lax.all_gather(local, "pert", axis=1, tiled=True)
        return jnp.transpose(traj, (2, 0, 1, 3))

    def transpose(value):
        return lax.all_to_all(value, "space", 0, 0, tiled=True)

    def inverse_rest(state):
        return call(
            lambda *refs: inverse_kernel(sz, 1, *refs),
            sends(1), (waves, state, table_t), [stages(1)], 6.0, "inverse_rest",
        )

    state, send_0 = call(
        lambda *refs: first_kernel(sz, *refs),
        (state_shape, sends(0)), (waves, spectra, turn, table_t), [stages(0)], 8.0, "first_inverse",
    )
    for step in range(STEPS):
        recv_0 = transpose(send_0)
        recv_1 = transpose(inverse_rest(state))
        back_0 = transpose(
            grid_stage(sz, 0, flip, recv_0, gather(step, 0), synth, slope, scale)
        )
        back_1 = transpose(
            grid_stage(sz, 1, flip, recv_1, gather(step, 1), synth, slope, scale)
        )
        partial = call(
            lambda *refs: forward_kernel(sz, 0, *refs),
            state_shape, (waves, state, back_0, table, weights), [stages(0)], 6.0, "forward_part",
        )
        if step < STEPS - 1:
            state, send_0 = call(
                lambda *refs: middle_kernel(sz, *refs),
                (state_shape, sends(0)),
                (waves, partial, back_1, table, table_t, weights, mixing, mixing_t, speeds),
                [stages(1), stages(0)], 12.0, "forward_inverse",
            )
        else:
            out = call(
                lambda *refs: last_kernel(sz, *refs),
                jax.ShapeDtypeStruct(spectra.shape, jnp.float32),
                (waves, partial, back_1, table, weights, mixing, mixing_t, speeds, turn_t),
                [stages(1)], 10.0, "forward_last",
            )
    return out


def solution(mesh):
    sz = Sizes(mesh.shape["space"])
    placed = (
        P("space", None, "pert"),
        P(),
        P(None, "pert", "space", None),
        P(None, None, "pert", "space", None),
        P(),
        P(),
    )
    return jax.shard_map(
        lambda *args: shards(sz, *args),
        mesh=mesh,
        in_specs=placed,
        out_specs=P("space", None, "pert"),
        check_vma=False,
    )
```

```python
import math

import jax
import jax.numpy as jnp
import numpy as np
from jax import lax
from jax.experimental import pallas as pl
from jax.experimental.pallas import tpu as pltpu
from jax.sharding import PartitionSpec as P

NLAT = 480
NLON = 960
M = 320
VARS = 2
LEV = 32
STEPS = 2
ROWS = 336
EACH = ROWS // 2
DEPTH = 384
VMEM_BYTES = 48 * 1024 * 1024
BIG = 2.0**32


def params():
    return pltpu.CompilerParams(vmem_limit_bytes=VMEM_BYTES)


def cost(microseconds):
    return pl.CostEstimate(flops=int(microseconds * 1.0e9), bytes_accessed=1 << 20, transcendentals=0)


def vmem(count):
    return [pl.BlockSpec(memory_space=pltpu.VMEM)] * count


def smem(count):
    return [pl.BlockSpec(memory_space=pltpu.SMEM)] * count


class Sizes:
    def __init__(self, space):
        self.space = space
        self.slots = M // space
        self.pairs = self.slots // 2
        self.lats = NLAT // space
        self.half = space // 2
        self.parts = 2
        self.part_pad = -(-self.lats // (8 * self.parts)) * 8
        first = -(-self.lats // self.parts)
        self.part_lats = [first, self.lats - first]
        self.part_start = [0, first]
        self.part_rows = self.half * self.part_pad
        self.north = self.parts * self.part_rows
        self.pair_pad = -(-self.pairs // 8) * 8
        self.group = 8

    def block(self, part):
        return self.slots * self.part_lats[part]

    def block_pad(self, part):
        last = (self.slots - 1) * self.part_lats[part] + self.part_pad
        return -(-last // 8) * 8


def table_kernel(sz, wave_a, wave_b, start_a, start_b, cosines, table, table_t, rows_ref):
    wide = range(sz.north // 128)
    wa, wb = wave_a[...], wave_b[...]
    length = M - wa

    def tile(ref, c):
        return ref[:, c * 128 : (c + 1) * 128]

    def body(block, carry):
        cur, prev, shift, inv_prev = carry
        second = (block * 8).astype(jnp.float32) > length
        cur, prev, shift, base, base_b = list(cur), list(prev), list(shift), [], []
        for c in wide:
            big = jnp.maximum(jnp.abs(cur[c]), jnp.abs(prev[c])) > BIG
            scale = jnp.where(big, 1.0 / BIG, 1.0)
            cur[c], prev[c] = cur[c] * scale, prev[c] * scale
            shift[c] = shift[c] + jnp.where(big, 32.0, 0.0)
            start = jnp.where(second, tile(start_b, c), tile(start_a, c))
            base.append(jnp.exp2(0.5 * (start + shift[c])))
            base_b.append(jnp.exp2(0.5 * tile(start_b, c)))
        for j in range(8):
            r = (block * 8 + j).astype(jnp.float32)
            fresh = r == length
            begin = jnp.logical_or(fresh, r == 0.0)
            in_b = r >= length
            m = jnp.where(in_b, wb, wa)
            k = jnp.where(in_b, r - length, r)
            n = m + k
            den = k * (m + n)
            num = 4.0 * n * n - 1.0
            root = lax.rsqrt(jnp.maximum(num * den, 1.0))
            upper = num * root
            lower = upper * inv_prev
            inv_prev = den * root
            for c in wide:
                new = upper * tile(cosines, c) * cur[c] - lower * prev[c]
                prev[c] = cur[c]
                cur[c] = jnp.where(begin, 1.0, new)
                shift[c] = jnp.where(fresh, 0.0, shift[c])
                base[c] = jnp.where(fresh, base_b[c], base[c])
                at = (j % 2) * EACH + block * 4 + j // 2
                rows_ref[c, pl.ds(at, sz.pair_pad, stride=ROWS), :] = (cur[c] * base[c]) * base[c]
        return tuple(cur), tuple(prev), tuple(shift), inv_prev

    zero = jnp.zeros((sz.pair_pad, 128), jnp.float32)
    zeros = tuple(zero for _ in wide)
    lax.fori_loop(0, ROWS // 8, body, (zeros, zeros, zeros, zero))
    index = lax.broadcasted_iota(jnp.int32, (EACH, sz.north), 0)
    blank = jnp.zeros((256 - EACH, sz.north), jnp.float32)

    def emit(i, _):
        for p in range(2):
            at = i * ROWS + p * EACH
            full = jnp.concatenate([rows_ref[c, pl.ds(at, EACH), :] for c in wide], axis=1)
            full = jnp.where(2 * index + p <= M, full, 0.0)
            table[i, p] = full.astype(jnp.bfloat16)
            turned = jnp.transpose(jnp.concatenate([full, blank], axis=0))
            table_t[i, p] = turned.astype(jnp.bfloat16)
        return 0

    lax.fori_loop(0, sz.pairs, emit, 0)


def make_tables(sz, wave_a, wave_b, log_a, log_b, cosines):
    return pl.pallas_call(
        lambda *refs: table_kernel(sz, *refs),
        out_shape=(
            jax.ShapeDtypeStruct((sz.pairs, 2, EACH, sz.north), jnp.bfloat16),
            jax.ShapeDtypeStruct((sz.pairs, 2, sz.north, 256), jnp.bfloat16),
        ),
        in_specs=vmem(5),
        out_specs=tuple(vmem(2)),
        scratch_shapes=[pltpu.VMEM((sz.north // 128, sz.pair_pad * ROWS, 128), jnp.float32)],
        compiler_params=params(),
        name="legendre_tables",
    )(wave_a, wave_b, log_a, log_b, cosines)


def row_facts(waves, i, columns):
    wave_a, wave_b = waves[2 * i], waves[2 * i + 1]
    length = M - wave_a
    q = lax.broadcasted_iota(jnp.int32, (ROWS, columns), 0)
    r = jnp.where(q < EACH, 2 * q, 2 * (q - EACH) + 1)
    in_a = r < length
    k = jnp.where(in_a, r, r - length)
    odd = jnp.bitwise_and(length, 1).astype(jnp.float32)
    sign_b = 1.0 - 2.0 * odd
    return wave_a, wave_b, length, r, in_a, k, sign_b


def send_rows(sz, part, i, state, facts, table_t, stage):
    in_a, sign_b = facts[4], facts[6]
    columns = state.shape[1]
    rhs = jnp.concatenate(
        [
            jnp.where(in_a, state, 0.0).astype(jnp.bfloat16),
            jnp.where(in_a, 0.0, state).astype(jnp.bfloat16),
        ],
        axis=1,
    )
    blank = jnp.zeros((256 - EACH, 2 * columns), jnp.bfloat16)
    sums = []
    for p in range(2):
        rows = table_t[i, p, part * sz.part_rows : (part + 1) * sz.part_rows, :]
        side = jnp.concatenate([rhs[p * EACH : (p + 1) * EACH], blank], axis=0)
        sums.append(jnp.dot(rows, side, preferred_element_type=jnp.float32))
    size = sz.part_pad
    plus, minus = sums[0] + sums[1], sums[0] - sums[1]
    for s in range(2):
        north = plus[:, s * columns : (s + 1) * columns]
        south = minus[:, s * columns : (s + 1) * columns]
        south = south * sign_b if s == 1 else south
        at = (2 * i + s) * sz.part_lats[part]
        for b in range(sz.half):
            lo = b * size
            stage[b, pl.ds(at, size), :] = north[lo : lo + size]
            stage[sz.space - 1 - b, pl.ds(at, size), :] = south[lo : lo + size]


def flush(sz, part, stage, send):
    def body(d, _):
        send[d] = stage[d, : sz.block(part), :].astype(jnp.bfloat16)
        return 0

    lax.fori_loop(0, sz.space, body, 0)


def load_rows(sz, part, recv, stage):
    rows = sz.block_pad(part)

    def body(d, _):
        stage[d, rows - 16 : rows, :] = jnp.zeros((16, stage.shape[2]), jnp.float32)
        stage[d, : sz.block(part), :] = recv[d].astype(jnp.float32)
        return 0

    lax.fori_loop(0, sz.space, body, 0)


def change_rows(sz, part, i, facts, table, weights, stage):
    in_a, sign_b = facts[4], facts[6]
    lo = part * sz.part_rows
    w = weights[lo : lo + sz.part_rows, :]
    size = sz.part_pad
    plus, minus = [], []
    for s in range(2):
        at = (2 * i + s) * sz.part_lats[part]
        north = jnp.concatenate([stage[b, pl.ds(at, size), :] for b in range(sz.half)], axis=0)
        south = jnp.concatenate(
            [stage[sz.space - 1 - b, pl.ds(at, size), :] for b in range(sz.half)], axis=0
        )
        north, south = north * w, south * (w * sign_b if s == 1 else w)
        plus.append((north + south).astype(jnp.bfloat16))
        minus.append((north - south).astype(jnp.bfloat16))
    pieces = []
    for p, rows in enumerate((plus, minus)):
        out = jnp.dot(
            table[i, p, :, lo : lo + sz.part_rows],
            jnp.concatenate(rows, axis=1),
            preferred_element_type=jnp.float32,
        )
        c = out.shape[1] // 2
        mine = in_a[p * EACH : (p + 1) * EACH]
        pieces.append(jnp.where(mine, out[:, :c], out[:, c:]))
    return jnp.concatenate(pieces, axis=0)


def kept(state, facts):
    wave_a, wave_b, _, r, in_a = facts[:5]
    columns = state.shape[1]
    imaginary = lax.broadcasted_iota(jnp.int32, state.shape, 1) >= columns // 2
    wave = jnp.where(in_a, wave_a, wave_b)
    dropped = jnp.logical_or(jnp.logical_and(wave == 0, imaginary), r > M)
    return jnp.where(dropped, 0.0, state)


def halves(x):
    high = x.astype(jnp.bfloat16)
    low = (x - high.astype(jnp.float32)).astype(jnp.bfloat16)
    return jnp.concatenate([high, low], axis=1)


def dot_split(x, both):
    out = jnp.dot(halves(x), both, preferred_element_type=jnp.float32)
    c = out.shape[1] // 2
    return out[:, :c] + out[:, c:]


def updated(state, change, facts, mixing, mixing_t, speeds):
    wave_a, wave_b, _, _, in_a, k = facts[:6]
    combined = state + change
    projected = dot_split(combined, mixing[...])
    n = (jnp.where(in_a, wave_a, wave_b) + k).astype(jnp.float32)
    stiffness = speeds[...] * (n * (n + 1.0))
    weighted = projected * (stiffness / (1.0 + stiffness))
    returned = dot_split(weighted, mixing_t[...])
    return kept(combined - returned, facts)


def first_kernel(sz, waves, spectra, turn, table_t, state_ref, send, stage, mixed):
    columns = spectra.shape[2]

    def body(i, _):
        facts = row_facts(waves, i, columns)
        length = facts[2]
        natural = lax.broadcasted_iota(jnp.int32, (ROWS, columns), 0)
        blank = jnp.zeros((ROWS - M, columns), jnp.float32)
        rows_a = jnp.concatenate([spectra[2 * i], blank], axis=0)
        rows_b = jnp.concatenate([spectra[2 * i + 1], blank], axis=0)
        packed = jnp.where(natural < length, rows_a, pltpu.roll(rows_b, length, 0))
        mixed[...] = dot_split(packed, turn[...])
        state = jnp.concatenate([mixed[pl.ds(p, EACH, stride=2), :] for p in range(2)], axis=0)
        state = kept(state, facts)
        state_ref[i] = state
        send_rows(sz, 0, i, state, facts, table_t, stage)
        return 0

    lax.fori_loop(0, sz.pairs, body, 0)
    flush(sz, 0, stage, send)


def inverse_kernel(sz, part, waves, state, table_t, send, stage):
    def body(i, _):
        facts = row_facts(waves, i, state.shape[2])
        send_rows(sz, part, i, state[i], facts, table_t, stage)
        return 0

    lax.fori_loop(0, sz.pairs, body, 0)
    flush(sz, part, stage, send)


def forward_kernel(sz, part, waves, state, recv, table, weights, out, stage):
    load_rows(sz, part, recv, stage)

    def body(i, _):
        facts = row_facts(waves, i, state.shape[2])
        out[i] = state[i] + change_rows(sz, part, i, facts, table, weights, stage)
        return 0

    lax.fori_loop(0, sz.pairs, body, 0)


def middle_kernel(
    sz, waves, partial, recv, table, table_t, weights, mixing, mixing_t, speeds,
    state_out, send, stage_in, stage,
):
    columns = partial.shape[2]
    part = sz.parts - 1
    load_rows(sz, part, recv, stage_in)

    def body(i, _):
        facts = row_facts(waves, i, columns)
        change = change_rows(sz, part, i, facts, table, weights, stage_in)
        state = updated(partial[i], change, facts, mixing, mixing_t, speeds)
        state_out[i] = state
        send_rows(sz, 0, i, state, facts, table_t, stage)
        return 0

    lax.fori_loop(0, sz.pairs, body, 0)
    flush(sz, 0, stage, send)


def last_kernel(
    sz, waves, partial, recv, table, weights, mixing, mixing_t, speeds, turn_t, out, stage_in, mixed
):
    columns = partial.shape[2]
    part = sz.parts - 1
    load_rows(sz, part, recv, stage_in)

    def body(i, _):
        facts = row_facts(waves, i, columns)
        wave_b, length = facts[1:3]
        r = lax.broadcasted_iota(jnp.int32, (ROWS, columns), 0)
        change = change_rows(sz, part, i, facts, table, weights, stage_in)
        state = updated(partial[i], change, facts, mixing, mixing_t, speeds)
        state = dot_split(state, turn_t[...])
        for p in range(2):
            mixed[pl.ds(p, EACH, stride=2), :] = state[p * EACH : (p + 1) * EACH]
        state = mixed[...]
        out[2 * i] = jnp.where(r < length, state, 0.0)[:M]
        rolled = pltpu.roll(state, ROWS - length, 0)
        out[2 * i + 1] = jnp.where(r < M - wave_b, rolled, 0.0)[:M]
        return 0

    lax.fori_loop(0, sz.pairs, body, 0)


def grid_kernel(
    sz, part, flip, recv, traj, synth, slope, scale, send, stage_in, stage, lhs, values, slopes, force
):
    lanes = recv.shape[2]
    rows = lanes // 2
    lats = sz.part_lats[part]
    block = sz.block(part)
    groups = -(-lats // sz.group)

    def load(d, _):
        stage_in[pl.ds(d * block, block), :] = recv[d].astype(jnp.float32)
        return 0

    lax.fori_loop(0, sz.space, load, 0)
    blank = jnp.zeros((DEPTH - M, lanes), jnp.float32)

    def body(g, _):
        for q in range(sz.group):
            t = jnp.minimum(g * sz.group + q, lats - 1)
            rows_t = stage_in[pl.ds(t, M, stride=lats), :]
            turned = jnp.transpose(jnp.concatenate([rows_t, blank], axis=0)).astype(jnp.bfloat16)
            lhs[q * rows : (q + 1) * rows, :DEPTH] = turned[:rows]
            lhs[q * rows : (q + 1) * rows, DEPTH:] = turned[rows:]
        left = lhs[...]
        values[...] = jnp.dot(left, synth[...], preferred_element_type=jnp.float32)
        slopes[...] = jnp.dot(left, slope[...], preferred_element_type=jnp.float32)
        for q in range(sz.group):
            t = jnp.minimum(g * sz.group + q, lats - 1)
            here = jnp.where(flip[0] == 1, lats - 1 - t, t)
            wind = traj[here, 0].astype(jnp.float32)
            for v in range(VARS):
                lo = q * rows + v * LEV
                other = traj[here, 1 + (v + 1) % VARS].astype(jnp.float32)
                force[lo : lo + LEV, :] = (
                    wind * slopes[lo : lo + LEV, :] + other * values[lo : lo + LEV, :]
                ).astype(jnp.bfloat16)
        forcing = force[...]
        spectrum = [
            lax.dot_general(
                synth[c * DEPTH : c * DEPTH + M, :],
                forcing,
                (((1,), (1,)), ((), ())),
                preferred_element_type=jnp.float32,
            )
            * scale[...][:, :1]
            for c in range(2)
        ]
        left_side = lax.broadcasted_iota(jnp.int32, (M, lanes), 1) < rows
        for q in range(0, sz.group, 2):
            re = spectrum[0][:, q * rows : (q + 2) * rows]
            im = spectrum[1][:, q * rows : (q + 2) * rows]
            pair = (
                jnp.where(left_side, re, pltpu.roll(im, rows, 1)),
                jnp.where(left_side, pltpu.roll(re, rows, 1), im),
            )
            for o in range(2):
                t = g * sz.group + q + o

                def store(t=t, value=pair[o]):
                    stage[pl.ds(t, M, stride=lats), :] = value

                if (groups - 1) * sz.group + q + o < lats:
                    store()
                else:
                    pl.when(t < lats)(store)
        return 0

    lax.fori_loop(0, groups, body, 0)

    def out(d, _):
        send[d] = stage[pl.ds(d * block, block), :].astype(jnp.bfloat16)
        return 0

    lax.fori_loop(0, sz.space, out, 0)


def grid_stage(sz, part, flip, recv, traj, synth, slope, scale):
    lanes = recv.shape[2]
    wide = sz.group * lanes // 2
    count = M * sz.part_lats[part]
    return pl.pallas_call(
        lambda *refs: grid_kernel(sz, part, *refs),
        out_shape=jax.ShapeDtypeStruct(recv.shape, jnp.bfloat16),
        in_specs=smem(1) + vmem(5),
        out_specs=vmem(1)[0],
        scratch_shapes=[
            pltpu.VMEM((count, lanes), jnp.float32),
            pltpu.VMEM((count, lanes), jnp.float32),
            pltpu.VMEM((wide, 2 * DEPTH), jnp.bfloat16),
            pltpu.VMEM((wide, NLON), jnp.float32),
            pltpu.VMEM((wide, NLON), jnp.float32),
            pltpu.VMEM((wide, NLON), jnp.bfloat16),
        ],
        compiler_params=params(),
        cost_estimate=cost(9.0),
        name="grid_stage",
    )(flip, recv, traj, synth, slope, scale)


def zonal_tables(wave_list):
    cell_index = jnp.arange(NLON, dtype=jnp.int32)
    wave_pad = jnp.concatenate([wave_list, jnp.zeros((DEPTH - M,), jnp.int32)])
    phase_index = wave_pad[:, None] * cell_index[None, :] % NLON
    angles = phase_index.astype(jnp.float32) * (2.0 * math.pi / NLON)
    factor = jnp.where(wave_pad == 0, 1.0, 2.0).astype(jnp.float32)
    inside = (jnp.arange(DEPTH) < M).astype(jnp.float32)
    gain = (factor * inside)[:, None]
    cosine, sine = gain * jnp.cos(angles), gain * jnp.sin(angles)
    wave = wave_pad.astype(jnp.float32)[:, None]
    synth = jnp.concatenate([-cosine, sine], axis=0).astype(jnp.bfloat16)
    slope = jnp.concatenate([wave * sine, wave * cosine], axis=0).astype(jnp.bfloat16)
    scale = jnp.broadcast_to((-1.0 / (NLON * factor[:M]))[:, None], (M, 128))
    return synth, slope, scale


def column_turn(columns):
    turn = np.zeros((columns, columns), np.float32)
    for c in range(columns):
        part, row = c % 2, c // 2
        turn[c, part * (columns // 2) + row] = 1.0
    return turn


def split_matrix(matrix):
    high = matrix.astype(jnp.bfloat16)
    low = (matrix - high.astype(jnp.float32)).astype(jnp.bfloat16)
    top = jnp.concatenate([high, low], axis=1)
    bottom = jnp.concatenate([high, jnp.zeros_like(low)], axis=1)
    return jnp.concatenate([top, bottom], axis=0)


def sectoral(wave, log_sine):
    gammas = jax.scipy.special.gammaln
    start = 0.5 * (
        gammas(wave + 1.5) - gammas(wave + 1.0) - gammas(jnp.float32(1.5))
    ) - 0.5 * math.log(2.0)
    return (start[:, None] + wave[:, None] * log_sine[None, :]) * (1.0 / math.log(2.0))


def shards(sz, spectra, wave_order, traj_wind, traj_state, vertical_modes, mode_speeds):
    columns = spectra.shape[2]
    rank = lax.axis_index("space")
    waves = lax.dynamic_slice_in_dim(wave_order, rank * sz.slots, sz.slots)

    place = np.arange(sz.north)
    part, within = place // sz.part_rows, place % sz.part_rows
    block, inner = within // sz.part_pad, within % sz.part_pad
    real = inner < np.asarray(sz.part_lats)[part]
    index = block * sz.lats + np.asarray(sz.part_start)[part] + inner
    colat = np.where(real, (index + 0.5) * (math.pi / NLAT), math.pi / 2)
    cosines = jnp.asarray(np.cos(colat), jnp.float32)[None, :]
    log_sine = jnp.asarray(np.log(np.sin(colat)), jnp.float32)
    weights = jnp.asarray(
        np.broadcast_to((np.sin(colat) * (math.pi / NLAT) * real)[:, None], (sz.north, columns)),
        jnp.float32,
    )

    pair_waves = jnp.zeros((sz.pair_pad, 2), jnp.int32).at[: sz.pairs].set(waves.reshape(-1, 2))
    pair_waves = pair_waves.astype(jnp.float32)
    wide_a = jnp.broadcast_to(pair_waves[:, :1], (sz.pair_pad, 128))
    wide_b = jnp.broadcast_to(pair_waves[:, 1:], (sz.pair_pad, 128))
    table, table_t = make_tables(
        sz, wide_a, wide_b, sectoral(pair_waves[:, 0], log_sine), sectoral(pair_waves[:, 1], log_sine), cosines
    )

    turn = column_turn(columns)
    same = np.kron(np.eye(columns // LEV, dtype=np.float32), np.ones((LEV, LEV), np.float32))
    mixing = split_matrix(jnp.tile(vertical_modes.T, (columns // LEV, columns // LEV)) * same)
    mixing_t = split_matrix(jnp.tile(vertical_modes, (columns // LEV, columns // LEV)) * same)
    speeds = jnp.tile(mode_speeds, columns // LEV)[None, :]
    turn, turn_t = split_matrix(jnp.asarray(turn)), split_matrix(jnp.asarray(turn.T))

    synth, slope, scale = zonal_tables(wave_order)
    south = rank >= sz.half
    flip = jnp.where(south, 1, 0).astype(jnp.int32).reshape(1)

    def stages(part):
        return pltpu.VMEM((sz.space, sz.block_pad(part), columns), jnp.float32)

    def sends(part):
        return jax.ShapeDtypeStruct((sz.space, sz.block(part), columns), jnp.bfloat16)

    state_shape = jax.ShapeDtypeStruct((sz.pairs, ROWS, columns), jnp.float32)

    def call(body, out_shape, args, scratch, microseconds, name):
        single = not isinstance(out_shape, tuple)
        outs = vmem(1)[0] if single else tuple(vmem(len(out_shape)))
        return pl.pallas_call(
            body,
            out_shape=out_shape,
            in_specs=smem(1) + vmem(len(args) - 1),
            out_specs=outs,
            scratch_shapes=scratch,
            compiler_params=params(),
            cost_estimate=cost(microseconds),
            name=name,
        )(*args)

    count = traj_wind.shape[1]
    members = LEV // count
    member = lax.axis_index("pert")

    def gather(step, part):
        local = jnp.concatenate([traj_wind[step][None], traj_state[step]], axis=0)
        start, size = sz.part_start[part], sz.part_lats[part]
        at = jnp.where(south, sz.lats - start - size, start)
        local = lax.dynamic_slice_in_dim(local, at, size, axis=2)
        local = jnp.transpose(local, (2, 0, 1, 3))
        pieces = [local]
        for shift in range(1, members):
            pieces.append(
                lax.ppermute(
                    local, "pert", [(i, (i - shift) % members) for i in range(members)]
                )
            )
        placed = []
        for place in range(members):
            chosen = pieces[0]
            for shift in range(1, members):
                chosen = jnp.where((member + shift) % members == place, pieces[shift], chosen)
            placed.append(chosen)
        return jnp.concatenate(placed, axis=2)

    def transpose(value):
        return lax.all_to_all(value, "space", 0, 0, tiled=True)

    def inverse_rest(state):
        return call(
            lambda *refs: inverse_kernel(sz, 1, *refs),
            sends(1), (waves, state, table_t), [stages(1)], 6.0, "inverse_rest",
        )

    state, send_0 = call(
        lambda *refs: first_kernel(sz, *refs),
        (state_shape, sends(0)), (waves, spectra, turn, table_t),
        [stages(0), pltpu.VMEM((ROWS, columns), jnp.float32)], 8.0, "first_inverse",
    )
    traj = {(0, 0): gather(0, 0)}
    for step in range(STEPS):
        recv_0 = transpose(send_0)
        send_1 = inverse_rest(state)
        if step == 0:
            traj[0, 1] = gather(0, 1)
            send_1, traj[0, 0] = lax.optimization_barrier((send_1, traj[0, 0]))
        recv_1 = transpose(send_1)
        grid_0 = grid_stage(sz, 0, flip, recv_0, traj[step, 0], synth, slope, scale)
        if step == 0:
            traj[1, 0] = gather(1, 0)
            grid_0, traj[0, 1] = lax.optimization_barrier((grid_0, traj[0, 1]))
        back_0 = transpose(grid_0)
        grid_1 = grid_stage(sz, 1, flip, recv_1, traj[step, 1], synth, slope, scale)
        if step == 0:
            traj[1, 1] = gather(1, 1)
            grid_1, traj[1, 0] = lax.optimization_barrier((grid_1, traj[1, 0]))
        back_1 = transpose(grid_1)
        if step == 0:
            back_0, traj[1, 1] = lax.optimization_barrier((back_0, traj[1, 1]))
        partial = call(
            lambda *refs: forward_kernel(sz, 0, *refs),
            state_shape, (waves, state, back_0, table, weights), [stages(0)], 6.0, "forward_part",
        )
        if step < STEPS - 1:
            state, send_0 = call(
                lambda *refs: middle_kernel(sz, *refs),
                (state_shape, sends(0)),
                (waves, partial, back_1, table, table_t, weights, mixing, mixing_t, speeds),
                [stages(1), stages(0)], 12.0, "forward_inverse",
            )
        else:
            out = call(
                lambda *refs: last_kernel(sz, *refs),
                jax.ShapeDtypeStruct(spectra.shape, jnp.float32),
                (waves, partial, back_1, table, weights, mixing, mixing_t, speeds, turn_t),
                [stages(1), pltpu.VMEM((ROWS, columns), jnp.float32)], 10.0, "forward_last",
            )
    return out


def solution(mesh):
    sz = Sizes(mesh.shape["space"])
    placed = (
        P("space", None, "pert"),
        P(),
        P(None, "pert", "space", None),
        P(None, None, "pert", "space", None),
        P(),
        P(),
    )
    return jax.shard_map(
        lambda *args: shards(sz, *args),
        mesh=mesh,
        in_specs=placed,
        out_specs=P("space", None, "pert"),
        check_vma=False,
    )
```

```python
import math

import jax
import jax.numpy as jnp
import numpy as np
from jax import lax
from jax.experimental import pallas as pl
from jax.experimental.pallas import tpu as pltpu
from jax.sharding import PartitionSpec as P

NLAT = 480
NLON = 960
M = 320
VARS = 2
LEV = 32
STEPS = 2
ROWS = 336
EACH = ROWS // 2
SHIFTED = 2 * ROWS
UNROLL = 5
DEPTH = 384
VMEM_BYTES = 48 * 1024 * 1024
BIG = 2.0**32


def params():
    return pltpu.CompilerParams(vmem_limit_bytes=VMEM_BYTES)


def cost(microseconds):
    return pl.CostEstimate(flops=int(microseconds * 30.0e9), bytes_accessed=1 << 20, transcendentals=0)


def vmem(count):
    return [pl.BlockSpec(memory_space=pltpu.VMEM)] * count


def smem(count):
    return [pl.BlockSpec(memory_space=pltpu.SMEM)] * count


class Sizes:
    def __init__(self, space):
        self.space = space
        self.slots = M // space
        self.pairs = self.slots // 2
        self.lats = NLAT // space
        self.half = space // 2
        self.parts = 2
        middle = self.lats // 2
        middle += (self.lats - middle) % 2
        edge = (self.lats - middle) // 2
        self.ranges = [[(edge, middle)], [(0, edge), (self.lats - edge, edge)]]
        self.part_lats = [middle, 2 * edge]
        self.part_pad = -(-max(self.part_lats) // 8) * 8
        self.part_rows = self.half * self.part_pad
        self.north = self.parts * self.part_rows
        self.pair_pad = -(-self.pairs // 8) * 8
        self.group = 8

    def block(self, part):
        return self.slots * self.part_lats[part]

    def block_pad(self, part):
        last = (self.slots - 1) * self.part_lats[part] + self.part_pad
        return -(-last // 8) * 8


def table_kernel(sz, wave_a, wave_b, start_a, start_b, cosines, table, table_t, rows_ref):
    wide = range(sz.north // 128)
    wa, wb = wave_a[...], wave_b[...]
    length = M - wa

    def tile(ref, c):
        return ref[:, c * 128 : (c + 1) * 128]

    def body(block, carry):
        cur, prev, shift, inv_prev = carry
        second = (block * 8).astype(jnp.float32) > length
        cur, prev, shift, base, base_b = list(cur), list(prev), list(shift), [], []
        for c in wide:
            big = jnp.maximum(jnp.abs(cur[c]), jnp.abs(prev[c])) > BIG
            scale = jnp.where(big, 1.0 / BIG, 1.0)
            cur[c], prev[c] = cur[c] * scale, prev[c] * scale
            shift[c] = shift[c] + jnp.where(big, 32.0, 0.0)
            start = jnp.where(second, tile(start_b, c), tile(start_a, c))
            base.append(jnp.exp2(0.5 * (start + shift[c])))
            base_b.append(jnp.exp2(0.5 * tile(start_b, c)))
        for j in range(8):
            r = (block * 8 + j).astype(jnp.float32)
            fresh = r == length
            begin = jnp.logical_or(fresh, r == 0.0)
            in_b = r >= length
            m = jnp.where(in_b, wb, wa)
            k = jnp.where(in_b, r - length, r)
            n = m + k
            den = k * (m + n)
            num = 4.0 * n * n - 1.0
            root = lax.rsqrt(jnp.maximum(num * den, 1.0))
            upper = num * root
            lower = upper * inv_prev
            inv_prev = den * root
            for c in wide:
                new = upper * tile(cosines, c) * cur[c] - lower * prev[c]
                prev[c] = cur[c]
                cur[c] = jnp.where(begin, 1.0, new)
                shift[c] = jnp.where(fresh, 0.0, shift[c])
                base[c] = jnp.where(fresh, base_b[c], base[c])
                at = (j % 2) * EACH + block * 4 + j // 2
                rows_ref[c, pl.ds(at, sz.pair_pad, stride=ROWS), :] = (cur[c] * base[c]) * base[c]
        return tuple(cur), tuple(prev), tuple(shift), inv_prev

    zero = jnp.zeros((sz.pair_pad, 128), jnp.float32)
    zeros = tuple(zero for _ in wide)
    lax.fori_loop(0, ROWS // 8, body, (zeros, zeros, zeros, zero))
    index = lax.broadcasted_iota(jnp.int32, (EACH, sz.north), 0)
    blank = jnp.zeros((256 - EACH, sz.north), jnp.float32)

    def emit(i, _):
        for p in range(2):
            at = i * ROWS + p * EACH
            full = jnp.concatenate([rows_ref[c, pl.ds(at, EACH), :] for c in wide], axis=1)
            full = jnp.where(2 * index + p <= M, full, 0.0)
            table[i, p] = full.astype(jnp.bfloat16)
            turned = jnp.transpose(jnp.concatenate([full, blank], axis=0))
            table_t[i, p] = turned.astype(jnp.bfloat16)
        return 0

    lax.fori_loop(0, sz.pairs, emit, 0)


def make_tables(sz, wave_a, wave_b, log_a, log_b, cosines):
    return pl.pallas_call(
        lambda *refs: table_kernel(sz, *refs),
        out_shape=(
            jax.ShapeDtypeStruct((sz.pairs, 2, EACH, sz.north), jnp.bfloat16),
            jax.ShapeDtypeStruct((sz.pairs, 2, sz.north, 256), jnp.bfloat16),
        ),
        in_specs=vmem(5),
        out_specs=tuple(vmem(2)),
        scratch_shapes=[pltpu.VMEM((sz.north // 128, sz.pair_pad * ROWS, 128), jnp.float32)],
        compiler_params=params(),
        name="legendre_tables",
    )(wave_a, wave_b, log_a, log_b, cosines)


def each_pair(sz, body):
    step = max(d for d in range(1, UNROLL + 1) if sz.pairs % d == 0)

    def several(g, carry):
        for u in range(step):
            body(g * step + u, u)
        return carry

    lax.fori_loop(0, sz.pairs // step, several, 0)


def row_facts(waves, i, columns):
    wave_a, wave_b = waves[2 * i], waves[2 * i + 1]
    length = M - wave_a
    q = lax.broadcasted_iota(jnp.int32, (ROWS, columns), 0)
    r = jnp.where(q < EACH, 2 * q, 2 * (q - EACH) + 1)
    in_a = r < length
    k = jnp.where(in_a, r, r - length)
    odd = jnp.bitwise_and(length, 1).astype(jnp.float32)
    sign_b = 1.0 - 2.0 * odd
    return wave_a, wave_b, length, r, in_a, k, sign_b


def send_rows(sz, part, i, state, facts, table_t, stage):
    in_a, sign_b = facts[4], facts[6]
    columns = state.shape[1]
    rhs = jnp.concatenate(
        [
            jnp.where(in_a, state, 0.0).astype(jnp.bfloat16),
            jnp.where(in_a, 0.0, state).astype(jnp.bfloat16),
        ],
        axis=1,
    )
    blank = jnp.zeros((256 - EACH, 2 * columns), jnp.bfloat16)
    sums = []
    for p in range(2):
        rows = table_t[i, p, part * sz.part_rows : (part + 1) * sz.part_rows, :]
        side = jnp.concatenate([rhs[p * EACH : (p + 1) * EACH], blank], axis=0)
        sums.append(jnp.dot(rows, side, preferred_element_type=jnp.float32))
    size = sz.part_pad
    plus, minus = sums[0] + sums[1], sums[0] - sums[1]
    for s in range(2):
        north = plus[:, s * columns : (s + 1) * columns]
        south = minus[:, s * columns : (s + 1) * columns]
        south = south * sign_b if s == 1 else south
        at = (2 * i + s) * sz.part_lats[part]
        for b in range(sz.half):
            lo = b * size
            stage[b, pl.ds(at, size), :] = north[lo : lo + size]
            stage[sz.space - 1 - b, pl.ds(at, size), :] = south[lo : lo + size]


def flush(sz, part, stage, send):
    def body(d, _):
        send[d] = stage[d, : sz.block(part), :].astype(jnp.bfloat16)
        return 0

    lax.fori_loop(0, sz.space, body, 0)


def load_rows(sz, part, recv, stage):
    rows = sz.block_pad(part)

    def body(d, _):
        stage[d, rows - 16 : rows, :] = jnp.zeros((16, stage.shape[2]), jnp.float32)
        stage[d, : sz.block(part), :] = recv[d].astype(jnp.float32)
        return 0

    lax.fori_loop(0, sz.space, body, 0)


def change_rows(sz, part, i, facts, table, weights, stage):
    in_a, sign_b = facts[4], facts[6]
    lo = part * sz.part_rows
    w = weights[lo : lo + sz.part_rows, :]
    size = sz.part_pad
    plus, minus = [], []
    for s in range(2):
        at = (2 * i + s) * sz.part_lats[part]
        north = jnp.concatenate([stage[b, pl.ds(at, size), :] for b in range(sz.half)], axis=0)
        south = jnp.concatenate(
            [stage[sz.space - 1 - b, pl.ds(at, size), :] for b in range(sz.half)], axis=0
        )
        north, south = north * w, south * (w * sign_b if s == 1 else w)
        plus.append((north + south).astype(jnp.bfloat16))
        minus.append((north - south).astype(jnp.bfloat16))
    pieces = []
    for p, rows in enumerate((plus, minus)):
        out = jnp.dot(
            table[i, p, :, lo : lo + sz.part_rows],
            jnp.concatenate(rows, axis=1),
            preferred_element_type=jnp.float32,
        )
        c = out.shape[1] // 2
        mine = in_a[p * EACH : (p + 1) * EACH]
        pieces.append(jnp.where(mine, out[:, :c], out[:, c:]))
    return jnp.concatenate(pieces, axis=0)


def kept(state, facts):
    wave_a, wave_b, _, r, in_a = facts[:5]
    columns = state.shape[1]
    imaginary = lax.broadcasted_iota(jnp.int32, state.shape, 1) >= columns // 2
    wave = jnp.where(in_a, wave_a, wave_b)
    dropped = jnp.logical_or(jnp.logical_and(wave == 0, imaginary), r > M)
    return jnp.where(dropped, 0.0, state)


def halves(x):
    high = x.astype(jnp.bfloat16)
    low = (x - high.astype(jnp.float32)).astype(jnp.bfloat16)
    return jnp.concatenate([high, low], axis=1)


def dot_split(x, both):
    out = jnp.dot(halves(x), both, preferred_element_type=jnp.float32)
    c = out.shape[1] // 2
    return out[:, :c] + out[:, c:]


def updated(state, change, facts, mixing, mixing_t, speeds):
    wave_a, wave_b, _, _, in_a, k = facts[:6]
    combined = state + change
    projected = dot_split(combined, mixing[...])
    n = (jnp.where(in_a, wave_a, wave_b) + k).astype(jnp.float32)
    stiffness = speeds[...] * (n * (n + 1.0))
    weighted = projected * (stiffness / (1.0 + stiffness))
    returned = dot_split(weighted, mixing_t[...])
    return kept(combined - returned, facts)


def first_kernel(sz, waves, spectra, turn, table_t, state_ref, send, stage, shifted):
    columns = spectra.shape[2]
    blank = jnp.zeros((EACH - M // 2, columns), jnp.float32)
    shifted[...] = jnp.zeros_like(shifted)

    def body(i, u):
        facts = row_facts(waves, i, columns)
        length, in_a = facts[2], facts[4]
        shifted[u, pl.ds(ROWS, M), :] = spectra[2 * i + 1]
        rows = []
        for p in range(2):
            rows_a = jnp.concatenate(
                [spectra[2 * i, pl.ds(p, M // 2, stride=2), :], blank], axis=0
            )
            rows_b = shifted[u, pl.ds(ROWS - length + p, EACH, stride=2), :]
            rows.append(jnp.where(in_a[p * EACH : (p + 1) * EACH], rows_a, rows_b))
        state = dot_split(jnp.concatenate(rows, axis=0), turn[...])
        state = kept(state, facts)
        state_ref[i] = state
        send_rows(sz, 0, i, state, facts, table_t, stage)

    each_pair(sz, body)
    flush(sz, 0, stage, send)


def inverse_kernel(sz, part, waves, state, table_t, send, stage):
    def body(i, u):
        facts = row_facts(waves, i, state.shape[2])
        send_rows(sz, part, i, state[i], facts, table_t, stage)

    each_pair(sz, body)
    flush(sz, part, stage, send)


def forward_kernel(sz, part, waves, state, recv, table, weights, out, stage):
    load_rows(sz, part, recv, stage)

    def body(i, u):
        facts = row_facts(waves, i, state.shape[2])
        out[i] = state[i] + change_rows(sz, part, i, facts, table, weights, stage)

    each_pair(sz, body)


def middle_kernel(
    sz, waves, partial, recv, table, table_t, weights, mixing, mixing_t, speeds,
    state_out, send, stage_in, stage,
):
    columns = partial.shape[2]
    part = sz.parts - 1
    load_rows(sz, part, recv, stage_in)

    def body(i, u):
        facts = row_facts(waves, i, columns)
        change = change_rows(sz, part, i, facts, table, weights, stage_in)
        state = updated(partial[i], change, facts, mixing, mixing_t, speeds)
        state_out[i] = state
        send_rows(sz, 0, i, state, facts, table_t, stage)

    each_pair(sz, body)
    flush(sz, 0, stage, send)


def last_kernel(
    sz, waves, partial, recv, table, weights, mixing, mixing_t, speeds, turn_t, out, stage_in, mixed
):
    columns = partial.shape[2]
    part = sz.parts - 1
    load_rows(sz, part, recv, stage_in)
    mixed[...] = jnp.zeros_like(mixed)

    def body(i, u):
        facts = row_facts(waves, i, columns)
        wave_b, length = facts[1:3]
        r = lax.broadcasted_iota(jnp.int32, (M, columns), 0)
        change = change_rows(sz, part, i, facts, table, weights, stage_in)
        state = updated(partial[i], change, facts, mixing, mixing_t, speeds)
        state = dot_split(state, turn_t[...])
        for p in range(2):
            mixed[u, pl.ds(p, EACH, stride=2), :] = state[p * EACH : (p + 1) * EACH]
        out[2 * i] = jnp.where(r < length, mixed[u, :M, :], 0.0)
        out[2 * i + 1] = jnp.where(r < M - wave_b, mixed[u, pl.ds(length, M), :], 0.0)

    each_pair(sz, body)


def grid_kernel(sz, part, members, place, recv, synth, slope, scale, *rest):
    pieces, rest = rest[:members], rest[members:]
    send, stage_in, stage, lhs, values, slopes, force, traj, sems = rest
    south, member = place[0], place[1]
    copies = [
        pltpu.make_async_copy(piece, traj.at[i], sems.at[i]) for i, piece in enumerate(pieces)
    ]
    for copy in copies:
        copy.start()
    lanes = recv.shape[2]
    rows = lanes // 2
    lats = sz.part_lats[part]
    block = sz.block(part)
    groups = -(-lats // sz.group)

    def load(d, _):
        stage_in[pl.ds(d * block, block), :] = recv[d].astype(jnp.float32)
        return 0

    lax.fori_loop(0, sz.space, load, 0)
    blank = jnp.zeros((DEPTH - M, lanes), jnp.float32)
    for copy in copies:
        copy.wait()

    def levels(t, field):
        mine = []
        for block in range(members):
            shift = lax.rem(block + members - member, members)
            value = traj[0, t, field].astype(jnp.float32)
            for i in range(1, members):
                value = jnp.where(shift == i, traj[i, t, field].astype(jnp.float32), value)
            mine.append(value)
        return jnp.concatenate(mine, axis=0)

    def body(g, _):
        for q in range(sz.group):
            t = jnp.minimum(g * sz.group + q, lats - 1)
            rows_t = stage_in[pl.ds(t, M, stride=lats), :]
            turned = jnp.transpose(jnp.concatenate([rows_t, blank], axis=0)).astype(jnp.bfloat16)
            lhs[q * rows : (q + 1) * rows, :DEPTH] = turned[:rows]
            lhs[q * rows : (q + 1) * rows, DEPTH:] = turned[rows:]
        left = lhs[...]
        values[...] = jnp.dot(left, synth[...], preferred_element_type=jnp.float32)
        slopes[...] = jnp.dot(left, slope[...], preferred_element_type=jnp.float32)
        for q in range(sz.group):
            t = jnp.minimum(g * sz.group + q, lats - 1)
            here = jnp.where(south == 1, lats - 1 - t, t)
            wind = levels(here, 0)
            for v in range(VARS):
                lo = q * rows + v * LEV
                other = levels(here, 1 + (v + 1) % VARS)
                force[lo : lo + LEV, :] = (
                    wind * slopes[lo : lo + LEV, :] + other * values[lo : lo + LEV, :]
                ).astype(jnp.bfloat16)
        forcing = force[...]
        spectrum = [
            lax.dot_general(
                synth[c * DEPTH : c * DEPTH + M, :],
                forcing,
                (((1,), (1,)), ((), ())),
                preferred_element_type=jnp.float32,
            )
            * scale[...][:, :1]
            for c in range(2)
        ]
        left_side = lax.broadcasted_iota(jnp.int32, (M, lanes), 1) < rows
        for q in range(0, sz.group, 2):
            re = spectrum[0][:, q * rows : (q + 2) * rows]
            im = spectrum[1][:, q * rows : (q + 2) * rows]
            pair = (
                jnp.where(left_side, re, pltpu.roll(im, rows, 1)),
                jnp.where(left_side, pltpu.roll(re, rows, 1), im),
            )
            for o in range(2):
                t = g * sz.group + q + o

                def store(t=t, value=pair[o]):
                    stage[pl.ds(t, M, stride=lats), :] = value

                if (groups - 1) * sz.group + q + o < lats:
                    store()
                else:
                    pl.when(t < lats)(store)
        return 0

    lax.fori_loop(0, groups, body, 0)

    def out(d, _):
        send[d] = stage[pl.ds(d * block, block), :].astype(jnp.bfloat16)
        return 0

    lax.fori_loop(0, sz.space, out, 0)


def grid_stage(sz, part, place, recv, pieces, synth, slope, scale):
    members = len(pieces)
    lanes = recv.shape[2]
    wide = sz.group * lanes // 2
    count = M * sz.part_lats[part]
    return pl.pallas_call(
        lambda *refs: grid_kernel(sz, part, members, *refs),
        out_shape=jax.ShapeDtypeStruct(recv.shape, jnp.bfloat16),
        in_specs=smem(1) + vmem(4) + [pl.BlockSpec(memory_space=pl.ANY)] * members,
        out_specs=vmem(1)[0],
        scratch_shapes=[
            pltpu.VMEM((count, lanes), jnp.float32),
            pltpu.VMEM((count, lanes), jnp.float32),
            pltpu.VMEM((wide, 2 * DEPTH), jnp.bfloat16),
            pltpu.VMEM((wide, NLON), jnp.float32),
            pltpu.VMEM((wide, NLON), jnp.float32),
            pltpu.VMEM((wide, NLON), jnp.bfloat16),
            pltpu.VMEM((members,) + pieces[0].shape, jnp.bfloat16),
            pltpu.SemaphoreType.DMA((members,)),
        ],
        compiler_params=params(),
        cost_estimate=cost(9.0),
        name="grid_stage",
    )(place, recv, synth, slope, scale, *pieces)


def zonal_tables(wave_list):
    cell_index = jnp.arange(NLON, dtype=jnp.int32)
    wave_pad = jnp.concatenate([wave_list, jnp.zeros((DEPTH - M,), jnp.int32)])
    phase_index = wave_pad[:, None] * cell_index[None, :] % NLON
    angles = phase_index.astype(jnp.float32) * (2.0 * math.pi / NLON)
    factor = jnp.where(wave_pad == 0, 1.0, 2.0).astype(jnp.float32)
    inside = (jnp.arange(DEPTH) < M).astype(jnp.float32)
    gain = (factor * inside)[:, None]
    cosine, sine = gain * jnp.cos(angles), gain * jnp.sin(angles)
    wave = wave_pad.astype(jnp.float32)[:, None]
    synth = jnp.concatenate([-cosine, sine], axis=0).astype(jnp.bfloat16)
    slope = jnp.concatenate([wave * sine, wave * cosine], axis=0).astype(jnp.bfloat16)
    scale = jnp.broadcast_to((-1.0 / (NLON * factor[:M]))[:, None], (M, 128))
    return synth, slope, scale


def column_turn(columns):
    turn = np.zeros((columns, columns), np.float32)
    for c in range(columns):
        part, row = c % 2, c // 2
        turn[c, part * (columns // 2) + row] = 1.0
    return turn


def split_matrix(matrix):
    high = matrix.astype(jnp.bfloat16)
    low = (matrix - high.astype(jnp.float32)).astype(jnp.bfloat16)
    top = jnp.concatenate([high, low], axis=1)
    bottom = jnp.concatenate([high, jnp.zeros_like(low)], axis=1)
    return jnp.concatenate([top, bottom], axis=0)


def sectoral(wave, log_sine):
    gammas = jax.scipy.special.gammaln
    start = 0.5 * (
        gammas(wave + 1.5) - gammas(wave + 1.0) - gammas(jnp.float32(1.5))
    ) - 0.5 * math.log(2.0)
    return (start[:, None] + wave[:, None] * log_sine[None, :]) * (1.0 / math.log(2.0))


def shards(sz, spectra, wave_order, traj_wind, traj_state, vertical_modes, mode_speeds):
    columns = spectra.shape[2]
    rank = lax.axis_index("space")
    waves = lax.dynamic_slice_in_dim(wave_order, rank * sz.slots, sz.slots)

    index, real = [], []
    for ranges in sz.ranges:
        within = np.concatenate([np.arange(lo, lo + size) for lo, size in ranges])
        pad = sz.part_pad - within.size
        for b in range(sz.half):
            index.append(np.pad(b * sz.lats + within, (0, pad)))
            real.append(np.pad(np.ones(within.size, bool), (0, pad)))
    index, real = np.concatenate(index), np.concatenate(real)
    colat = np.where(real, (index + 0.5) * (math.pi / NLAT), math.pi / 2)
    cosines = jnp.asarray(np.cos(colat), jnp.float32)[None, :]
    log_sine = jnp.asarray(np.log(np.sin(colat)), jnp.float32)
    weights = jnp.asarray(
        np.broadcast_to((np.sin(colat) * (math.pi / NLAT) * real)[:, None], (sz.north, columns)),
        jnp.float32,
    )

    pair_waves = jnp.zeros((sz.pair_pad, 2), jnp.int32).at[: sz.pairs].set(waves.reshape(-1, 2))
    pair_waves = pair_waves.astype(jnp.float32)
    wide_a = jnp.broadcast_to(pair_waves[:, :1], (sz.pair_pad, 128))
    wide_b = jnp.broadcast_to(pair_waves[:, 1:], (sz.pair_pad, 128))
    table, table_t = make_tables(
        sz, wide_a, wide_b, sectoral(pair_waves[:, 0], log_sine), sectoral(pair_waves[:, 1], log_sine), cosines
    )

    turn = column_turn(columns)
    same = np.kron(np.eye(columns // LEV, dtype=np.float32), np.ones((LEV, LEV), np.float32))
    mixing = split_matrix(jnp.tile(vertical_modes.T, (columns // LEV, columns // LEV)) * same)
    mixing_t = split_matrix(jnp.tile(vertical_modes, (columns // LEV, columns // LEV)) * same)
    speeds = jnp.tile(mode_speeds, columns // LEV)[None, :]
    turn, turn_t = split_matrix(jnp.asarray(turn)), split_matrix(jnp.asarray(turn.T))

    synth, slope, scale = zonal_tables(wave_order)
    member = lax.axis_index("pert")
    place = jnp.stack([jnp.where(rank >= sz.half, 1, 0), member]).astype(jnp.int32)

    def stages(part):
        return pltpu.VMEM((sz.space, sz.block_pad(part), columns), jnp.float32)

    def sends(part):
        return jax.ShapeDtypeStruct((sz.space, sz.block(part), columns), jnp.bfloat16)

    state_shape = jax.ShapeDtypeStruct((sz.pairs, ROWS, columns), jnp.float32)

    def call(body, out_shape, args, scratch, microseconds, name):
        single = not isinstance(out_shape, tuple)
        outs = vmem(1)[0] if single else tuple(vmem(len(out_shape)))
        return pl.pallas_call(
            body,
            out_shape=out_shape,
            in_specs=smem(1) + vmem(len(args) - 1),
            out_specs=outs,
            scratch_shapes=scratch,
            compiler_params=params(),
            cost_estimate=cost(microseconds),
            name=name,
        )(*args)

    members = LEV // traj_wind.shape[1]

    def shared(value):
        return [value] + [
            lax.ppermute(value, "pert", [(i, (i - shift) % members) for i in range(members)])
            for shift in range(1, members)
        ]

    def cut(step, part):
        fields = [traj_wind[step][None], traj_state[step]]
        local = jnp.concatenate(
            [
                jnp.concatenate([f[:, :, lo : lo + size] for f in fields], axis=0)
                for lo, size in sz.ranges[part]
            ],
            axis=2,
        )
        return shared(jnp.transpose(local, (2, 0, 1, 3)))

    def transpose(value):
        return lax.all_to_all(value, "space", 0, 0, tiled=True)

    def inverse_rest(state):
        return call(
            lambda *refs: inverse_kernel(sz, 1, *refs),
            sends(1), (waves, state, table_t), [stages(1)], 6.0, "inverse_rest",
        )

    traj = {(step, part): cut(step, part) for step in range(STEPS) for part in range(2)}

    state, send_0 = call(
        lambda *refs: first_kernel(sz, *refs),
        (state_shape, sends(0)), (waves, spectra, turn, table_t),
        [stages(0), pltpu.VMEM((UNROLL, SHIFTED, columns), jnp.float32)], 8.0, "first_inverse",
    )

    for step in range(STEPS):
        recv_0 = transpose(send_0)
        recv_1 = transpose(inverse_rest(state))
        back_0 = transpose(grid_stage(sz, 0, place, recv_0, traj[step, 0], synth, slope, scale))
        back_1 = transpose(grid_stage(sz, 1, place, recv_1, traj[step, 1], synth, slope, scale))
        partial = call(
            lambda *refs: forward_kernel(sz, 0, *refs),
            state_shape, (waves, state, back_0, table, weights), [stages(0)], 6.0, "forward_part",
        )
        if step < STEPS - 1:
            state, send_0 = call(
                lambda *refs: middle_kernel(sz, *refs),
                (state_shape, sends(0)),
                (waves, partial, back_1, table, table_t, weights, mixing, mixing_t, speeds),
                [stages(1), stages(0)], 12.0, "forward_inverse",
            )
        else:
            out = call(
                lambda *refs: last_kernel(sz, *refs),
                jax.ShapeDtypeStruct(spectra.shape, jnp.float32),
                (waves, partial, back_1, table, weights, mixing, mixing_t, speeds, turn_t),
                [stages(1), pltpu.VMEM((UNROLL, SHIFTED, columns), jnp.float32)], 10.0, "forward_last",
            )
    return out


def solution(mesh):
    sz = Sizes(mesh.shape["space"])
    placed = (
        P("space", None, "pert"),
        P(),
        P(None, "pert", "space", None),
        P(None, None, "pert", "space", None),
        P(),
        P(),
    )
    return jax.shard_map(
        lambda *args: shards(sz, *args),
        mesh=mesh,
        in_specs=placed,
        out_specs=P("space", None, "pert"),
        check_vma=False,
    )
```

```python
import math

import jax
import jax.numpy as jnp
import numpy as np
from jax import lax
from jax.experimental import pallas as pl
from jax.experimental.pallas import tpu as pltpu
from jax.sharding import PartitionSpec as P

NLAT = 480
NLON = 960
M = 320
VARS = 2
LEV = 32
STEPS = 2
ROWS = 336
EACH = ROWS // 2
SHIFTED = 2 * ROWS
UNROLL = 5
DEPTH = 384
VMEM_BYTES = 48 * 1024 * 1024
VMEM_ALONE = 60 * 1024 * 1024
BIG = 2.0**32


def params(limit=VMEM_BYTES):
    return pltpu.CompilerParams(vmem_limit_bytes=limit)


def cost(microseconds):
    return pl.CostEstimate(flops=int(microseconds * 30.0e9), bytes_accessed=1 << 20, transcendentals=0)


def vmem(count):
    return [pl.BlockSpec(memory_space=pltpu.VMEM)] * count


def smem(count):
    return [pl.BlockSpec(memory_space=pltpu.SMEM)] * count


class Sizes:
    def __init__(self, space):
        self.space = space
        self.slots = M // space
        self.pairs = self.slots // 2
        self.lats = NLAT // space
        self.half = space // 2
        self.parts = 2
        middle = self.lats // 2
        middle += (self.lats - middle) % 2
        edge = (self.lats - middle) // 2
        self.ranges = [[(edge, middle)], [(0, edge), (self.lats - edge, edge)]]
        self.part_lats = [middle, 2 * edge]
        self.part_pad = -(-max(self.part_lats) // 8) * 8
        self.part_rows = self.half * self.part_pad
        self.north = self.parts * self.part_rows
        self.pair_pad = -(-self.pairs // 8) * 8
        self.group = 8
        self.step = max(d for d in range(1, UNROLL + 1) if self.pairs % d == 0)
        self.loops = self.pairs // self.step
        self.bundle = space // 4 if space % 4 == 0 else space
        self.bundles = space // self.bundle

    def block(self, part):
        return self.slots * self.part_lats[part]

    def block_pad(self, part):
        last = (self.slots - 1) * self.part_lats[part] + self.part_pad
        return -(-last // 8) * 8


def sectoral_logs():
    ratios = [0.5 * math.log2((2.0 * i + 1.0) / (2.0 * i)) for i in range(1, M)]
    return np.concatenate([[-0.5], -0.5 + np.cumsum(ratios)]).astype(np.float32)


def build_tables(sz, part, waves, logs, angles, table, table_t, rows_ref):
    cosines, log_sines = angles[2 * part : 2 * part + 1, :], angles[2 * part + 1 : 2 * part + 2, :]
    base = lax.axis_index("space") * sz.slots
    shape = (sz.pair_pad, 128)
    zero = jnp.zeros(shape, jnp.float32)
    size = sz.pair_pad
    rows_ref[: 4 * size, :] = jnp.zeros((4 * size, 128), jnp.float32)
    for i in range(sz.pairs):
        wave_a, wave_b = waves[base + 2 * i], waves[base + 2 * i + 1]
        facts = (wave_a.astype(jnp.float32), wave_b.astype(jnp.float32), logs[wave_a // 128, wave_a % 128], logs[wave_b // 128, wave_b % 128])
        for j, fact in enumerate(facts):
            rows_ref[j * size + i : j * size + i + 1, :] = jnp.full((1, 128), fact, jnp.float32)
    wa, wb, ca, cb = (rows_ref[j * size : (j + 1) * size, :] for j in range(4))
    length = M - wa
    start_a = ca + wa * log_sines
    start_b = cb + wb * log_sines
    base_b = jnp.exp2(0.5 * start_b)
    x = jnp.broadcast_to(cosines, shape)

    def body(block, carry):
        cur, prev, shift, inv_prev = carry
        second = (block * 8).astype(jnp.float32) > length
        big = jnp.maximum(jnp.abs(cur), jnp.abs(prev)) > BIG
        scale = jnp.where(big, 1.0 / BIG, 1.0)
        cur, prev = cur * scale, prev * scale
        shift = shift + jnp.where(big, 32.0, 0.0)
        factor = jnp.exp2(0.5 * (jnp.where(second, start_b, start_a) + shift))
        for j in range(8):
            r = (block * 8 + j).astype(jnp.float32)
            fresh = r == length
            begin = jnp.logical_or(fresh, r == 0.0)
            in_b = r >= length
            m = jnp.where(in_b, wb, wa)
            k = jnp.where(in_b, r - length, r)
            n = m + k
            den = k * (m + n)
            num = 4.0 * n * n - 1.0
            root = lax.rsqrt(jnp.maximum(num * den, 1.0))
            upper = num * root
            lower = upper * inv_prev
            inv_prev = den * root
            new = upper * x * cur - lower * prev
            prev = cur
            cur = jnp.where(begin, 1.0, new)
            shift = jnp.where(fresh, 0.0, shift)
            factor = jnp.where(fresh, base_b, factor)
            at = (j % 2) * EACH + block * 4 + j // 2
            rows_ref[pl.ds(at, sz.pair_pad, stride=ROWS), :] = (cur * factor) * factor
        return cur, prev, shift, inv_prev

    lax.fori_loop(0, ROWS // 8, body, (zero, zero, zero, zero))
    index = lax.broadcasted_iota(jnp.int32, (EACH, 128), 0)
    blank = jnp.zeros((256 - EACH, 128), jnp.float32)

    def emit(i, u):
        for p in range(2):
            full = rows_ref[pl.ds(i * ROWS + p * EACH, EACH), :]
            full = jnp.where(2 * index + p <= M, full, 0.0)
            table[i, p] = full.astype(jnp.bfloat16)
            turned = jnp.transpose(jnp.concatenate([full, blank], axis=0))
            table_t[i, p] = turned.astype(jnp.bfloat16)

    each_pair(sz, emit)


def table_shapes(sz):
    return [(sz.pairs, 2, EACH, 128), (sz.pairs, 2, 128, 256)]


def move(source, target, sem):
    copy = pltpu.make_async_copy(source, target, sem)
    copy.start()
    return copy


def each_pair(sz, body, done=None):
    def several(g, carry):
        for u in range(sz.step):
            body(g * sz.step + u, u)
        if done is not None:
            done(g)
        return carry

    lax.fori_loop(0, sz.pairs // sz.step, several, 0)


def group_copy(source, target, sems, g, size):
    rows = pl.ds(g * size, size)
    return pltpu.make_async_copy(source.at[rows], target.at[rows], sems.at[g])


def row_facts(sz, waves, i, columns):
    base = lax.axis_index("space") * sz.slots
    wave_a, wave_b = waves[base + 2 * i], waves[base + 2 * i + 1]
    length = M - wave_a
    q = lax.broadcasted_iota(jnp.int32, (ROWS, columns), 0)
    r = jnp.where(q < EACH, 2 * q, 2 * (q - EACH) + 1)
    in_a = r < length
    k = jnp.where(in_a, r, r - length)
    odd = jnp.bitwise_and(length, 1).astype(jnp.float32)
    sign_b = 1.0 - 2.0 * odd
    return wave_a, wave_b, length, r, in_a, k, sign_b


def send_rows(sz, part, i, state, facts, table_t, stage):
    in_a, sign_b = facts[4], facts[6]
    columns = state.shape[1]
    rhs = jnp.concatenate(
        [
            jnp.where(in_a, state, 0.0).astype(jnp.bfloat16),
            jnp.where(in_a, 0.0, state).astype(jnp.bfloat16),
        ],
        axis=1,
    )
    blank = jnp.zeros((256 - EACH, 2 * columns), jnp.bfloat16)
    sums = []
    for p in range(2):
        rows = table_t[i, p]
        side = jnp.concatenate([rhs[p * EACH : (p + 1) * EACH], blank], axis=0)
        sums.append(jnp.dot(rows, side, preferred_element_type=jnp.float32))
    size = sz.part_pad
    plus, minus = sums[0] + sums[1], sums[0] - sums[1]
    for s in range(2):
        north = plus[:, s * columns : (s + 1) * columns]
        south = minus[:, s * columns : (s + 1) * columns]
        south = south * sign_b if s == 1 else south
        at = (2 * i + s) * sz.part_lats[part]
        for b in range(sz.half):
            lo = b * size
            stage[b, pl.ds(at, size), :] = north[lo : lo + size]
            stage[sz.space - 1 - b, pl.ds(at, size), :] = south[lo : lo + size]


def flush(sz, part, stage, send, target=None, sems=None):
    def body(g, _):
        for o in range(sz.bundle):
            d = g * sz.bundle + o
            send[d] = stage[d, : sz.block(part), :].astype(jnp.bfloat16)
        if target is not None:
            group_copy(send, target, sems, g, sz.bundle).start()
        return 0

    lax.fori_loop(0, sz.bundles, body, 0)
    if target is not None:
        for g in range(sz.bundles):
            group_copy(send, target, sems, g, sz.bundle).wait()


def load_rows(sz, part, recv, stage, source=None, sems=None):
    rows = sz.block_pad(part)
    if source is not None:
        for g in range(sz.bundles):
            group_copy(source, recv, sems, g, sz.bundle).start()

    def body(g, _):
        if source is not None:
            group_copy(source, recv, sems, g, sz.bundle).wait()
        for o in range(sz.bundle):
            d = g * sz.bundle + o
            stage[d, rows - 16 : rows, :] = jnp.zeros((16, stage.shape[2]), jnp.float32)
            stage[d, : sz.block(part), :] = recv[d].astype(jnp.float32)
        return 0

    lax.fori_loop(0, sz.bundles, body, 0)


def change_rows(sz, part, i, facts, table, weights, stage):
    in_a, sign_b = facts[4], facts[6]
    w = weights[...]
    size = sz.part_pad
    plus, minus = [], []
    for s in range(2):
        at = (2 * i + s) * sz.part_lats[part]
        north = jnp.concatenate([stage[b, pl.ds(at, size), :] for b in range(sz.half)], axis=0)
        south = jnp.concatenate(
            [stage[sz.space - 1 - b, pl.ds(at, size), :] for b in range(sz.half)], axis=0
        )
        north, south = north * w, south * (w * sign_b if s == 1 else w)
        plus.append((north + south).astype(jnp.bfloat16))
        minus.append((north - south).astype(jnp.bfloat16))
    pieces = []
    for p, rows in enumerate((plus, minus)):
        out = jnp.dot(
            table[i, p],
            jnp.concatenate(rows, axis=1),
            preferred_element_type=jnp.float32,
        )
        c = out.shape[1] // 2
        mine = in_a[p * EACH : (p + 1) * EACH]
        pieces.append(jnp.where(mine, out[:, :c], out[:, c:]))
    return jnp.concatenate(pieces, axis=0)


def kept(state, facts):
    wave_a, wave_b, _, r, in_a = facts[:5]
    columns = state.shape[1]
    imaginary = lax.broadcasted_iota(jnp.int32, state.shape, 1) >= columns // 2
    wave = jnp.where(in_a, wave_a, wave_b)
    dropped = jnp.logical_or(jnp.logical_and(wave == 0, imaginary), r > M)
    return jnp.where(dropped, 0.0, state)


def turn_matrix(columns, back=False):
    shape = (2 * columns, 2 * columns)
    r = lax.broadcasted_iota(jnp.int32, shape, 0)
    c = lax.broadcasted_iota(jnp.int32, shape, 1)
    r = jnp.where(r < columns, r, r - columns)
    old, new = (c, r) if back else (r, c)
    target = jnp.bitwise_and(old, 1) * (columns // 2) + jnp.right_shift(old, 1)
    match = jnp.logical_and(target == new, c < columns)
    return jnp.where(match, 1.0, 0.0).astype(jnp.bfloat16)


def halves(x):
    high = x.astype(jnp.bfloat16)
    low = (x - high.astype(jnp.float32)).astype(jnp.bfloat16)
    return jnp.concatenate([high, low], axis=1)


def dot_split(x, both):
    out = jnp.dot(halves(x), both, preferred_element_type=jnp.float32)
    c = out.shape[1] // 2
    return out[:, :c] + out[:, c:]


def updated(state, change, facts, mixing, mixing_t, speeds):
    wave_a, wave_b, _, _, in_a, k = facts[:6]
    combined = state + change
    projected = dot_split(combined, mixing[...])
    n = (jnp.where(in_a, wave_a, wave_b) + k).astype(jnp.float32)
    stiffness = speeds[...] * (n * (n + 1.0))
    weighted = projected * (stiffness / (1.0 + stiffness))
    returned = dot_split(weighted, mixing_t[...])
    return kept(combined - returned, facts)


def first_kernel(
    sz, waves_hbm, angles_hbm, spectra_hbm,
    table_hbm, table_t_hbm, state_hbm, send_hbm,
    waves, logs, angles, spectra, table, table_t, state_ref, send, stage, shifted, rows_ref, one, state_sems, send_sems,
):
    columns = spectra.shape[2]
    blank = jnp.zeros((EACH - M // 2, columns), jnp.float32)
    facts = [
        move(waves_hbm, waves, one.at[3]),
        move(angles_hbm.at[8:16], logs, one.at[4]),
        move(angles_hbm.at[0:8], angles, one.at[5]),
    ]
    arriving = move(spectra_hbm, spectra, one.at[0])
    turn = turn_matrix(columns)
    shifted[...] = jnp.zeros_like(shifted)
    for copy in facts:
        copy.wait()
    build_tables(sz, 0, waves, logs, angles, table, table_t, rows_ref)
    leaving = [move(table, table_hbm, one.at[1]), move(table_t, table_t_hbm, one.at[2])]
    arriving.wait()

    def body(i, u):
        facts = row_facts(sz, waves, i, columns)
        length, in_a = facts[2], facts[4]
        shifted[u, pl.ds(ROWS, M), :] = spectra[2 * i + 1]
        rows = []
        for p in range(2):
            rows_a = jnp.concatenate(
                [spectra[2 * i, pl.ds(p, M // 2, stride=2), :], blank], axis=0
            )
            rows_b = shifted[u, pl.ds(ROWS - length + p, EACH, stride=2), :]
            rows.append(jnp.where(in_a[p * EACH : (p + 1) * EACH], rows_a, rows_b))
        state = dot_split(jnp.concatenate(rows, axis=0), turn)
        state = kept(state, facts)
        state_ref[i] = state
        send_rows(sz, 0, i, state, facts, table_t, stage)

    each_pair(
        sz, body, lambda g: group_copy(state_ref, state_hbm, state_sems, g, sz.step).start()
    )
    flush(sz, 0, stage, send, send_hbm, send_sems)
    for g in range(sz.loops):
        group_copy(state_ref, state_hbm, state_sems, g, sz.step).wait()
    for copy in leaving:
        copy.wait()


def rest_kernel(
    sz, waves, angles, angles_hbm, state_hbm, table_hbm, table_t_hbm, send_hbm,
    table, table_t, send, state, logs, stage, rows_ref, one, send_sems,
):
    arriving = move(state_hbm, state, one.at[0])
    scalars = move(angles_hbm.at[8:16], logs, one.at[1])
    scalars.wait()
    build_tables(sz, 1, waves, logs, angles, table, table_t, rows_ref)
    leaving = [move(table, table_hbm, one.at[2]), move(table_t, table_t_hbm, one.at[3])]
    arriving.wait()
    inverse_kernel(sz, 1, waves, state, table_t, send, stage, send_hbm, send_sems)
    for copy in leaving:
        copy.wait()


def inverse_kernel(sz, part, waves, state, table_t, send, stage, target=None, sems=None):
    def body(i, u):
        facts = row_facts(sz, waves, i, state.shape[2])
        send_rows(sz, part, i, state[i], facts, table_t, stage)

    each_pair(sz, body)
    flush(sz, part, stage, send, target, sems)


def forward_kernel(sz, part, waves, state, recv, table, weights, out, stage):
    load_rows(sz, part, recv, stage)

    def body(i, u):
        facts = row_facts(sz, waves, i, state.shape[2])
        out[i] = state[i] + change_rows(sz, part, i, facts, table, weights, stage)

    each_pair(sz, body)


def middle_kernel(
    sz, waves, weights, mixing, mixing_t, speeds, partial_hbm, recv_hbm, table_hbm, table_t_hbm,
    state_hbm, send_hbm,
    state_ref, recv, table, table_t, send, stage_in, stage, one, state_sems, recv_sems, send_sems,
):
    part = sz.parts - 1
    columns = state_ref.shape[2]
    arriving = [
        move(partial_hbm, state_ref, one.at[0]),
        move(table_hbm, table, one.at[1]),
        move(table_t_hbm, table_t, one.at[2]),
    ]
    load_rows(sz, part, recv, stage_in, recv_hbm, recv_sems)
    for copy in arriving:
        copy.wait()

    def body(i, u):
        facts = row_facts(sz, waves, i, columns)
        change = change_rows(sz, part, i, facts, table, weights, stage_in)
        state = updated(state_ref[i], change, facts, mixing, mixing_t, speeds)
        state_ref[i] = state
        send_rows(sz, 0, i, state, facts, table_t, stage)

    each_pair(
        sz, body, lambda g: group_copy(state_ref, state_hbm, state_sems, g, sz.step).start()
    )
    flush(sz, 0, stage, send, send_hbm, send_sems)
    for g in range(sz.loops):
        group_copy(state_ref, state_hbm, state_sems, g, sz.step).wait()


def last_kernel(
    sz, waves, weights, mixing, mixing_t, speeds, partial_hbm, recv_hbm, table_hbm,
    out_hbm,
    state_ref, recv, table, out, stage_in, mixed, one, out_sems, recv_sems,
):
    part = sz.parts - 1
    columns = state_ref.shape[2]
    arriving = [move(partial_hbm, state_ref, one.at[0]), move(table_hbm, table, one.at[1])]
    mixed[...] = jnp.zeros_like(mixed)
    turn_t = turn_matrix(columns, back=True)
    load_rows(sz, part, recv, stage_in, recv_hbm, recv_sems)
    for copy in arriving:
        copy.wait()

    def body(i, u):
        facts = row_facts(sz, waves, i, columns)
        wave_b, length = facts[1:3]
        r = lax.broadcasted_iota(jnp.int32, (M, columns), 0)
        change = change_rows(sz, part, i, facts, table, weights, stage_in)
        state = updated(state_ref[i], change, facts, mixing, mixing_t, speeds)
        state = dot_split(state, turn_t)
        for p in range(2):
            mixed[u, pl.ds(p, EACH, stride=2), :] = state[p * EACH : (p + 1) * EACH]
        out[2 * i] = jnp.where(r < length, mixed[u, :M, :], 0.0)
        out[2 * i + 1] = jnp.where(r < M - wave_b, mixed[u, pl.ds(length, M), :], 0.0)

    each_pair(
        sz, body, lambda g: group_copy(out, out_hbm, out_sems, g, 2 * sz.step).start()
    )
    for g in range(sz.loops):
        group_copy(out, out_hbm, out_sems, g, 2 * sz.step).wait()


def grid_kernel(sz, part, members, recv, synth, slope, scale, *rest):
    pieces, rest = rest[:members], rest[members:]
    send, stage_in, stage, lhs, values, slopes, force, traj, sems = rest
    south = lax.axis_index("space") >= sz.half
    member = lax.axis_index("pert")
    copies = [
        pltpu.make_async_copy(piece, traj.at[i], sems.at[i]) for i, piece in enumerate(pieces)
    ]
    for copy in copies:
        copy.start()
    lanes = recv.shape[2]
    rows = lanes // 2
    lats = sz.part_lats[part]
    block = sz.block(part)
    groups = -(-lats // sz.group)

    def load(d, _):
        stage_in[pl.ds(d * block, block), :] = recv[d].astype(jnp.float32)
        return 0

    lax.fori_loop(0, sz.space, load, 0)
    blank = jnp.zeros((DEPTH - M, lanes), jnp.float32)
    for copy in copies:
        copy.wait()

    def levels(t, field):
        mine = []
        for block in range(members):
            shift = lax.rem(block + members - member, members)
            value = traj[0, t, field].astype(jnp.float32)
            for i in range(1, members):
                value = jnp.where(shift == i, traj[i, t, field].astype(jnp.float32), value)
            mine.append(value)
        return jnp.concatenate(mine, axis=0)

    def body(g, _):
        for q in range(sz.group):
            t = jnp.minimum(g * sz.group + q, lats - 1)
            rows_t = stage_in[pl.ds(t, M, stride=lats), :]
            turned = jnp.transpose(jnp.concatenate([rows_t, blank], axis=0)).astype(jnp.bfloat16)
            lhs[q * rows : (q + 1) * rows, :DEPTH] = turned[:rows]
            lhs[q * rows : (q + 1) * rows, DEPTH:] = turned[rows:]
        left = lhs[...]
        values[...] = jnp.dot(left, synth[...], preferred_element_type=jnp.float32)
        slopes[...] = jnp.dot(left, slope[...], preferred_element_type=jnp.float32)
        for q in range(sz.group):
            t = jnp.minimum(g * sz.group + q, lats - 1)
            here = jnp.where(south, lats - 1 - t, t)
            wind = levels(here, 0)
            for v in range(VARS):
                lo = q * rows + v * LEV
                other = levels(here, 1 + (v + 1) % VARS)
                force[lo : lo + LEV, :] = (
                    wind * slopes[lo : lo + LEV, :] + other * values[lo : lo + LEV, :]
                ).astype(jnp.bfloat16)
        forcing = force[...]
        spectrum = [
            lax.dot_general(
                synth[c * DEPTH : c * DEPTH + M, :],
                forcing,
                (((1,), (1,)), ((), ())),
                preferred_element_type=jnp.float32,
            )
            * scale[...][:, :1]
            for c in range(2)
        ]
        left_side = lax.broadcasted_iota(jnp.int32, (M, lanes), 1) < rows
        for q in range(0, sz.group, 2):
            re = spectrum[0][:, q * rows : (q + 2) * rows]
            im = spectrum[1][:, q * rows : (q + 2) * rows]
            pair = (
                jnp.where(left_side, re, pltpu.roll(im, rows, 1)),
                jnp.where(left_side, pltpu.roll(re, rows, 1), im),
            )
            for o in range(2):
                t = g * sz.group + q + o

                def store(t=t, value=pair[o]):
                    stage[pl.ds(t, M, stride=lats), :] = value

                if (groups - 1) * sz.group + q + o < lats:
                    store()
                else:
                    pl.when(t < lats)(store)
        return 0

    lax.fori_loop(0, groups, body, 0)

    def out(d, _):
        send[d] = stage[pl.ds(d * block, block), :].astype(jnp.bfloat16)
        return 0

    lax.fori_loop(0, sz.space, out, 0)


def grid_stage(sz, part, recv, pieces, synth, slope, scale):
    members = len(pieces)
    lanes = recv.shape[2]
    wide = sz.group * lanes // 2
    count = M * sz.part_lats[part]
    return pl.pallas_call(
        lambda *refs: grid_kernel(sz, part, members, *refs),
        out_shape=jax.ShapeDtypeStruct(recv.shape, jnp.bfloat16),
        in_specs=vmem(4) + [pl.BlockSpec(memory_space=pl.ANY)] * members,
        out_specs=vmem(1)[0],
        scratch_shapes=[
            pltpu.VMEM((count, lanes), jnp.float32),
            pltpu.VMEM((count, lanes), jnp.float32),
            pltpu.VMEM((wide, 2 * DEPTH), jnp.bfloat16),
            pltpu.VMEM((wide, NLON), jnp.float32),
            pltpu.VMEM((wide, NLON), jnp.float32),
            pltpu.VMEM((wide, NLON), jnp.bfloat16),
            pltpu.VMEM((members,) + pieces[0].shape, jnp.bfloat16),
            pltpu.SemaphoreType.DMA((members,)),
        ],
        compiler_params=params(),
        cost_estimate=cost(9.0),
        name="grid_stage",
    )(recv, synth, slope, scale, *pieces)


def zonal_tables(wave_list):
    cell_index = jnp.arange(NLON, dtype=jnp.int32)
    wave_pad = jnp.concatenate([wave_list, jnp.zeros((DEPTH - M,), jnp.int32)])
    phase_index = wave_pad[:, None] * cell_index[None, :] % NLON
    angles = phase_index.astype(jnp.float32) * (2.0 * math.pi / NLON)
    factor = jnp.where(wave_pad == 0, 1.0, 2.0).astype(jnp.float32)
    inside = (jnp.arange(DEPTH) < M).astype(jnp.float32)
    gain = (factor * inside)[:, None]
    cosine, sine = gain * jnp.cos(angles), gain * jnp.sin(angles)
    wave = wave_pad.astype(jnp.float32)[:, None]
    synth = jnp.concatenate([-cosine, sine], axis=0).astype(jnp.bfloat16)
    slope = jnp.concatenate([wave * sine, wave * cosine], axis=0).astype(jnp.bfloat16)
    scale = jnp.broadcast_to((-1.0 / (NLON * factor[:M]))[:, None], (M, 128))
    return synth, slope, scale


def split_matrix(matrix):
    high = matrix.astype(jnp.bfloat16)
    low = (matrix - high.astype(jnp.float32)).astype(jnp.bfloat16)
    top = jnp.concatenate([high, low], axis=1)
    bottom = jnp.concatenate([high, jnp.zeros_like(low)], axis=1)
    return jnp.concatenate([top, bottom], axis=0)


def shards(sz, spectra, wave_order, traj_wind, traj_state, vertical_modes, mode_speeds):
    columns = spectra.shape[2]
    index, real = [], []
    for ranges in sz.ranges:
        within = np.concatenate([np.arange(lo, lo + size) for lo, size in ranges])
        pad = sz.part_pad - within.size
        for b in range(sz.half):
            index.append(np.pad(b * sz.lats + within, (0, pad)))
            real.append(np.pad(np.ones(within.size, bool), (0, pad)))
    index, real = np.concatenate(index), np.concatenate(real)
    colat = np.where(real, (index + 0.5) * (math.pi / NLAT), math.pi / 2)
    angles = np.zeros((16, 128), np.float32)
    angles[8:11] = np.pad(sectoral_logs(), (0, 3 * 128 - M)).reshape(3, 128)
    for part in range(sz.parts):
        mine = colat[part * sz.part_rows : (part + 1) * sz.part_rows]
        angles[2 * part] = np.cos(mine)
        angles[2 * part + 1] = np.log2(np.sin(mine))
    angles = jnp.asarray(angles)
    weights = (np.sin(colat) * (math.pi / NLAT) * real).astype(np.float32)
    weights = np.broadcast_to(weights[:, None], (sz.north, columns))
    weights = [jnp.asarray(w) for w in np.split(weights, sz.parts)]

    same = np.kron(np.eye(columns // LEV, dtype=np.float32), np.ones((LEV, LEV), np.float32))
    mixing = split_matrix(jnp.tile(vertical_modes.T, (columns // LEV, columns // LEV)) * same)
    mixing_t = split_matrix(jnp.tile(vertical_modes, (columns // LEV, columns // LEV)) * same)
    speeds = jnp.tile(mode_speeds, columns // LEV)[None, :]

    def stages(part):
        return pltpu.VMEM((sz.space, sz.block_pad(part), columns), jnp.float32)

    def sends(part):
        return jax.ShapeDtypeStruct((sz.space, sz.block(part), columns), jnp.bfloat16)

    state_shape = jax.ShapeDtypeStruct((sz.pairs, ROWS, columns), jnp.float32)

    table_specs = [jax.ShapeDtypeStruct(shape, jnp.bfloat16) for shape in table_shapes(sz)]
    table_vmem = [pltpu.VMEM(shape, jnp.bfloat16) for shape in table_shapes(sz)]
    rows_vmem = pltpu.VMEM((sz.pair_pad * ROWS, 128), jnp.float32)
    shift_vmem = pltpu.VMEM((UNROLL, SHIFTED, columns), jnp.float32)
    state_vmem = pltpu.VMEM(state_shape.shape, jnp.float32)

    def block_vmem(part):
        return pltpu.VMEM(sends(part).shape, jnp.bfloat16)

    def dma(count):
        return pltpu.SemaphoreType.DMA((count,))

    def call(body, outs, scalars, near, far, scratch, microseconds, name, away=True):
        anywhere = pl.BlockSpec(memory_space=pltpu.HBM)
        return pl.pallas_call(
            lambda *refs: body(sz, *refs),
            out_shape=tuple(outs),
            in_specs=smem(len(scalars)) + vmem(len(near)) + [anywhere] * len(far),
            out_specs=(anywhere,) * len(outs) if away else tuple(vmem(len(outs))),
            scratch_shapes=scratch,
            compiler_params=params(VMEM_ALONE if away else VMEM_BYTES),
            cost_estimate=cost(microseconds),
            name=name,
        )(*scalars, *near, *far)

    members = LEV // traj_wind.shape[1]

    def shared(value):
        return [value] + [
            lax.ppermute(value, "pert", [(i, (i - shift) % members) for i in range(members)])
            for shift in range(1, members)
        ]

    def cut(step, part):
        fields = [traj_wind[step][None], traj_state[step]]
        local = jnp.concatenate(
            [
                jnp.concatenate([f[:, :, lo : lo + size] for f in fields], axis=0)
                for lo, size in sz.ranges[part]
            ],
            axis=2,
        )
        return shared(jnp.transpose(local, (2, 0, 1, 3)))

    def transpose(value):
        return lax.all_to_all(value, "space", 0, 0, tiled=True)

    traj = {(step, part): cut(step, part) for step in range(STEPS) for part in range(2)}

    table_0, table_t_0, state, send_0 = call(
        first_kernel,
        table_specs + [state_shape, sends(0)],
        [], [], [wave_order, angles, spectra],
        [
            pltpu.SMEM((M,), jnp.int32), pltpu.SMEM((8, 128), jnp.float32),
            pltpu.VMEM((8, 128), jnp.float32),
            pltpu.VMEM(spectra.shape, jnp.float32), *table_vmem, state_vmem, block_vmem(0),
            stages(0), shift_vmem, rows_vmem, dma(7), dma(sz.loops), dma(sz.bundles),
        ],
        12.0, "tables_inverse",
    )
    table_1 = table_t_1 = None
    for step in range(STEPS):
        recv_0 = transpose(send_0)
        if step == 0:
            table_1, table_t_1, send_1 = call(
                rest_kernel,
                table_specs + [sends(1)],
                [wave_order], [angles], [angles, state],
                [
                    *table_vmem, block_vmem(1), state_vmem, pltpu.SMEM((8, 128), jnp.float32),
                    stages(1), rows_vmem, dma(4), dma(sz.bundles),
                ],
                8.0, "tables_inverse_rest",
            )
        else:
            (send_1,) = call(
                lambda s, *refs: inverse_kernel(s, 1, *refs),
                [sends(1)], [wave_order], [state, table_t_1], [], [stages(1)],
                4.0, "inverse_rest", away=False,
            )
        recv_1 = transpose(send_1)
        if step == 0:
            recv_0, later = lax.optimization_barrier((recv_0, wave_order))
            synth, slope, scale = zonal_tables(later)
        back_0 = transpose(grid_stage(sz, 0, recv_0, traj[step, 0], synth, slope, scale))
        back_1 = transpose(grid_stage(sz, 1, recv_1, traj[step, 1], synth, slope, scale))
        (partial,) = call(
            lambda s, *refs: forward_kernel(s, 0, *refs),
            [state_shape], [wave_order], [state, back_0, table_0, weights[0]], [], [stages(0)],
            5.0, "forward_part", away=False,
        )
        near = [weights[1], mixing, mixing_t, speeds]
        if step < STEPS - 1:
            state, send_0 = call(
                middle_kernel,
                [state_shape, sends(0)],
                [wave_order], near, [partial, back_1, table_1, table_t_0],
                [
                    state_vmem, block_vmem(1), *table_vmem, block_vmem(0), stages(1), stages(0),
                    dma(3), dma(sz.loops), dma(sz.bundles), dma(sz.bundles),
                ],
                12.0, "forward_inverse",
            )
        else:
            (out,) = call(
                last_kernel,
                [jax.ShapeDtypeStruct(spectra.shape, jnp.float32)],
                [wave_order], near, [partial, back_1, table_1],
                [
                    state_vmem, block_vmem(1), table_vmem[0],
                    pltpu.VMEM(spectra.shape, jnp.float32), stages(1), shift_vmem,
                    dma(2), dma(sz.loops), dma(sz.bundles),
                ],
                10.0, "forward_last",
            )
    return out


def solution(mesh):
    sz = Sizes(mesh.shape["space"])
    placed = (
        P("space", None, "pert"),
        P(),
        P(None, "pert", "space", None),
        P(None, None, "pert", "space", None),
        P(),
        P(),
    )
    return jax.shard_map(
        lambda *args: shards(sz, *args),
        mesh=mesh,
        in_specs=placed,
        out_specs=P("space", None, "pert"),
        check_vma=False,
    )
```

```python
import math

import jax
import jax.numpy as jnp
import numpy as np
from jax import lax
from jax.experimental import pallas as pl
from jax.experimental.pallas import tpu as pltpu
from jax.sharding import PartitionSpec as P

NLAT = 480
NLON = 960
M = 320
VARS = 2
LEV = 32
STEPS = 2
ROWS = 336
EACH = ROWS // 2
SHIFTED = 2 * ROWS
UNROLL = 5
DEPTH = 384
VMEM_BYTES = 48 * 1024 * 1024
VMEM_ALONE = 60 * 1024 * 1024
BIG = 2.0**32


def params(limit=VMEM_BYTES):
    return pltpu.CompilerParams(vmem_limit_bytes=limit)


def cost(microseconds):
    return pl.CostEstimate(flops=int(microseconds * 30.0e9), bytes_accessed=1 << 20, transcendentals=0)


def vmem(count):
    return [pl.BlockSpec(memory_space=pltpu.VMEM)] * count


def smem(count):
    return [pl.BlockSpec(memory_space=pltpu.SMEM)] * count


class Sizes:
    def __init__(self, space):
        self.space = space
        self.slots = M // space
        self.pairs = self.slots // 2
        self.lats = NLAT // space
        self.half = space // 2
        self.parts = 2
        middle = self.lats // 2
        middle += (self.lats - middle) % 2
        edge = (self.lats - middle) // 2
        self.ranges = [[(edge, middle)], [(0, edge), (self.lats - edge, edge)]]
        self.part_lats = [middle, 2 * edge]
        self.part_pad = -(-max(self.part_lats) // 8) * 8
        self.part_rows = self.half * self.part_pad
        self.north = self.parts * self.part_rows
        self.pair_pad = -(-self.pairs // 8) * 8
        self.group = 8
        self.step = max(d for d in range(1, UNROLL + 1) if self.pairs % d == 0)
        self.loops = self.pairs // self.step
        self.bundle = space // 4 if space % 4 == 0 else space
        self.bundles = space // self.bundle

    def direct(self, part):
        return self.part_lats[part] % 16 == 0

    def block(self, part):
        return self.slots * self.part_lats[part]

    def block_pad(self, part):
        last = (self.slots - 1) * self.part_lats[part] + self.part_pad
        return -(-last // 8) * 8


def sectoral_logs():
    ratios = [0.5 * math.log2((2.0 * i + 1.0) / (2.0 * i)) for i in range(1, M)]
    return np.concatenate([[-0.5], -0.5 + np.cumsum(ratios)]).astype(np.float32)


def build_tables(sz, part, waves, logs, angles, table, table_t, rows_ref):
    cosines, log_sines = angles[2 * part : 2 * part + 1, :], angles[2 * part + 1 : 2 * part + 2, :]
    quadrature = angles[4 + part : 5 + part, :]
    base = lax.axis_index("space") * sz.slots
    shape = (sz.pair_pad, 128)
    zero = jnp.zeros(shape, jnp.float32)
    size = sz.pair_pad
    rows_ref[: 4 * size, :] = jnp.zeros((4 * size, 128), jnp.float32)
    for i in range(sz.pairs):
        wave_a, wave_b = waves[base + 2 * i], waves[base + 2 * i + 1]
        facts = (wave_a.astype(jnp.float32), wave_b.astype(jnp.float32), logs[wave_a // 128, wave_a % 128], logs[wave_b // 128, wave_b % 128])
        for j, fact in enumerate(facts):
            rows_ref[j * size + i : j * size + i + 1, :] = jnp.full((1, 128), fact, jnp.float32)
    wa, wb, ca, cb = (rows_ref[j * size : (j + 1) * size, :] for j in range(4))
    length = M - wa
    start_a = ca + wa * log_sines
    start_b = cb + wb * log_sines
    base_b = jnp.exp2(0.5 * start_b)
    x = jnp.broadcast_to(cosines, shape)

    def body(block, carry):
        cur, prev, shift, inv_prev = carry
        second = (block * 8).astype(jnp.float32) > length
        big = jnp.maximum(jnp.abs(cur), jnp.abs(prev)) > BIG
        scale = jnp.where(big, 1.0 / BIG, 1.0)
        cur, prev = cur * scale, prev * scale
        shift = shift + jnp.where(big, 32.0, 0.0)
        factor = jnp.exp2(0.5 * (jnp.where(second, start_b, start_a) + shift))
        for j in range(8):
            r = (block * 8 + j).astype(jnp.float32)
            fresh = r == length
            begin = jnp.logical_or(fresh, r == 0.0)
            in_b = r >= length
            m = jnp.where(in_b, wb, wa)
            k = jnp.where(in_b, r - length, r)
            n = m + k
            den = k * (m + n)
            num = 4.0 * n * n - 1.0
            root = lax.rsqrt(jnp.maximum(num * den, 1.0))
            upper = num * root
            lower = upper * inv_prev
            inv_prev = den * root
            new = upper * x * cur - lower * prev
            prev = cur
            cur = jnp.where(begin, 1.0, new)
            shift = jnp.where(fresh, 0.0, shift)
            factor = jnp.where(fresh, base_b, factor)
            at = (j % 2) * EACH + block * 4 + j // 2
            rows_ref[pl.ds(at, sz.pair_pad, stride=ROWS), :] = (cur * factor) * factor
        return cur, prev, shift, inv_prev

    lax.fori_loop(0, ROWS // 8, body, (zero, zero, zero, zero))
    index = lax.broadcasted_iota(jnp.int32, (EACH, 128), 0)
    blank = jnp.zeros((256 - EACH, 128), jnp.float32)

    def emit(i, u):
        for p in range(2):
            full = rows_ref[pl.ds(i * ROWS + p * EACH, EACH), :]
            full = jnp.where(2 * index + p <= M, full, 0.0)
            table[i, p] = (full * quadrature).astype(jnp.bfloat16)
            turned = jnp.transpose(jnp.concatenate([full, blank], axis=0))
            table_t[i, p] = turned.astype(jnp.bfloat16)

    each_pair(sz, emit)


def table_shapes(sz):
    return [(sz.pairs, 2, EACH, 128), (sz.pairs, 2, 128, 256)]


def move(source, target, sem):
    copy = pltpu.make_async_copy(source, target, sem)
    copy.start()
    return copy


def each_pair(sz, body, done=None, static=False):
    def several(g, carry=0):
        for u in range(sz.step):
            body(g * sz.step + u, u)
        if done is not None:
            done(g)
        return carry

    if sz.loops == 1 or static:
        for g in range(sz.loops):
            several(g)
    else:
        lax.fori_loop(0, sz.loops, several, 0)


def group_copy(source, target, sems, g, size):
    rows = pl.ds(g * size, size)
    return pltpu.make_async_copy(source.at[rows], target.at[rows], sems.at[g])


def row_facts(sz, waves, i, columns):
    base = lax.axis_index("space") * sz.slots
    wave_a, wave_b = waves[base + 2 * i], waves[base + 2 * i + 1]
    length = M - wave_a
    q = lax.broadcasted_iota(jnp.int32, (ROWS, columns), 0)
    r = jnp.where(q < EACH, 2 * q, 2 * (q - EACH) + 1)
    in_a = r < length
    k = jnp.where(in_a, r, r - length)
    odd = jnp.bitwise_and(length, 1).astype(jnp.float32)
    sign_b = 1.0 - 2.0 * odd
    return wave_a, wave_b, length, r, in_a, k, sign_b


def slot_offset(sz, part, slot):
    lats = sz.part_lats[part]
    at = slot * lats
    if isinstance(at, int):
        return at
    return pl.multiple_of(at, 16 if sz.direct(part) else 8) if lats % 8 == 0 else at


def send_rows(sz, part, i, state, facts, table_t, stage):
    in_a, sign_b = facts[4], facts[6]
    columns = state.shape[1]
    rhs = jnp.concatenate(
        [
            jnp.where(in_a, state, 0.0).astype(jnp.bfloat16),
            jnp.where(in_a, 0.0, state).astype(jnp.bfloat16),
        ],
        axis=1,
    )
    blank = jnp.zeros((256 - EACH, 2 * columns), jnp.bfloat16)
    sums = []
    for p in range(2):
        rows = table_t[i, p]
        side = jnp.concatenate([rhs[p * EACH : (p + 1) * EACH], blank], axis=0)
        sums.append(jnp.dot(rows, side, preferred_element_type=jnp.float32))
    size = sz.part_pad
    plus, minus = sums[0] + sums[1], sums[0] - sums[1]
    for s in range(2):
        north = plus[:, s * columns : (s + 1) * columns]
        south = minus[:, s * columns : (s + 1) * columns]
        south = south * sign_b if s == 1 else south
        at = slot_offset(sz, part, 2 * i + s)
        for b in range(sz.half):
            lo = b * size
            kind = stage.dtype
            stage[b, pl.ds(at, size), :] = north[lo : lo + size].astype(kind)
            stage[sz.space - 1 - b, pl.ds(at, size), :] = south[lo : lo + size].astype(kind)


def flush(sz, part, stage, send, target=None, sems=None):
    def body(g, _):
        for o in range(sz.bundle):
            d = g * sz.bundle + o
            send[d] = stage[d, : sz.block(part), :].astype(jnp.bfloat16)
        if target is not None:
            group_copy(send, target, sems, g, sz.bundle).start()
        return 0

    lax.fori_loop(0, sz.bundles, body, 0)
    if target is not None:
        for g in range(sz.bundles):
            group_copy(send, target, sems, g, sz.bundle).wait()


def rows_copy(sz, part, send, target, sems, g):
    size = 2 * sz.step * sz.part_lats[part]
    rows = pl.ds(g * size, size)
    return pltpu.make_async_copy(send.at[:, rows, :], target.at[:, rows, :], sems.at[g])


def send_pairs(sz, part, body, send, stage, target, sems, done):
    if sz.direct(part):
        def finish(g):
            done(g)
            rows_copy(sz, part, send, target, sems, g).start()

        each_pair(sz, lambda i, u: body(i, u, send), finish, static=True)
        for g in range(sz.loops):
            rows_copy(sz, part, send, target, sems, g).wait()
    else:
        each_pair(sz, lambda i, u: body(i, u, stage), done)
        flush(sz, part, stage, send, target, sems)


def fetch_rows(sz, source, recv, sems):
    for g in range(sz.bundles):
        group_copy(source, recv, sems, g, sz.bundle).start()


def load_rows(sz, part, recv, stage, source=None, sems=None):
    rows = sz.block_pad(part)

    def body(g, _):
        if source is not None:
            group_copy(source, recv, sems, g, sz.bundle).wait()
        for o in range(sz.bundle):
            d = g * sz.bundle + o
            stage[d, rows - 16 : rows, :] = jnp.zeros((16, stage.shape[2]), jnp.float32)
            stage[d, : sz.block(part), :] = recv[d].astype(jnp.float32)
        return 0

    lax.fori_loop(0, sz.bundles, body, 0)


def change_rows(sz, part, i, facts, table, stage):
    in_a, sign_b = facts[4], facts[6]
    size = sz.part_pad
    plus, minus = [], []
    for s in range(2):
        at = slot_offset(sz, part, 2 * i + s)
        north = jnp.concatenate([stage[b, pl.ds(at, size), :] for b in range(sz.half)], axis=0)
        south = jnp.concatenate(
            [stage[sz.space - 1 - b, pl.ds(at, size), :] for b in range(sz.half)], axis=0
        )
        south = south * sign_b if s == 1 else south
        plus.append((north + south).astype(jnp.bfloat16))
        minus.append((north - south).astype(jnp.bfloat16))
    pieces = []
    for p, rows in enumerate((plus, minus)):
        out = jnp.dot(
            table[i, p],
            jnp.concatenate(rows, axis=1),
            preferred_element_type=jnp.float32,
        )
        c = out.shape[1] // 2
        mine = in_a[p * EACH : (p + 1) * EACH]
        pieces.append(jnp.where(mine, out[:, :c], out[:, c:]))
    return jnp.concatenate(pieces, axis=0)


def kept(state, facts):
    wave_a, wave_b, _, r, in_a = facts[:5]
    columns = state.shape[1]
    imaginary = lax.broadcasted_iota(jnp.int32, state.shape, 1) >= columns // 2
    wave = jnp.where(in_a, wave_a, wave_b)
    dropped = jnp.logical_or(jnp.logical_and(wave == 0, imaginary), r > M)
    return jnp.where(dropped, 0.0, state)


def turn_matrix(columns, back=False):
    shape = (2 * columns, 2 * columns)
    r = lax.broadcasted_iota(jnp.int32, shape, 0)
    c = lax.broadcasted_iota(jnp.int32, shape, 1)
    r = jnp.where(r < columns, r, r - columns)
    old, new = (c, r) if back else (r, c)
    target = jnp.bitwise_and(old, 1) * (columns // 2) + jnp.right_shift(old, 1)
    match = jnp.logical_and(target == new, c < columns)
    return jnp.where(match, 1.0, 0.0).astype(jnp.bfloat16)


def halves(x):
    high = x.astype(jnp.bfloat16)
    low = (x - high.astype(jnp.float32)).astype(jnp.bfloat16)
    return jnp.concatenate([high, low], axis=1)


def dot_split(x, both):
    out = jnp.dot(halves(x), both, preferred_element_type=jnp.float32)
    c = out.shape[1] // 2
    return out[:, :c] + out[:, c:]


def inverse_of(x):
    guess = pl.reciprocal(x, approx=True)
    return guess * (2.0 - x * guess)


def updated(state, change, facts, mixing, mixing_t, speeds):
    wave_a, wave_b, _, _, in_a, k = facts[:6]
    combined = state + change
    projected = dot_split(combined, mixing[...])
    n = (jnp.where(in_a, wave_a, wave_b) + k).astype(jnp.float32)
    stiffness = speeds[...] * (n * (n + 1.0))
    weighted = projected * (stiffness * inverse_of(1.0 + stiffness))
    returned = dot_split(weighted, mixing_t[...])
    return kept(combined - returned, facts)


def first_kernel(
    sz, waves_hbm, angles_hbm, spectra_hbm,
    table_hbm, table_t_hbm, state_hbm, send_hbm,
    waves, logs, angles, spectra, table, table_t, state_ref, send, stage, shifted, rows_ref, one, state_sems, send_sems,
):
    columns = spectra.shape[2]
    blank = jnp.zeros((EACH - M // 2, columns), jnp.float32)
    facts = [
        move(waves_hbm, waves, one.at[3]),
        move(angles_hbm.at[8:16], logs, one.at[4]),
        move(angles_hbm.at[0:8], angles, one.at[5]),
    ]
    arriving = move(spectra_hbm, spectra, one.at[0])
    turn = turn_matrix(columns)
    shifted[...] = jnp.zeros_like(shifted)
    for copy in facts:
        copy.wait()
    build_tables(sz, 0, waves, logs, angles, table, table_t, rows_ref)
    leaving = [move(table, table_hbm, one.at[1]), move(table_t, table_t_hbm, one.at[2])]
    arriving.wait()

    def body(i, u, rows_out):
        facts = row_facts(sz, waves, i, columns)
        length, in_a = facts[2], facts[4]
        shifted[u, pl.ds(ROWS, M), :] = spectra[2 * i + 1]
        rows = []
        for p in range(2):
            rows_a = jnp.concatenate(
                [spectra[2 * i, pl.ds(p, M // 2, stride=2), :], blank], axis=0
            )
            rows_b = shifted[u, pl.ds(ROWS - length + p, EACH, stride=2), :]
            rows.append(jnp.where(in_a[p * EACH : (p + 1) * EACH], rows_a, rows_b))
        state = dot_split(jnp.concatenate(rows, axis=0), turn)
        state = kept(state, facts)
        state_ref[i] = state
        send_rows(sz, 0, i, state, facts, table_t, rows_out)

    def state_out(g):
        group_copy(state_ref, state_hbm, state_sems, g, sz.step).start()

    send_pairs(sz, 0, body, send, stage, send_hbm, send_sems, state_out)
    for g in range(sz.loops):
        group_copy(state_ref, state_hbm, state_sems, g, sz.step).wait()
    for copy in leaving:
        copy.wait()


def rest_kernel(
    sz, waves, angles, angles_hbm, state_hbm, table_hbm, table_t_hbm, send_hbm,
    table, table_t, send, state, logs, stage, rows_ref, one, send_sems,
):
    arriving = move(state_hbm, state, one.at[0])
    scalars = move(angles_hbm.at[8:16], logs, one.at[1])
    scalars.wait()
    build_tables(sz, 1, waves, logs, angles, table, table_t, rows_ref)
    leaving = [move(table, table_hbm, one.at[2]), move(table_t, table_t_hbm, one.at[3])]
    arriving.wait()
    inverse_kernel(sz, 1, waves, state, table_t, send, stage, send_hbm, send_sems)
    for copy in leaving:
        copy.wait()


def inverse_kernel(sz, part, waves, state, table_t, send, stage, target=None, sems=None):
    def body(i, u):
        facts = row_facts(sz, waves, i, state.shape[2])
        send_rows(sz, part, i, state[i], facts, table_t, stage)

    each_pair(sz, body)
    flush(sz, part, stage, send, target, sems)


def forward_kernel(sz, part, waves, state, recv, table, out, stage):
    load_rows(sz, part, recv, stage)

    def body(i, u):
        facts = row_facts(sz, waves, i, state.shape[2])
        out[i] = state[i] + change_rows(sz, part, i, facts, table, stage)

    each_pair(sz, body)


def middle_kernel(
    sz, waves, mixing, mixing_t, speeds, partial_hbm, recv_hbm, table_hbm, table_t_hbm,
    state_hbm, send_hbm,
    state_ref, recv, table, table_t, send, stage_in, stage, one, state_sems, recv_sems, send_sems,
):
    part = sz.parts - 1
    columns = state_ref.shape[2]
    fetch_rows(sz, recv_hbm, recv, recv_sems)
    arriving = [
        move(table_hbm, table, one.at[1]),
        move(partial_hbm, state_ref, one.at[0]),
        move(table_t_hbm, table_t, one.at[2]),
    ]
    load_rows(sz, part, recv, stage_in, recv_hbm, recv_sems)
    for copy in arriving:
        copy.wait()

    def body(i, u, rows_out):
        facts = row_facts(sz, waves, i, columns)
        change = change_rows(sz, part, i, facts, table, stage_in)
        state = updated(state_ref[i], change, facts, mixing, mixing_t, speeds)
        state_ref[i] = state
        send_rows(sz, 0, i, state, facts, table_t, rows_out)

    def state_out(g):
        group_copy(state_ref, state_hbm, state_sems, g, sz.step).start()

    send_pairs(sz, 0, body, send, stage, send_hbm, send_sems, state_out)
    for g in range(sz.loops):
        group_copy(state_ref, state_hbm, state_sems, g, sz.step).wait()


def last_kernel(
    sz, waves, mixing, mixing_t, speeds, partial_hbm, recv_hbm, table_hbm,
    out_hbm,
    state_ref, recv, table, out, stage_in, mixed, one, out_sems, recv_sems,
):
    part = sz.parts - 1
    columns = state_ref.shape[2]
    fetch_rows(sz, recv_hbm, recv, recv_sems)
    arriving = [
        move(table_hbm, table, one.at[1]),
        move(partial_hbm, state_ref, one.at[0]),
    ]
    mixed[...] = jnp.zeros_like(mixed)
    turn_t = turn_matrix(columns, back=True)
    load_rows(sz, part, recv, stage_in, recv_hbm, recv_sems)
    for copy in arriving:
        copy.wait()

    def body(i, u):
        facts = row_facts(sz, waves, i, columns)
        wave_b, length = facts[1:3]
        r = lax.broadcasted_iota(jnp.int32, (M, columns), 0)
        change = change_rows(sz, part, i, facts, table, stage_in)
        state = updated(state_ref[i], change, facts, mixing, mixing_t, speeds)
        state = dot_split(state, turn_t)
        for p in range(2):
            mixed[u, pl.ds(p, EACH, stride=2), :] = state[p * EACH : (p + 1) * EACH]
        out[2 * i] = jnp.where(r < length, mixed[u, :M, :], 0.0)
        out[2 * i + 1] = jnp.where(r < M - wave_b, mixed[u, pl.ds(length, M), :], 0.0)

    each_pair(
        sz, body, lambda g: group_copy(out, out_hbm, out_sems, g, 2 * sz.step).start()
    )
    for g in range(sz.loops):
        group_copy(out, out_hbm, out_sems, g, 2 * sz.step).wait()


def grid_kernel(sz, part, members, recv, synth, slope, scale, *rest):
    pieces, rest = rest[:members], rest[members:]
    send, stage_in, stage, lhs, values, slopes, force, traj, sems = rest
    south = lax.axis_index("space") >= sz.half
    member = lax.axis_index("pert")
    copies = [
        pltpu.make_async_copy(piece, traj.at[i], sems.at[i]) for i, piece in enumerate(pieces)
    ]
    for copy in copies:
        copy.start()
    lanes = recv.shape[2]
    rows = lanes // 2
    lats = sz.part_lats[part]
    block = sz.block(part)
    groups = -(-lats // sz.group)

    def load(d, _):
        stage_in[pl.ds(d * block, block), :] = recv[d].astype(jnp.float32)
        return 0

    lax.fori_loop(0, sz.space, load, 0)
    blank = jnp.zeros((DEPTH - M, lanes), jnp.float32)
    for copy in copies:
        copy.wait()

    def levels(t, field):
        mine = []
        for block in range(members):
            shift = lax.rem(block + members - member, members)
            value = traj[0, t, field].astype(jnp.float32)
            for i in range(1, members):
                value = jnp.where(shift == i, traj[i, t, field].astype(jnp.float32), value)
            mine.append(value)
        return jnp.concatenate(mine, axis=0)

    def body(g, _):
        for q in range(sz.group):
            t = jnp.minimum(g * sz.group + q, lats - 1)
            rows_t = stage_in[pl.ds(t, M, stride=lats), :]
            turned = jnp.transpose(jnp.concatenate([rows_t, blank], axis=0)).astype(jnp.bfloat16)
            lhs[q * rows : (q + 1) * rows, :DEPTH] = turned[:rows]
            lhs[q * rows : (q + 1) * rows, DEPTH:] = turned[rows:]
        left = lhs[...]
        values[...] = jnp.dot(left, synth[...], preferred_element_type=jnp.float32)
        slopes[...] = jnp.dot(left, slope[...], preferred_element_type=jnp.float32)
        for q in range(sz.group):
            t = jnp.minimum(g * sz.group + q, lats - 1)
            here = jnp.where(south, lats - 1 - t, t)
            wind = levels(here, 0)
            for v in range(VARS):
                lo = q * rows + v * LEV
                other = levels(here, 1 + (v + 1) % VARS)
                force[lo : lo + LEV, :] = (
                    wind * slopes[lo : lo + LEV, :] + other * values[lo : lo + LEV, :]
                ).astype(jnp.bfloat16)
        forcing = force[...]
        spectrum = [
            lax.dot_general(
                synth[c * DEPTH : c * DEPTH + M, :],
                forcing,
                (((1,), (1,)), ((), ())),
                preferred_element_type=jnp.float32,
            )
            * scale[...][:, :1]
            for c in range(2)
        ]
        left_side = lax.broadcasted_iota(jnp.int32, (M, lanes), 1) < rows
        for q in range(0, sz.group, 2):
            re = spectrum[0][:, q * rows : (q + 2) * rows]
            im = spectrum[1][:, q * rows : (q + 2) * rows]
            pair = (
                jnp.where(left_side, re, pltpu.roll(im, rows, 1)),
                jnp.where(left_side, pltpu.roll(re, rows, 1), im),
            )
            for o in range(2):
                t = g * sz.group + q + o

                def store(t=t, value=pair[o]):
                    stage[pl.ds(t, M, stride=lats), :] = value

                if (groups - 1) * sz.group + q + o < lats:
                    store()
                else:
                    pl.when(t < lats)(store)
        return 0

    lax.fori_loop(0, groups, body, 0)

    def out(d, _):
        send[d] = stage[pl.ds(d * block, block), :].astype(jnp.bfloat16)
        return 0

    lax.fori_loop(0, sz.space, out, 0)


def grid_stage(sz, part, recv, pieces, synth, slope, scale):
    members = len(pieces)
    lanes = recv.shape[2]
    wide = sz.group * lanes // 2
    count = M * sz.part_lats[part]
    return pl.pallas_call(
        lambda *refs: grid_kernel(sz, part, members, *refs),
        out_shape=jax.ShapeDtypeStruct(recv.shape, jnp.bfloat16),
        in_specs=vmem(4) + [pl.BlockSpec(memory_space=pl.ANY)] * members,
        out_specs=vmem(1)[0],
        scratch_shapes=[
            pltpu.VMEM((count, lanes), jnp.float32),
            pltpu.VMEM((count, lanes), jnp.float32),
            pltpu.VMEM((wide, 2 * DEPTH), jnp.bfloat16),
            pltpu.VMEM((wide, NLON), jnp.float32),
            pltpu.VMEM((wide, NLON), jnp.float32),
            pltpu.VMEM((wide, NLON), jnp.bfloat16),
            pltpu.VMEM((members,) + pieces[0].shape, jnp.bfloat16),
            pltpu.SemaphoreType.DMA((members,)),
        ],
        compiler_params=params(),
        cost_estimate=cost(9.0),
        name="grid_stage",
    )(recv, synth, slope, scale, *pieces)


def zonal_tables(wave_list):
    cell_index = jnp.arange(NLON, dtype=jnp.int32)
    wave_pad = jnp.concatenate([wave_list, jnp.zeros((DEPTH - M,), jnp.int32)])
    phase_index = wave_pad[:, None] * cell_index[None, :] % NLON
    angles = phase_index.astype(jnp.float32) * (2.0 * math.pi / NLON)
    factor = jnp.where(wave_pad == 0, 1.0, 2.0).astype(jnp.float32)
    inside = (jnp.arange(DEPTH) < M).astype(jnp.float32)
    gain = (factor * inside)[:, None]
    cosine, sine = gain * jnp.cos(angles), gain * jnp.sin(angles)
    wave = wave_pad.astype(jnp.float32)[:, None]
    synth = jnp.concatenate([-cosine, sine], axis=0).astype(jnp.bfloat16)
    slope = jnp.concatenate([wave * sine, wave * cosine], axis=0).astype(jnp.bfloat16)
    scale = jnp.broadcast_to((-1.0 / (NLON * factor[:M]))[:, None], (M, 128))
    return synth, slope, scale


def split_matrix(matrix):
    high = matrix.astype(jnp.bfloat16)
    low = (matrix - high.astype(jnp.float32)).astype(jnp.bfloat16)
    top = jnp.concatenate([high, low], axis=1)
    bottom = jnp.concatenate([high, jnp.zeros_like(low)], axis=1)
    return jnp.concatenate([top, bottom], axis=0)


def shards(sz, spectra, wave_order, traj_wind, traj_state, vertical_modes, mode_speeds):
    columns = spectra.shape[2]
    index, real = [], []
    for ranges in sz.ranges:
        within = np.concatenate([np.arange(lo, lo + size) for lo, size in ranges])
        pad = sz.part_pad - within.size
        for b in range(sz.half):
            index.append(np.pad(b * sz.lats + within, (0, pad)))
            real.append(np.pad(np.ones(within.size, bool), (0, pad)))
    index, real = np.concatenate(index), np.concatenate(real)
    colat = np.where(real, (index + 0.5) * (math.pi / NLAT), math.pi / 2)
    angles = np.zeros((16, 128), np.float32)
    angles[8:11] = np.pad(sectoral_logs(), (0, 3 * 128 - M)).reshape(3, 128)
    for part in range(sz.parts):
        lanes = slice(part * sz.part_rows, (part + 1) * sz.part_rows)
        mine = colat[lanes]
        angles[2 * part] = np.cos(mine)
        angles[2 * part + 1] = np.log2(np.sin(mine))
        angles[4 + part] = np.sin(mine) * (math.pi / NLAT) * real[lanes]
    angles = jnp.asarray(angles)
    same = np.kron(np.eye(columns // LEV, dtype=np.float32), np.ones((LEV, LEV), np.float32))
    mixing = split_matrix(jnp.tile(vertical_modes.T, (columns // LEV, columns // LEV)) * same)
    mixing_t = split_matrix(jnp.tile(vertical_modes, (columns // LEV, columns // LEV)) * same)
    speeds = jnp.tile(mode_speeds, columns // LEV)[None, :]

    def stages(part):
        return pltpu.VMEM((sz.space, sz.block_pad(part), columns), jnp.float32)

    def sends(part):
        return jax.ShapeDtypeStruct((sz.space, sz.block(part), columns), jnp.bfloat16)

    state_shape = jax.ShapeDtypeStruct((sz.pairs, ROWS, columns), jnp.float32)

    table_specs = [jax.ShapeDtypeStruct(shape, jnp.bfloat16) for shape in table_shapes(sz)]
    table_vmem = [pltpu.VMEM(shape, jnp.bfloat16) for shape in table_shapes(sz)]
    rows_vmem = pltpu.VMEM((sz.pair_pad * ROWS, 128), jnp.float32)
    shift_vmem = pltpu.VMEM((UNROLL, SHIFTED, columns), jnp.float32)
    state_vmem = pltpu.VMEM(state_shape.shape, jnp.float32)

    def block_vmem(part):
        return pltpu.VMEM(sends(part).shape, jnp.bfloat16)

    def dma(count):
        return pltpu.SemaphoreType.DMA((count,))

    def call(body, outs, scalars, near, far, scratch, microseconds, name, away=True):
        anywhere = pl.BlockSpec(memory_space=pltpu.HBM)
        return pl.pallas_call(
            lambda *refs: body(sz, *refs),
            out_shape=tuple(outs),
            in_specs=smem(len(scalars)) + vmem(len(near)) + [anywhere] * len(far),
            out_specs=(anywhere,) * len(outs) if away else tuple(vmem(len(outs))),
            scratch_shapes=scratch,
            compiler_params=params(VMEM_ALONE if away else VMEM_BYTES),
            cost_estimate=cost(microseconds),
            name=name,
        )(*scalars, *near, *far)

    members = LEV // traj_wind.shape[1]

    def shared(value):
        return [value] + [
            lax.ppermute(value, "pert", [(i, (i - shift) % members) for i in range(members)])
            for shift in range(1, members)
        ]

    def cut(step, part):
        fields = [traj_wind[step][None], traj_state[step]]
        local = jnp.concatenate(
            [
                jnp.concatenate([f[:, :, lo : lo + size] for f in fields], axis=0)
                for lo, size in sz.ranges[part]
            ],
            axis=2,
        )
        return shared(jnp.transpose(local, (2, 0, 1, 3)))

    def transpose(value):
        return lax.all_to_all(value, "space", 0, 0, tiled=True)

    traj = {(step, part): cut(step, part) for step in range(STEPS) for part in range(2)}

    table_0, table_t_0, state, send_0 = call(
        first_kernel,
        table_specs + [state_shape, sends(0)],
        [], [], [wave_order, angles, spectra],
        [
            pltpu.SMEM((M,), jnp.int32), pltpu.SMEM((8, 128), jnp.float32),
            pltpu.VMEM((8, 128), jnp.float32),
            pltpu.VMEM(spectra.shape, jnp.float32), *table_vmem, state_vmem, block_vmem(0),
            stages(0), shift_vmem, rows_vmem, dma(7), dma(sz.loops), dma(sz.bundles),
        ],
        12.0, "tables_inverse",
    )
    table_1 = table_t_1 = None
    for step in range(STEPS):
        recv_0 = transpose(send_0)
        if step == 0:
            table_1, table_t_1, send_1 = call(
                rest_kernel,
                table_specs + [sends(1)],
                [wave_order], [angles], [angles, state],
                [
                    *table_vmem, block_vmem(1), state_vmem, pltpu.SMEM((8, 128), jnp.float32),
                    stages(1), rows_vmem, dma(4), dma(sz.bundles),
                ],
                8.0, "tables_inverse_rest",
            )
        else:
            (send_1,) = call(
                lambda s, *refs: inverse_kernel(s, 1, *refs),
                [sends(1)], [wave_order], [state, table_t_1], [], [stages(1)],
                4.0, "inverse_rest", away=False,
            )
        recv_1 = transpose(send_1)
        if step == 0:
            recv_0, later = lax.optimization_barrier((recv_0, wave_order))
            synth, slope, scale = zonal_tables(later)
        back_0 = transpose(grid_stage(sz, 0, recv_0, traj[step, 0], synth, slope, scale))
        back_1 = transpose(grid_stage(sz, 1, recv_1, traj[step, 1], synth, slope, scale))
        (partial,) = call(
            lambda s, *refs: forward_kernel(s, 0, *refs),
            [state_shape], [wave_order], [state, back_0, table_0], [], [stages(0)],
            5.0, "forward_part", away=False,
        )
        near = [mixing, mixing_t, speeds]
        if step < STEPS - 1:
            state, send_0 = call(
                middle_kernel,
                [state_shape, sends(0)],
                [wave_order], near, [partial, back_1, table_1, table_t_0],
                [
                    state_vmem, block_vmem(1), *table_vmem, block_vmem(0), stages(1), stages(0),
                    dma(3), dma(sz.loops), dma(sz.bundles), dma(sz.bundles),
                ],
                12.0, "forward_inverse",
            )
        else:
            (out,) = call(
                last_kernel,
                [jax.ShapeDtypeStruct(spectra.shape, jnp.float32)],
                [wave_order], near, [partial, back_1, table_1],
                [
                    state_vmem, block_vmem(1), table_vmem[0],
                    pltpu.VMEM(spectra.shape, jnp.float32), stages(1), shift_vmem,
                    dma(3), dma(sz.loops), dma(sz.bundles),
                ],
                10.0, "forward_last",
            )
    return out


def solution(mesh):
    sz = Sizes(mesh.shape["space"])
    placed = (
        P("space", None, "pert"),
        P(),
        P(None, "pert", "space", None),
        P(None, None, "pert", "space", None),
        P(),
        P(),
    )
    return jax.shard_map(
        lambda *args: shards(sz, *args),
        mesh=mesh,
        in_specs=placed,
        out_specs=P("space", None, "pert"),
        check_vma=False,
    )
```

```python
import math

import jax
import jax.numpy as jnp
import numpy as np
from jax import lax
from jax.experimental import pallas as pl
from jax.experimental.pallas import tpu as pltpu
from jax.sharding import PartitionSpec as P

NLAT = 480
NLON = 960
M = 320
VARS = 2
LEV = 32
STEPS = 2
ROWS = 336
EACH = ROWS // 2
SPAN = 16
SHIFTED = 2 * ROWS
UNROLL = 5
DEPTH = 384
VMEM_BYTES = 48 * 1024 * 1024
VMEM_ALONE = 60 * 1024 * 1024
BIG = 2.0**32


def params(limit=VMEM_BYTES):
    return pltpu.CompilerParams(vmem_limit_bytes=limit)


def cost(microseconds):
    return pl.CostEstimate(flops=int(microseconds * 30.0e9), bytes_accessed=1 << 20, transcendentals=0)


def vmem(count):
    return [pl.BlockSpec(memory_space=pltpu.VMEM)] * count


def smem(count):
    return [pl.BlockSpec(memory_space=pltpu.SMEM)] * count


class Sizes:
    def __init__(self, space):
        self.space = space
        self.slots = M // space
        self.pairs = self.slots // 2
        self.lats = NLAT // space
        self.half = space // 2
        self.parts = 2
        middle = self.lats // 2
        middle += (self.lats - middle) % 2
        edge = (self.lats - middle) // 2
        self.ranges = [[(edge, middle)], [(0, edge), (self.lats - edge, edge)]]
        self.part_lats = [middle, 2 * edge]
        self.part_pad = -(-max(self.part_lats) // 8) * 8
        self.part_rows = self.half * self.part_pad
        self.north = self.parts * self.part_rows
        self.pair_pad = -(-self.pairs // 8) * 8
        self.group = 8
        self.step = max(d for d in range(1, UNROLL + 1) if self.pairs % d == 0)
        self.loops = self.pairs // self.step
        self.bundle = space // 4 if space % 4 == 0 else space
        self.bundles = space // self.bundle

    def direct(self, part):
        return self.part_lats[part] % 16 == 0

    def block(self, part):
        return self.slots * self.part_lats[part]

    def block_pad(self, part):
        last = (self.slots - 1) * self.part_lats[part] + self.part_pad
        return -(-last // 8) * 8


def sectoral_logs():
    ratios = [0.5 * math.log2((2.0 * i + 1.0) / (2.0 * i)) for i in range(1, M)]
    return np.concatenate([[-0.5], -0.5 + np.cumsum(ratios)]).astype(np.float32)


def build_tables(sz, part, waves, logs, angles, table, table_t, rows_ref):
    cosines, log_sines = angles[2 * part : 2 * part + 1, :], angles[2 * part + 1 : 2 * part + 2, :]
    quadrature = angles[4 + part : 5 + part, :]
    base = lax.axis_index("space") * sz.slots
    shape = (sz.pair_pad, 128)
    zero = jnp.zeros(shape, jnp.float32)
    size = sz.pair_pad
    rows_ref[: 4 * size, :] = jnp.zeros((4 * size, 128), jnp.float32)
    for i in range(sz.pairs):
        wave_a, wave_b = waves[base + 2 * i], waves[base + 2 * i + 1]
        facts = (wave_a.astype(jnp.float32), wave_b.astype(jnp.float32), logs[wave_a // 128, wave_a % 128], logs[wave_b // 128, wave_b % 128])
        for j, fact in enumerate(facts):
            rows_ref[j * size + i : j * size + i + 1, :] = jnp.full((1, 128), fact, jnp.float32)
    wa, wb, ca, cb = (rows_ref[j * size : (j + 1) * size, :] for j in range(4))
    length = M - wa
    start_a = ca + wa * log_sines
    start_b = cb + wb * log_sines
    base_b = jnp.exp2(0.5 * start_b)
    x = jnp.broadcast_to(cosines, shape)

    def body(block, carry):
        cur, prev, shift, inv_prev = carry
        second = (block * SPAN).astype(jnp.float32) > length
        big = jnp.maximum(jnp.abs(cur), jnp.abs(prev)) > BIG
        scale = jnp.where(big, 1.0 / BIG, 1.0)
        cur, prev = cur * scale, prev * scale
        shift = shift + jnp.where(big, 32.0, 0.0)
        factor = jnp.exp2(0.5 * (jnp.where(second, start_b, start_a) + shift))
        for j in range(SPAN):
            r = (block * SPAN + j).astype(jnp.float32)
            fresh = r == length
            begin = jnp.logical_or(fresh, r == 0.0)
            in_b = r >= length
            m = jnp.where(in_b, wb, wa)
            k = jnp.where(in_b, r - length, r)
            n = m + k
            den = k * (m + n)
            num = 4.0 * n * n - 1.0
            root = lax.rsqrt(jnp.maximum(num * den, 1.0))
            upper = num * root
            lower = upper * inv_prev
            inv_prev = den * root
            new = upper * x * cur - lower * prev
            prev = cur
            cur = jnp.where(begin, 1.0, new)
            shift = jnp.where(fresh, 0.0, shift)
            factor = jnp.where(fresh, base_b, factor)
            at = (j % 2) * EACH + block * (SPAN // 2) + j // 2
            rows_ref[pl.ds(at, sz.pair_pad, stride=ROWS), :] = (cur * factor) * factor
        return cur, prev, shift, inv_prev

    lax.fori_loop(0, ROWS // SPAN, body, (zero, zero, zero, zero))
    index = lax.broadcasted_iota(jnp.int32, (EACH, 128), 0)
    blank = jnp.zeros((256 - EACH, 128), jnp.float32)

    def emit(i, u):
        for p in range(2):
            full = rows_ref[pl.ds(i * ROWS + p * EACH, EACH), :]
            full = jnp.where(2 * index + p <= M, full, 0.0)
            table[i, p] = (full * quadrature).astype(jnp.bfloat16)
            turned = jnp.transpose(jnp.concatenate([full, blank], axis=0))
            table_t[i, p] = turned.astype(jnp.bfloat16)

    each_pair(sz, emit)


def table_shapes(sz):
    return [(sz.pairs, 2, EACH, 128), (sz.pairs, 2, 128, 256)]


def move(source, target, sem):
    copy = pltpu.make_async_copy(source, target, sem)
    copy.start()
    return copy


def each_pair(sz, body, done=None, static=False):
    def several(g, carry=0):
        for u in range(sz.step):
            body(g * sz.step + u, u)
        if done is not None:
            done(g)
        return carry

    if sz.loops == 1 or static:
        for g in range(sz.loops):
            several(g)
    else:
        lax.fori_loop(0, sz.loops, several, 0)


def group_copy(source, target, sems, g, size):
    rows = pl.ds(g * size, size)
    return pltpu.make_async_copy(source.at[rows], target.at[rows], sems.at[g])


def row_facts(sz, waves, i, columns):
    base = lax.axis_index("space") * sz.slots
    wave_a, wave_b = waves[base + 2 * i], waves[base + 2 * i + 1]
    length = M - wave_a
    q = lax.broadcasted_iota(jnp.int32, (ROWS, columns), 0)
    r = jnp.where(q < EACH, 2 * q, 2 * (q - EACH) + 1)
    in_a = r < length
    k = jnp.where(in_a, r, r - length)
    odd = jnp.bitwise_and(length, 1).astype(jnp.float32)
    sign_b = 1.0 - 2.0 * odd
    return wave_a, wave_b, length, r, in_a, k, sign_b


def slot_offset(sz, part, slot):
    lats = sz.part_lats[part]
    at = slot * lats
    if isinstance(at, int):
        return at
    return pl.multiple_of(at, 16 if sz.direct(part) else 8) if lats % 8 == 0 else at


def send_rows(sz, part, i, state, facts, table_t, stage):
    in_a, sign_b = facts[4], facts[6]
    columns = state.shape[1]
    rhs = jnp.concatenate(
        [
            jnp.where(in_a, state, 0.0).astype(jnp.bfloat16),
            jnp.where(in_a, 0.0, state).astype(jnp.bfloat16),
        ],
        axis=1,
    )
    blank = jnp.zeros((256 - EACH, 2 * columns), jnp.bfloat16)
    sums = []
    for p in range(2):
        rows = table_t[i, p]
        side = jnp.concatenate([rhs[p * EACH : (p + 1) * EACH], blank], axis=0)
        sums.append(jnp.dot(rows, side, preferred_element_type=jnp.float32))
    size = sz.part_pad
    plus, minus = sums[0] + sums[1], sums[0] - sums[1]
    for s in range(2):
        north = plus[:, s * columns : (s + 1) * columns]
        south = minus[:, s * columns : (s + 1) * columns]
        south = south * sign_b if s == 1 else south
        at = slot_offset(sz, part, 2 * i + s)
        for b in range(sz.half):
            lo = b * size
            kind = stage.dtype
            stage[b, pl.ds(at, size), :] = north[lo : lo + size].astype(kind)
            stage[sz.space - 1 - b, pl.ds(at, size), :] = south[lo : lo + size].astype(kind)


def flush(sz, part, stage, send, target=None, sems=None):
    def body(g, _):
        for o in range(sz.bundle):
            d = g * sz.bundle + o
            send[d] = stage[d, : sz.block(part), :].astype(jnp.bfloat16)
        if target is not None:
            group_copy(send, target, sems, g, sz.bundle).start()
        return 0

    lax.fori_loop(0, sz.bundles, body, 0)
    if target is not None:
        for g in range(sz.bundles):
            group_copy(send, target, sems, g, sz.bundle).wait()


def rows_copy(sz, part, send, target, sems, g):
    size = 2 * sz.step * sz.part_lats[part]
    rows = pl.ds(g * size, size)
    return pltpu.make_async_copy(send.at[:, rows, :], target.at[:, rows, :], sems.at[g])


def send_pairs(sz, part, body, send, stage, target, sems, done):
    if sz.direct(part):
        def finish(g):
            done(g)
            rows_copy(sz, part, send, target, sems, g).start()

        each_pair(sz, lambda i, u: body(i, u, send), finish, static=True)
        for g in range(sz.loops):
            rows_copy(sz, part, send, target, sems, g).wait()
    else:
        each_pair(sz, lambda i, u: body(i, u, stage), done, static=True)
        flush(sz, part, stage, send, target, sems)


def fetch_rows(sz, source, recv, sems):
    for g in range(sz.bundles):
        group_copy(source, recv, sems, g, sz.bundle).start()


def load_rows(sz, part, recv, stage, source=None, sems=None):
    rows = sz.block_pad(part)

    def body(g, _):
        if source is not None:
            group_copy(source, recv, sems, g, sz.bundle).wait()
        for o in range(sz.bundle):
            d = g * sz.bundle + o
            stage[d, rows - 16 : rows, :] = jnp.zeros((16, stage.shape[2]), jnp.float32)
            stage[d, : sz.block(part), :] = recv[d].astype(jnp.float32)
        return 0

    lax.fori_loop(0, sz.bundles, body, 0)


def change_rows(sz, part, i, facts, table, stage):
    in_a, sign_b = facts[4], facts[6]
    size = sz.part_pad
    plus, minus = [], []
    for s in range(2):
        at = slot_offset(sz, part, 2 * i + s)
        north = jnp.concatenate([stage[b, pl.ds(at, size), :] for b in range(sz.half)], axis=0)
        south = jnp.concatenate(
            [stage[sz.space - 1 - b, pl.ds(at, size), :] for b in range(sz.half)], axis=0
        )
        south = south * sign_b if s == 1 else south
        plus.append((north + south).astype(jnp.bfloat16))
        minus.append((north - south).astype(jnp.bfloat16))
    pieces = []
    for p, rows in enumerate((plus, minus)):
        out = jnp.dot(
            table[i, p],
            jnp.concatenate(rows, axis=1),
            preferred_element_type=jnp.float32,
        )
        c = out.shape[1] // 2
        mine = in_a[p * EACH : (p + 1) * EACH]
        pieces.append(jnp.where(mine, out[:, :c], out[:, c:]))
    return jnp.concatenate(pieces, axis=0)


def kept(state, facts):
    wave_a, wave_b, _, r, in_a = facts[:5]
    columns = state.shape[1]
    imaginary = lax.broadcasted_iota(jnp.int32, state.shape, 1) >= columns // 2
    wave = jnp.where(in_a, wave_a, wave_b)
    dropped = jnp.logical_or(jnp.logical_and(wave == 0, imaginary), r > M)
    return jnp.where(dropped, 0.0, state)


def turn_matrix(columns, back=False):
    shape = (2 * columns, 2 * columns)
    r = lax.broadcasted_iota(jnp.int32, shape, 0)
    c = lax.broadcasted_iota(jnp.int32, shape, 1)
    r = jnp.where(r < columns, r, r - columns)
    old, new = (c, r) if back else (r, c)
    target = jnp.bitwise_and(old, 1) * (columns // 2) + jnp.right_shift(old, 1)
    match = jnp.logical_and(target == new, c < columns)
    return jnp.where(match, 1.0, 0.0).astype(jnp.bfloat16)


def halves(x):
    high = x.astype(jnp.bfloat16)
    low = (x - high.astype(jnp.float32)).astype(jnp.bfloat16)
    return jnp.concatenate([high, low], axis=1)


def dot_split(x, both):
    out = jnp.dot(halves(x), both, preferred_element_type=jnp.float32)
    c = out.shape[1] // 2
    return out[:, :c] + out[:, c:]


def inverse_of(x):
    guess = pl.reciprocal(x, approx=True)
    return guess * (2.0 - x * guess)


def updated(state, change, facts, mixing, mixing_t, speeds):
    wave_a, wave_b, _, _, in_a, k = facts[:6]
    combined = state + change
    projected = dot_split(combined, mixing[...])
    n = (jnp.where(in_a, wave_a, wave_b) + k).astype(jnp.float32)
    stiffness = speeds[...] * (n * (n + 1.0))
    weighted = projected * (stiffness * inverse_of(1.0 + stiffness))
    returned = dot_split(weighted, mixing_t[...])
    return kept(combined - returned, facts)


def first_kernel(
    sz, waves_hbm, angles_hbm, spectra_hbm,
    table_hbm, table_t_hbm, state_hbm, send_hbm,
    waves, logs, angles, spectra, table, table_t, state_ref, send, stage, shifted, rows_ref, one, state_sems, send_sems,
):
    columns = spectra.shape[2]
    blank = jnp.zeros((EACH - M // 2, columns), jnp.float32)
    facts = [
        move(waves_hbm, waves, one.at[3]),
        move(angles_hbm.at[8:16], logs, one.at[4]),
        move(angles_hbm.at[0:8], angles, one.at[5]),
    ]
    arriving = move(spectra_hbm, spectra, one.at[0])
    turn = turn_matrix(columns)
    shifted[...] = jnp.zeros_like(shifted)
    for copy in facts:
        copy.wait()
    build_tables(sz, 0, waves, logs, angles, table, table_t, rows_ref)
    leaving = [move(table, table_hbm, one.at[1]), move(table_t, table_t_hbm, one.at[2])]
    arriving.wait()

    def body(i, u, rows_out):
        facts = row_facts(sz, waves, i, columns)
        length, in_a = facts[2], facts[4]
        shifted[u, pl.ds(ROWS, M), :] = spectra[2 * i + 1]
        rows = []
        for p in range(2):
            rows_a = jnp.concatenate(
                [spectra[2 * i, pl.ds(p, M // 2, stride=2), :], blank], axis=0
            )
            rows_b = shifted[u, pl.ds(ROWS - length + p, EACH, stride=2), :]
            rows.append(jnp.where(in_a[p * EACH : (p + 1) * EACH], rows_a, rows_b))
        state = dot_split(jnp.concatenate(rows, axis=0), turn)
        state = kept(state, facts)
        state_ref[i] = state
        send_rows(sz, 0, i, state, facts, table_t, rows_out)

    def state_out(g):
        group_copy(state_ref, state_hbm, state_sems, g, sz.step).start()

    send_pairs(sz, 0, body, send, stage, send_hbm, send_sems, state_out)
    for g in range(sz.loops):
        group_copy(state_ref, state_hbm, state_sems, g, sz.step).wait()
    for copy in leaving:
        copy.wait()


def rest_kernel(
    sz, waves, angles, angles_hbm, state_hbm, table_hbm, table_t_hbm, send_hbm,
    table, table_t, send, state, logs, stage, rows_ref, one, send_sems,
):
    arriving = move(state_hbm, state, one.at[0])
    scalars = move(angles_hbm.at[8:16], logs, one.at[1])
    scalars.wait()
    build_tables(sz, 1, waves, logs, angles, table, table_t, rows_ref)
    leaving = [move(table, table_hbm, one.at[2]), move(table_t, table_t_hbm, one.at[3])]
    arriving.wait()
    inverse_kernel(sz, 1, waves, state, table_t, send, stage, send_hbm, send_sems)
    for copy in leaving:
        copy.wait()


def inverse_kernel(sz, part, waves, state, table_t, send, stage, target=None, sems=None):
    def body(i, u):
        facts = row_facts(sz, waves, i, state.shape[2])
        send_rows(sz, part, i, state[i], facts, table_t, stage)

    each_pair(sz, body)
    flush(sz, part, stage, send, target, sems)


def forward_kernel(sz, part, waves, state, recv, table, out, stage):
    load_rows(sz, part, recv, stage)

    def body(i, u):
        facts = row_facts(sz, waves, i, state.shape[2])
        out[i] = state[i] + change_rows(sz, part, i, facts, table, stage)

    each_pair(sz, body)


def middle_kernel(
    sz, waves, mixing, mixing_t, speeds, partial_hbm, recv_hbm, table_hbm, table_t_hbm,
    state_hbm, send_hbm,
    state_ref, recv, table, table_t, send, stage_in, stage, one, part_sems, state_sems, recv_sems, send_sems,
):
    part = sz.parts - 1
    columns = state_ref.shape[2]
    fetch_rows(sz, recv_hbm, recv, recv_sems)
    early = move(table_hbm, table, one.at[1])
    late = pltpu.make_async_copy(table_t_hbm, table_t, one.at[2])
    group_copy(partial_hbm, state_ref, part_sems, 0, sz.step).start()
    late.start()
    for g in range(1, sz.loops):
        group_copy(partial_hbm, state_ref, part_sems, g, sz.step).start()
    load_rows(sz, part, recv, stage_in, recv_hbm, recv_sems)
    early.wait()

    def body(i, u, rows_out):
        if u == 0:
            group_copy(partial_hbm, state_ref, part_sems, i // sz.step, sz.step).wait()
        facts = row_facts(sz, waves, i, columns)
        change = change_rows(sz, part, i, facts, table, stage_in)
        state = updated(state_ref[i], change, facts, mixing, mixing_t, speeds)
        state_ref[i] = state
        if isinstance(i, int) and i == 0:
            late.wait()
        send_rows(sz, 0, i, state, facts, table_t, rows_out)

    def state_out(g):
        group_copy(state_ref, state_hbm, state_sems, g, sz.step).start()

    send_pairs(sz, 0, body, send, stage, send_hbm, send_sems, state_out)
    for g in range(sz.loops):
        group_copy(state_ref, state_hbm, state_sems, g, sz.step).wait()


def last_kernel(
    sz, waves, mixing, mixing_t, speeds, partial_hbm, recv_hbm, table_hbm,
    out_hbm,
    state_ref, recv, table, out, stage_in, mixed, one, part_sems, out_sems, recv_sems,
):
    part = sz.parts - 1
    columns = state_ref.shape[2]
    fetch_rows(sz, recv_hbm, recv, recv_sems)
    early = move(table_hbm, table, one.at[1])
    for g in range(sz.loops):
        group_copy(partial_hbm, state_ref, part_sems, g, sz.step).start()
    mixed[...] = jnp.zeros_like(mixed)
    turn_t = turn_matrix(columns, back=True)
    load_rows(sz, part, recv, stage_in, recv_hbm, recv_sems)
    early.wait()

    def body(i, u):
        if u == 0:
            group_copy(partial_hbm, state_ref, part_sems, i // sz.step, sz.step).wait()
        facts = row_facts(sz, waves, i, columns)
        wave_b, length = facts[1:3]
        r = lax.broadcasted_iota(jnp.int32, (M, columns), 0)
        change = change_rows(sz, part, i, facts, table, stage_in)
        state = updated(state_ref[i], change, facts, mixing, mixing_t, speeds)
        state = dot_split(state, turn_t)
        for p in range(2):
            mixed[u, pl.ds(p, EACH, stride=2), :] = state[p * EACH : (p + 1) * EACH]
        out[2 * i] = jnp.where(r < length, mixed[u, :M, :], 0.0)
        out[2 * i + 1] = jnp.where(r < M - wave_b, mixed[u, pl.ds(length, M), :], 0.0)

    each_pair(
        sz,
        body,
        lambda g: group_copy(out, out_hbm, out_sems, g, 2 * sz.step).start(),
        static=True,
    )
    for g in range(sz.loops):
        group_copy(out, out_hbm, out_sems, g, 2 * sz.step).wait()


def grid_kernel(sz, part, members, recv, synth, slope, scale, *rest):
    pieces, rest = rest[:members], rest[members:]
    send, stage_in, stage, lhs, values, slopes, force, traj, sems = rest
    south = lax.axis_index("space") >= sz.half
    member = lax.axis_index("pert")
    copies = [
        pltpu.make_async_copy(piece, traj.at[i], sems.at[i]) for i, piece in enumerate(pieces)
    ]
    for copy in copies:
        copy.start()
    lanes = recv.shape[2]
    rows = lanes // 2
    lats = sz.part_lats[part]
    block = sz.block(part)
    groups = -(-lats // sz.group)

    def load(d, _):
        stage_in[pl.ds(d * block, block), :] = recv[d].astype(jnp.float32)
        return 0

    lax.fori_loop(0, sz.space, load, 0)
    blank = jnp.zeros((DEPTH - M, lanes), jnp.float32)
    for copy in copies:
        copy.wait()

    def levels(t, field):
        mine = []
        for block in range(members):
            shift = lax.rem(block + members - member, members)
            value = traj[0, t, field].astype(jnp.float32)
            for i in range(1, members):
                value = jnp.where(shift == i, traj[i, t, field].astype(jnp.float32), value)
            mine.append(value)
        return jnp.concatenate(mine, axis=0)

    def body(g, _):
        for q in range(sz.group):
            t = jnp.minimum(g * sz.group + q, lats - 1)
            rows_t = stage_in[pl.ds(t, M, stride=lats), :]
            turned = jnp.transpose(jnp.concatenate([rows_t, blank], axis=0)).astype(jnp.bfloat16)
            lhs[q * rows : (q + 1) * rows, :DEPTH] = turned[:rows]
            lhs[q * rows : (q + 1) * rows, DEPTH:] = turned[rows:]
        left = lhs[...]
        values[...] = jnp.dot(left, synth[...], preferred_element_type=jnp.float32)
        slopes[...] = jnp.dot(left, slope[...], preferred_element_type=jnp.float32)
        for q in range(sz.group):
            t = jnp.minimum(g * sz.group + q, lats - 1)
            here = jnp.where(south, lats - 1 - t, t)
            wind = levels(here, 0)
            for v in range(VARS):
                lo = q * rows + v * LEV
                other = levels(here, 1 + (v + 1) % VARS)
                force[lo : lo + LEV, :] = (
                    wind * slopes[lo : lo + LEV, :] + other * values[lo : lo + LEV, :]
                ).astype(jnp.bfloat16)
        forcing = force[...]
        spectrum = [
            lax.dot_general(
                synth[c * DEPTH : c * DEPTH + M, :],
                forcing,
                (((1,), (1,)), ((), ())),
                preferred_element_type=jnp.float32,
            )
            * scale[...][:, :1]
            for c in range(2)
        ]
        left_side = lax.broadcasted_iota(jnp.int32, (M, lanes), 1) < rows
        for q in range(0, sz.group, 2):
            re = spectrum[0][:, q * rows : (q + 2) * rows]
            im = spectrum[1][:, q * rows : (q + 2) * rows]
            pair = (
                jnp.where(left_side, re, pltpu.roll(im, rows, 1)),
                jnp.where(left_side, pltpu.roll(re, rows, 1), im),
            )
            for o in range(2):
                t = g * sz.group + q + o

                def store(t=t, value=pair[o]):
                    stage[pl.ds(t, M, stride=lats), :] = value

                if (groups - 1) * sz.group + q + o < lats:
                    store()
                else:
                    pl.when(t < lats)(store)
        return 0

    lax.fori_loop(0, groups, body, 0)

    def out(d, _):
        send[d] = stage[pl.ds(d * block, block), :].astype(jnp.bfloat16)
        return 0

    lax.fori_loop(0, sz.space, out, 0)


def grid_stage(sz, part, recv, pieces, synth, slope, scale):
    members = len(pieces)
    lanes = recv.shape[2]
    wide = sz.group * lanes // 2
    count = M * sz.part_lats[part]
    return pl.pallas_call(
        lambda *refs: grid_kernel(sz, part, members, *refs),
        out_shape=jax.ShapeDtypeStruct(recv.shape, jnp.bfloat16),
        in_specs=vmem(4) + [pl.BlockSpec(memory_space=pl.ANY)] * members,
        out_specs=vmem(1)[0],
        scratch_shapes=[
            pltpu.VMEM((count, lanes), jnp.float32),
            pltpu.VMEM((count, lanes), jnp.float32),
            pltpu.VMEM((wide, 2 * DEPTH), jnp.bfloat16),
            pltpu.VMEM((wide, NLON), jnp.float32),
            pltpu.VMEM((wide, NLON), jnp.float32),
            pltpu.VMEM((wide, NLON), jnp.bfloat16),
            pltpu.VMEM((members,) + pieces[0].shape, jnp.bfloat16),
            pltpu.SemaphoreType.DMA((members,)),
        ],
        compiler_params=params(),
        cost_estimate=cost(9.0),
        name="grid_stage",
    )(recv, synth, slope, scale, *pieces)


def zonal_tables(wave_list):
    cell_index = jnp.arange(NLON, dtype=jnp.int32)
    wave_pad = jnp.concatenate([wave_list, jnp.zeros((DEPTH - M,), jnp.int32)])
    phase_index = wave_pad[:, None] * cell_index[None, :] % NLON
    angles = phase_index.astype(jnp.float32) * (2.0 * math.pi / NLON)
    factor = jnp.where(wave_pad == 0, 1.0, 2.0).astype(jnp.float32)
    inside = (jnp.arange(DEPTH) < M).astype(jnp.float32)
    gain = (factor * inside)[:, None]
    cosine, sine = gain * jnp.cos(angles), gain * jnp.sin(angles)
    wave = wave_pad.astype(jnp.float32)[:, None]
    synth = jnp.concatenate([-cosine, sine], axis=0).astype(jnp.bfloat16)
    slope = jnp.concatenate([wave * sine, wave * cosine], axis=0).astype(jnp.bfloat16)
    scale = jnp.broadcast_to((-1.0 / (NLON * factor[:M]))[:, None], (M, 128))
    return synth, slope, scale


def split_matrix(matrix):
    high = matrix.astype(jnp.bfloat16)
    low = (matrix - high.astype(jnp.float32)).astype(jnp.bfloat16)
    top = jnp.concatenate([high, low], axis=1)
    bottom = jnp.concatenate([high, jnp.zeros_like(low)], axis=1)
    return jnp.concatenate([top, bottom], axis=0)


def shards(sz, spectra, wave_order, traj_wind, traj_state, vertical_modes, mode_speeds):
    columns = spectra.shape[2]
    index, real = [], []
    for ranges in sz.ranges:
        within = np.concatenate([np.arange(lo, lo + size) for lo, size in ranges])
        pad = sz.part_pad - within.size
        for b in range(sz.half):
            index.append(np.pad(b * sz.lats + within, (0, pad)))
            real.append(np.pad(np.ones(within.size, bool), (0, pad)))
    index, real = np.concatenate(index), np.concatenate(real)
    colat = np.where(real, (index + 0.5) * (math.pi / NLAT), math.pi / 2)
    angles = np.zeros((16, 128), np.float32)
    angles[8:11] = np.pad(sectoral_logs(), (0, 3 * 128 - M)).reshape(3, 128)
    for part in range(sz.parts):
        lanes = slice(part * sz.part_rows, (part + 1) * sz.part_rows)
        mine = colat[lanes]
        angles[2 * part] = np.cos(mine)
        angles[2 * part + 1] = np.log2(np.sin(mine))
        angles[4 + part] = np.sin(mine) * (math.pi / NLAT) * real[lanes]
    angles = jnp.asarray(angles)
    same = np.kron(np.eye(columns // LEV, dtype=np.float32), np.ones((LEV, LEV), np.float32))
    mixing = split_matrix(jnp.tile(vertical_modes.T, (columns // LEV, columns // LEV)) * same)
    mixing_t = split_matrix(jnp.tile(vertical_modes, (columns // LEV, columns // LEV)) * same)
    speeds = jnp.tile(mode_speeds, columns // LEV)[None, :]

    def stages(part):
        return pltpu.VMEM((sz.space, sz.block_pad(part), columns), jnp.float32)

    def sends(part):
        return jax.ShapeDtypeStruct((sz.space, sz.block(part), columns), jnp.bfloat16)

    state_shape = jax.ShapeDtypeStruct((sz.pairs, ROWS, columns), jnp.float32)

    table_specs = [jax.ShapeDtypeStruct(shape, jnp.bfloat16) for shape in table_shapes(sz)]
    table_vmem = [pltpu.VMEM(shape, jnp.bfloat16) for shape in table_shapes(sz)]
    rows_vmem = pltpu.VMEM((sz.pair_pad * ROWS, 128), jnp.float32)
    shift_vmem = pltpu.VMEM((UNROLL, SHIFTED, columns), jnp.float32)
    state_vmem = pltpu.VMEM(state_shape.shape, jnp.float32)

    def block_vmem(part):
        return pltpu.VMEM(sends(part).shape, jnp.bfloat16)

    def dma(count):
        return pltpu.SemaphoreType.DMA((count,))

    def call(body, outs, scalars, near, far, scratch, microseconds, name, away=True):
        anywhere = pl.BlockSpec(memory_space=pltpu.HBM)
        return pl.pallas_call(
            lambda *refs: body(sz, *refs),
            out_shape=tuple(outs),
            in_specs=smem(len(scalars)) + vmem(len(near)) + [anywhere] * len(far),
            out_specs=(anywhere,) * len(outs) if away else tuple(vmem(len(outs))),
            scratch_shapes=scratch,
            compiler_params=params(VMEM_ALONE if away else VMEM_BYTES),
            cost_estimate=cost(microseconds),
            name=name,
        )(*scalars, *near, *far)

    members = LEV // traj_wind.shape[1]

    def shared(value):
        return [value] + [
            lax.ppermute(value, "pert", [(i, (i - shift) % members) for i in range(members)])
            for shift in range(1, members)
        ]

    def cut(step, part):
        fields = [traj_wind[step][None], traj_state[step]]
        local = jnp.concatenate(
            [
                jnp.concatenate([f[:, :, lo : lo + size] for f in fields], axis=0)
                for lo, size in sz.ranges[part]
            ],
            axis=2,
        )
        return shared(jnp.transpose(local, (2, 0, 1, 3)))

    def transpose(value):
        return lax.all_to_all(value, "space", 0, 0, tiled=True)

    traj = {(step, part): cut(step, part) for step in range(STEPS) for part in range(2)}

    table_0, table_t_0, state, send_0 = call(
        first_kernel,
        table_specs + [state_shape, sends(0)],
        [], [], [wave_order, angles, spectra],
        [
            pltpu.SMEM((M,), jnp.int32), pltpu.SMEM((8, 128), jnp.float32),
            pltpu.VMEM((8, 128), jnp.float32),
            pltpu.VMEM(spectra.shape, jnp.float32), *table_vmem, state_vmem, block_vmem(0),
            stages(0), shift_vmem, rows_vmem, dma(7), dma(sz.loops), dma(sz.bundles),
        ],
        12.0, "tables_inverse",
    )
    table_1 = table_t_1 = None
    for step in range(STEPS):
        recv_0 = transpose(send_0)
        if step == 0:
            table_1, table_t_1, send_1 = call(
                rest_kernel,
                table_specs + [sends(1)],
                [wave_order], [angles], [angles, state],
                [
                    *table_vmem, block_vmem(1), state_vmem, pltpu.SMEM((8, 128), jnp.float32),
                    stages(1), rows_vmem, dma(4), dma(sz.bundles),
                ],
                8.0, "tables_inverse_rest",
            )
        else:
            (send_1,) = call(
                lambda s, *refs: inverse_kernel(s, 1, *refs),
                [sends(1)], [wave_order], [state, table_t_1], [], [stages(1)],
                4.0, "inverse_rest", away=False,
            )
        recv_1 = transpose(send_1)
        if step == 0:
            recv_0, later = lax.optimization_barrier((recv_0, wave_order))
            synth, slope, scale = zonal_tables(later)
        back_0 = transpose(grid_stage(sz, 0, recv_0, traj[step, 0], synth, slope, scale))
        back_1 = transpose(grid_stage(sz, 1, recv_1, traj[step, 1], synth, slope, scale))
        (partial,) = call(
            lambda s, *refs: forward_kernel(s, 0, *refs),
            [state_shape], [wave_order], [state, back_0, table_0], [], [stages(0)],
            5.0, "forward_part", away=False,
        )
        near = [mixing, mixing_t, speeds]
        if step < STEPS - 1:
            state, send_0 = call(
                middle_kernel,
                [state_shape, sends(0)],
                [wave_order], near, [partial, back_1, table_1, table_t_0],
                [
                    state_vmem, block_vmem(1), *table_vmem, block_vmem(0), stages(1), stages(0),
                    dma(3), dma(sz.loops), dma(sz.loops), dma(sz.bundles),
                    dma(sz.bundles),
                ],
                12.0, "forward_inverse",
            )
        else:
            (out,) = call(
                last_kernel,
                [jax.ShapeDtypeStruct(spectra.shape, jnp.float32)],
                [wave_order], near, [partial, back_1, table_1],
                [
                    state_vmem, block_vmem(1), table_vmem[0],
                    pltpu.VMEM(spectra.shape, jnp.float32), stages(1), shift_vmem,
                    dma(2), dma(sz.loops), dma(sz.loops), dma(sz.bundles),
                ],
                10.0, "forward_last",
            )
    return out


def solution(mesh):
    sz = Sizes(mesh.shape["space"])
    placed = (
        P("space", None, "pert"),
        P(),
        P(None, "pert", "space", None),
        P(None, None, "pert", "space", None),
        P(),
        P(),
    )
    return jax.shard_map(
        lambda *args: shards(sz, *args),
        mesh=mesh,
        in_specs=placed,
        out_specs=P("space", None, "pert"),
        check_vma=False,
    )
```

```python
import math

import jax
import jax.numpy as jnp
import numpy as np
from jax import lax
from jax.experimental import pallas as pl
from jax.experimental.pallas import tpu as pltpu
from jax.sharding import PartitionSpec as P

NLAT = 480
NLON = 960
M = 320
VARS = 2
LEV = 32
STEPS = 2
ROWS = 336
EACH = ROWS // 2
SPAN = 16
SHIFTED = 2 * ROWS
UNROLL = 5
DEPTH = 384
VMEM_BYTES = 48 * 1024 * 1024
VMEM_ALONE = 60 * 1024 * 1024
BIG = 2.0**32


def params(limit=VMEM_BYTES):
    return pltpu.CompilerParams(vmem_limit_bytes=limit)


def cost(microseconds):
    return pl.CostEstimate(flops=int(microseconds * 30.0e9), bytes_accessed=1 << 20, transcendentals=0)


def vmem(count):
    return [pl.BlockSpec(memory_space=pltpu.VMEM)] * count


def smem(count):
    return [pl.BlockSpec(memory_space=pltpu.SMEM)] * count


class Sizes:
    def __init__(self, space):
        self.space = space
        self.slots = M // space
        self.pairs = self.slots // 2
        self.lats = NLAT // space
        self.half = space // 2
        self.parts = 2
        middle = self.lats // 2
        middle += (self.lats - middle) % 2
        edge = (self.lats - middle) // 2
        self.ranges = [[(edge, middle)], [(0, edge), (self.lats - edge, edge)]]
        self.part_lats = [middle, 2 * edge]
        self.part_pad = -(-max(self.part_lats) // 8) * 8
        self.part_rows = self.half * self.part_pad
        self.north = self.parts * self.part_rows
        self.pair_pad = -(-self.pairs // 8) * 8
        self.group = 8
        self.step = max(d for d in range(1, UNROLL + 1) if self.pairs % d == 0)
        self.loops = self.pairs // self.step
        self.bundle = space // 8 if space % 8 == 0 else space
        self.bundles = space // self.bundle

    def direct(self, part):
        return self.part_lats[part] % 16 == 0

    def block(self, part):
        return self.slots * self.part_lats[part]

    def block_pad(self, part):
        last = (self.slots - 1) * self.part_lats[part] + self.part_pad
        return -(-last // 8) * 8


def sectoral_logs():
    ratios = [0.5 * math.log2((2.0 * i + 1.0) / (2.0 * i)) for i in range(1, M)]
    return np.concatenate([[-0.5], -0.5 + np.cumsum(ratios)]).astype(np.float32)


def build_tables(sz, part, waves, logs, angles, table, table_t, rows_ref):
    cosines, log_sines = angles[2 * part : 2 * part + 1, :], angles[2 * part + 1 : 2 * part + 2, :]
    quadrature = angles[4 + part : 5 + part, :]
    base = lax.axis_index("space") * sz.slots
    shape = (sz.pair_pad, 128)
    zero = jnp.zeros(shape, jnp.float32)
    size = sz.pair_pad
    rows_ref[: 4 * size, :] = jnp.zeros((4 * size, 128), jnp.float32)
    for i in range(sz.pairs):
        wave_a, wave_b = waves[base + 2 * i], waves[base + 2 * i + 1]
        facts = (wave_a.astype(jnp.float32), wave_b.astype(jnp.float32), logs[wave_a // 128, wave_a % 128], logs[wave_b // 128, wave_b % 128])
        for j, fact in enumerate(facts):
            rows_ref[j * size + i : j * size + i + 1, :] = jnp.full((1, 128), fact, jnp.float32)
    wa, wb, ca, cb = (rows_ref[j * size : (j + 1) * size, :] for j in range(4))
    length = M - wa
    start_a = ca + wa * log_sines
    start_b = cb + wb * log_sines
    base_b = jnp.exp2(0.5 * start_b)
    x = jnp.broadcast_to(cosines, shape)

    def body(block, carry):
        cur, prev, shift, inv_prev = carry
        second = (block * SPAN).astype(jnp.float32) > length
        big = jnp.maximum(jnp.abs(cur), jnp.abs(prev)) > BIG
        scale = jnp.where(big, 1.0 / BIG, 1.0)
        cur, prev = cur * scale, prev * scale
        shift = shift + jnp.where(big, 32.0, 0.0)
        factor = jnp.exp2(0.5 * (jnp.where(second, start_b, start_a) + shift))
        for j in range(SPAN):
            r = (block * SPAN + j).astype(jnp.float32)
            fresh = r == length
            begin = jnp.logical_or(fresh, r == 0.0)
            in_b = r >= length
            m = jnp.where(in_b, wb, wa)
            k = jnp.where(in_b, r - length, r)
            n = m + k
            den = k * (m + n)
            num = 4.0 * n * n - 1.0
            root = lax.rsqrt(jnp.maximum(num * den, 1.0))
            upper = num * root
            lower = upper * inv_prev
            inv_prev = den * root
            new = upper * x * cur - lower * prev
            prev = cur
            cur = jnp.where(begin, 1.0, new)
            shift = jnp.where(fresh, 0.0, shift)
            factor = jnp.where(fresh, base_b, factor)
            at = (j % 2) * EACH + block * (SPAN // 2) + j // 2
            rows_ref[pl.ds(at, sz.pair_pad, stride=ROWS), :] = (cur * factor) * factor
        return cur, prev, shift, inv_prev

    lax.fori_loop(0, ROWS // SPAN, body, (zero, zero, zero, zero))
    index = lax.broadcasted_iota(jnp.int32, (EACH, 128), 0)
    blank = jnp.zeros((256 - EACH, 128), jnp.float32)

    def emit(i, u):
        for p in range(2):
            full = rows_ref[pl.ds(i * ROWS + p * EACH, EACH), :]
            full = jnp.where(2 * index + p <= M, full, 0.0)
            table[i, p] = (full * quadrature).astype(jnp.bfloat16)
            turned = jnp.transpose(jnp.concatenate([full, blank], axis=0))
            table_t[i, p] = turned.astype(jnp.bfloat16)

    each_pair(sz, emit)


def table_shapes(sz):
    return [(sz.pairs, 2, EACH, 128), (sz.pairs, 2, 128, 256)]


def move(source, target, sem):
    copy = pltpu.make_async_copy(source, target, sem)
    copy.start()
    return copy


def each_pair(sz, body, done=None, static=False):
    def several(g, carry=0):
        for u in range(sz.step):
            body(g * sz.step + u, u)
        if done is not None:
            done(g)
        return carry

    if sz.loops == 1 or static:
        for g in range(sz.loops):
            several(g)
    else:
        lax.fori_loop(0, sz.loops, several, 0)


def group_copy(source, target, sems, g, size):
    rows = pl.ds(g * size, size)
    return pltpu.make_async_copy(source.at[rows], target.at[rows], sems.at[g])


def row_facts(sz, waves, i, columns):
    base = lax.axis_index("space") * sz.slots
    wave_a, wave_b = waves[base + 2 * i], waves[base + 2 * i + 1]
    length = M - wave_a
    q = lax.broadcasted_iota(jnp.int32, (ROWS, columns), 0)
    r = jnp.where(q < EACH, 2 * q, 2 * (q - EACH) + 1)
    in_a = r < length
    k = jnp.where(in_a, r, r - length)
    odd = jnp.bitwise_and(length, 1).astype(jnp.float32)
    sign_b = 1.0 - 2.0 * odd
    return wave_a, wave_b, length, r, in_a, k, sign_b


def slot_offset(sz, part, slot):
    lats = sz.part_lats[part]
    at = slot * lats
    if isinstance(at, int):
        return at
    return pl.multiple_of(at, 16 if sz.direct(part) else 8) if lats % 8 == 0 else at


def send_rows(sz, part, i, state, facts, table_t, stage):
    in_a, sign_b = facts[4], facts[6]
    columns = state.shape[1]
    rhs = jnp.concatenate(
        [
            jnp.where(in_a, state, 0.0).astype(jnp.bfloat16),
            jnp.where(in_a, 0.0, state).astype(jnp.bfloat16),
        ],
        axis=1,
    )
    blank = jnp.zeros((256 - EACH, 2 * columns), jnp.bfloat16)
    sums = []
    for p in range(2):
        rows = table_t[i, p]
        side = jnp.concatenate([rhs[p * EACH : (p + 1) * EACH], blank], axis=0)
        sums.append(jnp.dot(rows, side, preferred_element_type=jnp.float32))
    size = sz.part_pad
    plus, minus = sums[0] + sums[1], sums[0] - sums[1]
    for s in range(2):
        north = plus[:, s * columns : (s + 1) * columns]
        south = minus[:, s * columns : (s + 1) * columns]
        south = south * sign_b if s == 1 else south
        at = slot_offset(sz, part, 2 * i + s)
        for b in range(sz.half):
            lo = b * size
            kind = stage.dtype
            stage[b, pl.ds(at, size), :] = north[lo : lo + size].astype(kind)
            stage[sz.space - 1 - b, pl.ds(at, size), :] = south[lo : lo + size].astype(kind)


def flush(sz, part, stage, send, target=None, sems=None):
    def body(g, _):
        for o in range(sz.bundle):
            d = g * sz.bundle + o
            send[d] = stage[d, : sz.block(part), :].astype(jnp.bfloat16)
        if target is not None:
            group_copy(send, target, sems, g, sz.bundle).start()
        return 0

    lax.fori_loop(0, sz.bundles, body, 0)
    if target is not None:
        for g in range(sz.bundles):
            group_copy(send, target, sems, g, sz.bundle).wait()


def rows_copy(sz, part, send, target, sems, g):
    size = 2 * sz.step * sz.part_lats[part]
    rows = pl.ds(g * size, size)
    return pltpu.make_async_copy(send.at[:, rows, :], target.at[:, rows, :], sems.at[g])


def send_pairs(sz, part, body, send, stage, target, sems, done):
    if sz.direct(part):
        def finish(g):
            done(g)
            rows_copy(sz, part, send, target, sems, g).start()

        each_pair(sz, lambda i, u: body(i, u, send), finish, static=True)
        for g in range(sz.loops):
            rows_copy(sz, part, send, target, sems, g).wait()
    else:
        each_pair(sz, lambda i, u: body(i, u, stage), done, static=True)
        flush(sz, part, stage, send, target, sems)


def fetch_rows(sz, source, recv, sems):
    for g in range(sz.bundles):
        group_copy(source, recv, sems, g, sz.bundle).start()


def load_rows(sz, part, recv, stage, source=None, sems=None):
    rows = sz.block_pad(part)

    def body(g, _):
        if source is not None:
            group_copy(source, recv, sems, g, sz.bundle).wait()
        for o in range(sz.bundle):
            d = g * sz.bundle + o
            stage[d, rows - 16 : rows, :] = jnp.zeros((16, stage.shape[2]), jnp.float32)
            stage[d, : sz.block(part), :] = recv[d].astype(jnp.float32)
        return 0

    if source is None:
        lax.fori_loop(0, sz.bundles, body, 0)
    else:
        for g in range(sz.bundles):
            body(g, 0)


def change_rows(sz, part, i, facts, table, stage):
    in_a, sign_b = facts[4], facts[6]
    size = sz.part_pad
    plus, minus = [], []
    for s in range(2):
        at = slot_offset(sz, part, 2 * i + s)
        north = jnp.concatenate([stage[b, pl.ds(at, size), :] for b in range(sz.half)], axis=0)
        south = jnp.concatenate(
            [stage[sz.space - 1 - b, pl.ds(at, size), :] for b in range(sz.half)], axis=0
        )
        south = south * sign_b if s == 1 else south
        plus.append((north + south).astype(jnp.bfloat16))
        minus.append((north - south).astype(jnp.bfloat16))
    pieces = []
    for p, rows in enumerate((plus, minus)):
        out = jnp.dot(
            table[i, p],
            jnp.concatenate(rows, axis=1),
            preferred_element_type=jnp.float32,
        )
        c = out.shape[1] // 2
        mine = in_a[p * EACH : (p + 1) * EACH]
        pieces.append(jnp.where(mine, out[:, :c], out[:, c:]))
    return jnp.concatenate(pieces, axis=0)


def kept(state, facts):
    wave_a, wave_b, _, r, in_a = facts[:5]
    columns = state.shape[1]
    imaginary = lax.broadcasted_iota(jnp.int32, state.shape, 1) >= columns // 2
    wave = jnp.where(in_a, wave_a, wave_b)
    dropped = jnp.logical_or(jnp.logical_and(wave == 0, imaginary), r > M)
    return jnp.where(dropped, 0.0, state)


def turn_matrix(columns, back=False):
    shape = (2 * columns, 2 * columns)
    r = lax.broadcasted_iota(jnp.int32, shape, 0)
    c = lax.broadcasted_iota(jnp.int32, shape, 1)
    r = jnp.where(r < columns, r, r - columns)
    old, new = (c, r) if back else (r, c)
    target = jnp.bitwise_and(old, 1) * (columns // 2) + jnp.right_shift(old, 1)
    match = jnp.logical_and(target == new, c < columns)
    return jnp.where(match, 1.0, 0.0).astype(jnp.bfloat16)


def halves(x):
    high = x.astype(jnp.bfloat16)
    low = (x - high.astype(jnp.float32)).astype(jnp.bfloat16)
    return jnp.concatenate([high, low], axis=1)


def dot_split(x, both):
    out = jnp.dot(halves(x), both, preferred_element_type=jnp.float32)
    c = out.shape[1] // 2
    return out[:, :c] + out[:, c:]


def inverse_of(x):
    guess = pl.reciprocal(x, approx=True)
    return guess * (2.0 - x * guess)


def updated(state, change, facts, mixing, mixing_t, speeds):
    wave_a, wave_b, _, _, in_a, k = facts[:6]
    combined = state + change
    projected = dot_split(combined, mixing[...])
    n = (jnp.where(in_a, wave_a, wave_b) + k).astype(jnp.float32)
    stiffness = speeds[...] * (n * (n + 1.0))
    weighted = projected * (stiffness * inverse_of(1.0 + stiffness))
    returned = dot_split(weighted, mixing_t[...])
    return kept(combined - returned, facts)


def first_kernel(
    sz, waves_hbm, angles_hbm, spectra_hbm,
    table_hbm, table_t_hbm, state_hbm, send_hbm,
    waves, logs, angles, spectra, table, table_t, state_ref, send, stage, shifted, rows_ref, one, state_sems, send_sems,
):
    columns = spectra.shape[2]
    blank = jnp.zeros((EACH - M // 2, columns), jnp.float32)
    facts = [
        move(waves_hbm, waves, one.at[3]),
        move(angles_hbm.at[8:16], logs, one.at[4]),
        move(angles_hbm.at[0:8], angles, one.at[5]),
    ]
    arriving = move(spectra_hbm, spectra, one.at[0])
    turn = turn_matrix(columns)
    shifted[...] = jnp.zeros_like(shifted)
    for copy in facts:
        copy.wait()
    build_tables(sz, 0, waves, logs, angles, table, table_t, rows_ref)
    leaving = [move(table, table_hbm, one.at[1]), move(table_t, table_t_hbm, one.at[2])]
    arriving.wait()

    def body(i, u, rows_out):
        facts = row_facts(sz, waves, i, columns)
        length, in_a = facts[2], facts[4]
        shifted[u, pl.ds(ROWS, M), :] = spectra[2 * i + 1]
        rows = []
        for p in range(2):
            rows_a = jnp.concatenate(
                [spectra[2 * i, pl.ds(p, M // 2, stride=2), :], blank], axis=0
            )
            rows_b = shifted[u, pl.ds(ROWS - length + p, EACH, stride=2), :]
            rows.append(jnp.where(in_a[p * EACH : (p + 1) * EACH], rows_a, rows_b))
        state = dot_split(jnp.concatenate(rows, axis=0), turn)
        state = kept(state, facts)
        state_ref[i] = state
        send_rows(sz, 0, i, state, facts, table_t, rows_out)

    def state_out(g):
        group_copy(state_ref, state_hbm, state_sems, g, sz.step).start()

    send_pairs(sz, 0, body, send, stage, send_hbm, send_sems, state_out)
    for g in range(sz.loops):
        group_copy(state_ref, state_hbm, state_sems, g, sz.step).wait()
    for copy in leaving:
        copy.wait()


def rest_kernel(
    sz, waves, angles, angles_hbm, state_hbm, table_hbm, table_t_hbm, send_hbm,
    table, table_t, send, state, logs, stage, rows_ref, one, send_sems,
):
    arriving = move(state_hbm, state, one.at[0])
    scalars = move(angles_hbm.at[8:16], logs, one.at[1])
    scalars.wait()
    build_tables(sz, 1, waves, logs, angles, table, table_t, rows_ref)
    leaving = [move(table, table_hbm, one.at[2]), move(table_t, table_t_hbm, one.at[3])]
    arriving.wait()
    inverse_kernel(sz, 1, waves, state, table_t, send, stage, send_hbm, send_sems)
    for copy in leaving:
        copy.wait()


def inverse_kernel(sz, part, waves, state, table_t, send, stage, target=None, sems=None):
    def body(i, u):
        facts = row_facts(sz, waves, i, state.shape[2])
        send_rows(sz, part, i, state[i], facts, table_t, stage)

    each_pair(sz, body)
    flush(sz, part, stage, send, target, sems)


def forward_kernel(sz, part, waves, state, recv, table, out, stage):
    load_rows(sz, part, recv, stage)

    def body(i, u):
        facts = row_facts(sz, waves, i, state.shape[2])
        out[i] = state[i] + change_rows(sz, part, i, facts, table, stage)

    each_pair(sz, body)


def middle_kernel(
    sz, waves, mixing, mixing_t, speeds, partial_hbm, recv_hbm, table_hbm, table_t_hbm,
    state_hbm, send_hbm,
    state_ref, recv, table, table_t, send, stage_in, stage, one, part_sems, state_sems, recv_sems, send_sems,
):
    part = sz.parts - 1
    columns = state_ref.shape[2]
    fetch_rows(sz, recv_hbm, recv, recv_sems)
    early = move(table_hbm, table, one.at[1])
    late = pltpu.make_async_copy(table_t_hbm, table_t, one.at[2])
    group_copy(partial_hbm, state_ref, part_sems, 0, sz.step).start()
    late.start()
    for g in range(1, sz.loops):
        group_copy(partial_hbm, state_ref, part_sems, g, sz.step).start()
    load_rows(sz, part, recv, stage_in, recv_hbm, recv_sems)
    early.wait()

    def body(i, u, rows_out):
        if u == 0:
            group_copy(partial_hbm, state_ref, part_sems, i // sz.step, sz.step).wait()
        facts = row_facts(sz, waves, i, columns)
        change = change_rows(sz, part, i, facts, table, stage_in)
        state = updated(state_ref[i], change, facts, mixing, mixing_t, speeds)
        state_ref[i] = state
        if isinstance(i, int) and i == 0:
            late.wait()
        send_rows(sz, 0, i, state, facts, table_t, rows_out)

    def state_out(g):
        group_copy(state_ref, state_hbm, state_sems, g, sz.step).start()

    send_pairs(sz, 0, body, send, stage, send_hbm, send_sems, state_out)
    for g in range(sz.loops):
        group_copy(state_ref, state_hbm, state_sems, g, sz.step).wait()


def last_kernel(
    sz, waves, mixing, mixing_t, speeds, partial_hbm, recv_hbm, table_hbm,
    out_hbm,
    state_ref, recv, table, out, stage_in, mixed, one, part_sems, out_sems, recv_sems,
):
    part = sz.parts - 1
    columns = state_ref.shape[2]
    fetch_rows(sz, recv_hbm, recv, recv_sems)
    early = move(table_hbm, table, one.at[1])
    for g in range(sz.loops):
        group_copy(partial_hbm, state_ref, part_sems, g, sz.step).start()
    mixed[...] = jnp.zeros_like(mixed)
    turn_t = turn_matrix(columns, back=True)
    load_rows(sz, part, recv, stage_in, recv_hbm, recv_sems)
    early.wait()

    def body(i, u):
        if u == 0:
            group_copy(partial_hbm, state_ref, part_sems, i // sz.step, sz.step).wait()
        facts = row_facts(sz, waves, i, columns)
        wave_b, length = facts[1:3]
        r = lax.broadcasted_iota(jnp.int32, (M, columns), 0)
        change = change_rows(sz, part, i, facts, table, stage_in)
        state = updated(state_ref[i], change, facts, mixing, mixing_t, speeds)
        state = dot_split(state, turn_t)
        for p in range(2):
            mixed[u, pl.ds(p, EACH, stride=2), :] = state[p * EACH : (p + 1) * EACH]
        out[2 * i] = jnp.where(r < length, mixed[u, :M, :], 0.0)
        out[2 * i + 1] = jnp.where(r < M - wave_b, mixed[u, pl.ds(length, M), :], 0.0)

    each_pair(
        sz,
        body,
        lambda g: group_copy(out, out_hbm, out_sems, g, 2 * sz.step).start(),
        static=True,
    )
    for g in range(sz.loops):
        group_copy(out, out_hbm, out_sems, g, 2 * sz.step).wait()


def grid_kernel(sz, part, members, recv, synth, slope, scale, *rest):
    pieces, rest = rest[:members], rest[members:]
    send, stage_in, stage, lhs, values, slopes, force, traj, sems = rest
    south = lax.axis_index("space") >= sz.half
    member = lax.axis_index("pert")
    copies = [
        pltpu.make_async_copy(piece, traj.at[i], sems.at[i]) for i, piece in enumerate(pieces)
    ]
    for copy in copies:
        copy.start()
    lanes = recv.shape[2]
    rows = lanes // 2
    lats = sz.part_lats[part]
    block = sz.block(part)
    groups = -(-lats // sz.group)

    def load(d, _):
        stage_in[pl.ds(d * block, block), :] = recv[d].astype(jnp.float32)
        return 0

    lax.fori_loop(0, sz.space, load, 0)
    blank = jnp.zeros((DEPTH - M, lanes), jnp.float32)
    for copy in copies:
        copy.wait()

    def levels(t, field):
        mine = []
        for block in range(members):
            shift = lax.rem(block + members - member, members)
            value = traj[0, t, field].astype(jnp.float32)
            for i in range(1, members):
                value = jnp.where(shift == i, traj[i, t, field].astype(jnp.float32), value)
            mine.append(value)
        return jnp.concatenate(mine, axis=0)

    def body(g, _):
        for q in range(sz.group):
            t = jnp.minimum(g * sz.group + q, lats - 1)
            rows_t = stage_in[pl.ds(t, M, stride=lats), :]
            turned = jnp.transpose(jnp.concatenate([rows_t, blank], axis=0)).astype(jnp.bfloat16)
            lhs[q * rows : (q + 1) * rows, :DEPTH] = turned[:rows]
            lhs[q * rows : (q + 1) * rows, DEPTH:] = turned[rows:]
        left = lhs[...]
        values[...] = jnp.dot(left, synth[...], preferred_element_type=jnp.float32)
        slopes[...] = jnp.dot(left, slope[...], preferred_element_type=jnp.float32)
        for q in range(sz.group):
            t = jnp.minimum(g * sz.group + q, lats - 1)
            here = jnp.where(south, lats - 1 - t, t)
            wind = levels(here, 0)
            for v in range(VARS):
                lo = q * rows + v * LEV
                other = levels(here, 1 + (v + 1) % VARS)
                force[lo : lo + LEV, :] = (
                    wind * slopes[lo : lo + LEV, :] + other * values[lo : lo + LEV, :]
                ).astype(jnp.bfloat16)
        forcing = force[...]
        spectrum = [
            lax.dot_general(
                synth[c * DEPTH : c * DEPTH + M, :],
                forcing,
                (((1,), (1,)), ((), ())),
                preferred_element_type=jnp.float32,
            )
            * scale[...][:, :1]
            for c in range(2)
        ]
        left_side = lax.broadcasted_iota(jnp.int32, (M, lanes), 1) < rows
        for q in range(0, sz.group, 2):
            re = spectrum[0][:, q * rows : (q + 2) * rows]
            im = spectrum[1][:, q * rows : (q + 2) * rows]
            pair = (
                jnp.where(left_side, re, pltpu.roll(im, rows, 1)),
                jnp.where(left_side, pltpu.roll(re, rows, 1), im),
            )
            for o in range(2):
                t = g * sz.group + q + o

                def store(t=t, value=pair[o]):
                    stage[pl.ds(t, M, stride=lats), :] = value

                if (groups - 1) * sz.group + q + o < lats:
                    store()
                else:
                    pl.when(t < lats)(store)
        return 0

    lax.fori_loop(0, groups, body, 0)

    def out(d, _):
        send[d] = stage[pl.ds(d * block, block), :].astype(jnp.bfloat16)
        return 0

    lax.fori_loop(0, sz.space, out, 0)


def grid_stage(sz, part, recv, pieces, synth, slope, scale):
    members = len(pieces)
    lanes = recv.shape[2]
    wide = sz.group * lanes // 2
    count = M * sz.part_lats[part]
    return pl.pallas_call(
        lambda *refs: grid_kernel(sz, part, members, *refs),
        out_shape=jax.ShapeDtypeStruct(recv.shape, jnp.bfloat16),
        in_specs=vmem(4) + [pl.BlockSpec(memory_space=pl.ANY)] * members,
        out_specs=vmem(1)[0],
        scratch_shapes=[
            pltpu.VMEM((count, lanes), jnp.float32),
            pltpu.VMEM((count, lanes), jnp.float32),
            pltpu.VMEM((wide, 2 * DEPTH), jnp.bfloat16),
            pltpu.VMEM((wide, NLON), jnp.float32),
            pltpu.VMEM((wide, NLON), jnp.float32),
            pltpu.VMEM((wide, NLON), jnp.bfloat16),
            pltpu.VMEM((members,) + pieces[0].shape, jnp.bfloat16),
            pltpu.SemaphoreType.DMA((members,)),
        ],
        compiler_params=params(),
        cost_estimate=cost(9.0),
        name="grid_stage",
    )(recv, synth, slope, scale, *pieces)


def zonal_tables(wave_list):
    cell_index = jnp.arange(NLON, dtype=jnp.int32)
    wave_pad = jnp.concatenate([wave_list, jnp.zeros((DEPTH - M,), jnp.int32)])
    phase_index = wave_pad[:, None] * cell_index[None, :] % NLON
    angles = phase_index.astype(jnp.float32) * (2.0 * math.pi / NLON)
    factor = jnp.where(wave_pad == 0, 1.0, 2.0).astype(jnp.float32)
    inside = (jnp.arange(DEPTH) < M).astype(jnp.float32)
    gain = (factor * inside)[:, None]
    cosine, sine = gain * jnp.cos(angles), gain * jnp.sin(angles)
    wave = wave_pad.astype(jnp.float32)[:, None]
    synth = jnp.concatenate([-cosine, sine], axis=0).astype(jnp.bfloat16)
    slope = jnp.concatenate([wave * sine, wave * cosine], axis=0).astype(jnp.bfloat16)
    scale = jnp.broadcast_to((-1.0 / (NLON * factor[:M]))[:, None], (M, 128))
    return synth, slope, scale


def split_matrix(matrix):
    high = matrix.astype(jnp.bfloat16)
    low = (matrix - high.astype(jnp.float32)).astype(jnp.bfloat16)
    top = jnp.concatenate([high, low], axis=1)
    bottom = jnp.concatenate([high, jnp.zeros_like(low)], axis=1)
    return jnp.concatenate([top, bottom], axis=0)


def shards(sz, spectra, wave_order, traj_wind, traj_state, vertical_modes, mode_speeds):
    columns = spectra.shape[2]
    index, real = [], []
    for ranges in sz.ranges:
        within = np.concatenate([np.arange(lo, lo + size) for lo, size in ranges])
        pad = sz.part_pad - within.size
        for b in range(sz.half):
            index.append(np.pad(b * sz.lats + within, (0, pad)))
            real.append(np.pad(np.ones(within.size, bool), (0, pad)))
    index, real = np.concatenate(index), np.concatenate(real)
    colat = np.where(real, (index + 0.5) * (math.pi / NLAT), math.pi / 2)
    angles = np.zeros((16, 128), np.float32)
    angles[8:11] = np.pad(sectoral_logs(), (0, 3 * 128 - M)).reshape(3, 128)
    for part in range(sz.parts):
        lanes = slice(part * sz.part_rows, (part + 1) * sz.part_rows)
        mine = colat[lanes]
        angles[2 * part] = np.cos(mine)
        angles[2 * part + 1] = np.log2(np.sin(mine))
        angles[4 + part] = np.sin(mine) * (math.pi / NLAT) * real[lanes]
    angles = jnp.asarray(angles)
    same = np.kron(np.eye(columns // LEV, dtype=np.float32), np.ones((LEV, LEV), np.float32))
    mixing = split_matrix(jnp.tile(vertical_modes.T, (columns // LEV, columns // LEV)) * same)
    mixing_t = split_matrix(jnp.tile(vertical_modes, (columns // LEV, columns // LEV)) * same)
    speeds = jnp.tile(mode_speeds, columns // LEV)[None, :]

    def stages(part):
        return pltpu.VMEM((sz.space, sz.block_pad(part), columns), jnp.float32)

    def sends(part):
        return jax.ShapeDtypeStruct((sz.space, sz.block(part), columns), jnp.bfloat16)

    state_shape = jax.ShapeDtypeStruct((sz.pairs, ROWS, columns), jnp.float32)

    table_specs = [jax.ShapeDtypeStruct(shape, jnp.bfloat16) for shape in table_shapes(sz)]
    table_vmem = [pltpu.VMEM(shape, jnp.bfloat16) for shape in table_shapes(sz)]
    rows_vmem = pltpu.VMEM((sz.pair_pad * ROWS, 128), jnp.float32)
    shift_vmem = pltpu.VMEM((UNROLL, SHIFTED, columns), jnp.float32)
    state_vmem = pltpu.VMEM(state_shape.shape, jnp.float32)

    def block_vmem(part):
        return pltpu.VMEM(sends(part).shape, jnp.bfloat16)

    def dma(count):
        return pltpu.SemaphoreType.DMA((count,))

    def call(body, outs, scalars, near, far, scratch, microseconds, name, away=True):
        anywhere = pl.BlockSpec(memory_space=pltpu.HBM)
        return pl.pallas_call(
            lambda *refs: body(sz, *refs),
            out_shape=tuple(outs),
            in_specs=smem(len(scalars)) + vmem(len(near)) + [anywhere] * len(far),
            out_specs=(anywhere,) * len(outs) if away else tuple(vmem(len(outs))),
            scratch_shapes=scratch,
            compiler_params=params(VMEM_ALONE if away else VMEM_BYTES),
            cost_estimate=cost(microseconds),
            name=name,
        )(*scalars, *near, *far)

    members = LEV // traj_wind.shape[1]

    def shared(value):
        return [value] + [
            lax.ppermute(value, "pert", [(i, (i - shift) % members) for i in range(members)])
            for shift in range(1, members)
        ]

    def cut(step, part):
        fields = [traj_wind[step][None], traj_state[step]]
        local = jnp.concatenate(
            [
                jnp.concatenate([f[:, :, lo : lo + size] for f in fields], axis=0)
                for lo, size in sz.ranges[part]
            ],
            axis=2,
        )
        return shared(jnp.transpose(local, (2, 0, 1, 3)))

    def transpose(value):
        return lax.all_to_all(value, "space", 0, 0, tiled=True)

    traj = {(step, part): cut(step, part) for step in range(STEPS) for part in range(2)}

    table_0, table_t_0, state, send_0 = call(
        first_kernel,
        table_specs + [state_shape, sends(0)],
        [], [], [wave_order, angles, spectra],
        [
            pltpu.SMEM((M,), jnp.int32), pltpu.SMEM((8, 128), jnp.float32),
            pltpu.VMEM((8, 128), jnp.float32),
            pltpu.VMEM(spectra.shape, jnp.float32), *table_vmem, state_vmem, block_vmem(0),
            stages(0), shift_vmem, rows_vmem, dma(7), dma(sz.loops), dma(sz.bundles),
        ],
        12.0, "tables_inverse",
    )
    table_1 = table_t_1 = None
    for step in range(STEPS):
        recv_0 = transpose(send_0)
        if step == 0:
            table_1, table_t_1, send_1 = call(
                rest_kernel,
                table_specs + [sends(1)],
                [wave_order], [angles], [angles, state],
                [
                    *table_vmem, block_vmem(1), state_vmem, pltpu.SMEM((8, 128), jnp.float32),
                    stages(1), rows_vmem, dma(4), dma(sz.bundles),
                ],
                8.0, "tables_inverse_rest",
            )
        else:
            (send_1,) = call(
                lambda s, *refs: inverse_kernel(s, 1, *refs),
                [sends(1)], [wave_order], [state, table_t_1], [], [stages(1)],
                4.0, "inverse_rest", away=False,
            )
        recv_1 = transpose(send_1)
        if step == 0:
            recv_0, later = lax.optimization_barrier((recv_0, wave_order))
            synth, slope, scale = zonal_tables(later)
        back_0 = transpose(grid_stage(sz, 0, recv_0, traj[step, 0], synth, slope, scale))
        back_1 = transpose(grid_stage(sz, 1, recv_1, traj[step, 1], synth, slope, scale))
        (partial,) = call(
            lambda s, *refs: forward_kernel(s, 0, *refs),
            [state_shape], [wave_order], [state, back_0, table_0], [], [stages(0)],
            5.0, "forward_part", away=False,
        )
        near = [mixing, mixing_t, speeds]
        if step < STEPS - 1:
            state, send_0 = call(
                middle_kernel,
                [state_shape, sends(0)],
                [wave_order], near, [partial, back_1, table_1, table_t_0],
                [
                    state_vmem, block_vmem(1), *table_vmem, block_vmem(0), stages(1), stages(0),
                    dma(3), dma(sz.loops), dma(sz.loops), dma(sz.bundles),
                    dma(sz.bundles),
                ],
                12.0, "forward_inverse",
            )
        else:
            (out,) = call(
                last_kernel,
                [jax.ShapeDtypeStruct(spectra.shape, jnp.float32)],
                [wave_order], near, [partial, back_1, table_1],
                [
                    state_vmem, block_vmem(1), table_vmem[0],
                    pltpu.VMEM(spectra.shape, jnp.float32), stages(1), shift_vmem,
                    dma(2), dma(sz.loops), dma(sz.loops), dma(sz.bundles),
                ],
                10.0, "forward_last",
            )
    return out


def solution(mesh):
    sz = Sizes(mesh.shape["space"])
    placed = (
        P("space", None, "pert"),
        P(),
        P(None, "pert", "space", None),
        P(None, None, "pert", "space", None),
        P(),
        P(),
    )
    return jax.shard_map(
        lambda *args: shards(sz, *args),
        mesh=mesh,
        in_specs=placed,
        out_specs=P("space", None, "pert"),
        check_vma=False,
    )
```
